32 devices in a mesh: gx: 16 (over z, y, core), gy: 2 (over x).
Axes of the slice: x: 2, y: 2, z: 4, core: 2. Of those that a mesh axis runs over, the one named last changes fastest.
Arguments:
- fwd_pops: bfloat16 [3, 19, 64, 16, 128], P(None, None, 'gx', 'gy'), may hold values from -4 to 4
- fwd_scale: float32 [3, 64, 16, 128], P(None, 'gx', 'gy'), may hold values from 0.01 to 0.1
- seed_adjoint: float32 [19, 64, 16, 128], P(None, 'gx', 'gy'), may hold values from -16 to 16
- turbine_map: int32 [64, 16, 128], P('gx', 'gy'), may hold values from -1 to 9, as said below
- thrust: float32 [10], replicated, may hold values from 0.4 to 0.88
Outputs:
- adjoint_out: float32 [19, 64, 16, 128], P(None, 'gx', 'gy')
- thrust_grad: float32 [10], replicated
The draws below stay inside these ranges and needn't reach their ends.
Inputs may be any that keep to these rules, and one draw needn't show every extreme that they name: `turbine_map`: every turbine's disk is the set of cells in one streamwise plane within 4 cells (Euclidean, spanwise distance wrapping) of its centre; disks never intersect and every turbine covers cells.
All inputs are finite; a program needn't handle non-finite values.
Results may differ from the reference program's by a relative error of at most 0.0003.
Values sent between devices are 32-bit elements; how exact they have to be, the bound alone decides.
No kernel may reach another device: no remote copies, remote signals or barrier semaphores. Data moves between devices by JAX's collectives and lax.ppermute only.
A program may use at most 64 MiB of HBM per device.

```python
import math
import jax
import jax.numpy as jnp
from jax import lax

CX = 4
NZ = 128
STEPS = 3
TROWS = 10
RAD = 4
NX = 64
NY = 16
TURB = 10
N_GX = 16


def draw_turbine_map(key, part):
    key_rows, key_cols, key_high = jax.random.split(jax.random.fold_in(key, 7), 3)
    columns = TURB // TROWS
    offset_rows = jax.random.randint(key_rows, (TURB,), -1, 2)
    offset_cols = jax.random.randint(key_cols, (TURB,), -2, 3)
    offset_high = jax.random.randint(key_high, (TURB,), -2, 3)
    plane_x = jnp.arange(NX, dtype=jnp.int32)[:, None, None]
    plane_y = jnp.arange(NY, dtype=jnp.int32)[None, :, None]
    plane_z = jnp.arange(NZ, dtype=jnp.int32)[None, None, :]
    result = jnp.full((NX, NY, NZ), -1, jnp.int32)
    for turbine in range(TURB):
        row_pos = turbine // columns
        col_pos = turbine % columns
        centre_x = (2 * row_pos + 1) * NX // (2 * TROWS) + offset_rows[turbine]
        centre_y = (2 * col_pos + 1) * NY // (2 * columns) + offset_cols[turbine]
        centre_z = NZ // 3 + offset_high[turbine]
        across = (plane_y - centre_y + NY // 2) % NY - NY // 2
        upward = plane_z - centre_z
        cover = (plane_x == centre_x) & (across * across + upward * upward <= RAD * RAD)
        result = jnp.where(cover, jnp.int32(turbine), result)
    return result


def block_scale(stream_key, dims, cuts, low, high):
    def one(dim, parts):
        draws = jax.random.uniform(jax.random.fold_in(jax.random.fold_in(stream_key, 6), dim), (parts,), jnp.float32, low / len(cuts), high / len(cuts))
        return jnp.repeat(jnp.exp(draws), dims[dim] // parts).reshape((-1,) + (1,) * (len(dims) - dim - 1))

    loudness = one(*cuts[0])
    for cut in cuts[1:]:
        loudness = loudness * one(*cut)
    return loudness


def gaussian(rng, dims, scale, reach, cuts=(), kind=jnp.bfloat16):
    entries = scale * jax.random.normal(rng, dims, jnp.float32)
    if cuts:
        entries = entries * block_scale(rng, dims, cuts, -0.22, 0.18)
    return jnp.clip(entries, -reach, reach).astype(kind)


def setup_inputs(seed: int = 0) -> dict:
    arg_keys = jax.random.split(jax.random.key(seed), 6)
    return {
        "fwd_pops": gaussian(arg_keys[0], (STEPS, 19, NX, NY, NZ), 1.0, 4.0, ((2, 16), (3, 2))),
        "fwd_scale": jnp.clip(jnp.exp(math.log(0.1) - 2.3025851 * jax.random.uniform(arg_keys[1], (STEPS, NX, NY, NZ), jnp.float32) ** block_scale(arg_keys[1], (STEPS, NX, NY, NZ), ((1, 16), (2, 2)), -0.2, 0.2)), 0.01, 0.1),
        "seed_adjoint": gaussian(arg_keys[2], (19, NX, NY, NZ), 4.0, 16.0, ((1, 16), (2, 2)), jnp.float32),
        "turbine_map": draw_turbine_map(jax.random.fold_in(arg_keys[5], 71), 0),
        "thrust": jnp.clip(jax.random.uniform(arg_keys[4], (TURB,), jnp.float32, 0.4, 0.88), 0.4, 0.88),
    }


VELOCITIES = ((0, 0, 0), (1, 0, 0), (-1, 0, 0), (0, 1, 0), (0, -1, 0), (0, 0, 1), (0, 0, -1), (1, 1, 0), (-1, -1, 0), (1, -1, 0), (-1, 1, 0), (1, 0, 1), (-1, 0, -1), (1, 0, -1), (-1, 0, 1), (0, 1, 1), (0, -1, -1), (0, 1, -1), (0, -1, 1))
OPPOSITE = (0, 2, 1, 4, 3, 6, 5, 8, 7, 10, 9, 12, 11, 14, 13, 16, 15, 18, 17)
WEIGHTS = tuple([1.0 / 3.0] + [1.0 / 18.0] * 6 + [1.0 / 36.0] * 12)
MEAN_FLOW = 0.1
TAU_BASE = 0.51
SMAG_COEF = 18.0 * 1.4142135623730951 * 0.17 * 0.17
QUAD_FLOOR = 0.0001
PAIRS = ((0, 0, 1.0), (1, 1, 1.0), (2, 2, 1.0), (0, 1, 2.0), (0, 2, 2.0), (1, 2, 2.0))

def base_values():
    values = []
    for member in range(19):
        along = float(VELOCITIES[member][0])
        values.append(WEIGHTS[member] * (1.0 + 3.0 * MEAN_FLOW * along + 4.5 * MEAN_FLOW * MEAN_FLOW * along * along - 1.5 * MEAN_FLOW * MEAN_FLOW))
    return values

def decode(stored, scaling):
    base = jnp.asarray(base_values(), dtype=jnp.float32)
    return base[:, None, None, None] * (1.0 + scaling[None] * stored.astype(jnp.float32))

def collide(populations, thrust_cell):
    density = populations[0]
    for member in range(1, 19):
        density = density + populations[member]
    velocity = []
    for axis_id in range(3):
        moment = jnp.zeros_like(density)
        for member in range(19):
            component = VELOCITIES[member][axis_id]
            if component != 0:
                moment = moment + float(component) * populations[member]
        velocity.append(moment / density)
    speed_sq = velocity[0] * velocity[0] + velocity[1] * velocity[1] + velocity[2] * velocity[2]
    nonequil = []
    for member in range(19):
        proj = float(VELOCITIES[member][0]) * velocity[0] + float(VELOCITIES[member][1]) * velocity[1] + float(VELOCITIES[member][2]) * velocity[2]
        equilib = WEIGHTS[member] * density * (1.0 + 3.0 * proj + 4.5 * proj * proj - 1.5 * speed_sq)
        nonequil.append(populations[member] - equilib)
    stress_sum = jnp.zeros_like(density)
    for first, second, factor in PAIRS:
        stress = jnp.zeros_like(density)
        for member in range(19):
            product = VELOCITIES[member][first] * VELOCITIES[member][second]
            if product != 0:
                stress = stress + float(product) * nonequil[member]
        stress_sum = stress_sum + factor * stress * stress
    magnitude = jnp.sqrt(stress_sum + QUAD_FLOOR)
    relaxation = 0.5 * (TAU_BASE + jnp.sqrt(TAU_BASE * TAU_BASE + SMAG_COEF * magnitude / density))
    thrust_force = -0.5 * thrust_cell * velocity[0] * jnp.abs(velocity[0])
    result = []
    for member in range(19):
        result.append(populations[member] - nonequil[member] / relaxation + 3.0 * WEIGHTS[member] * float(VELOCITIES[member][0]) * thrust_force)
    return jnp.stack(result)

def local_thrust(values):
    return 4.0 * values / jnp.square(1.0 + jnp.sqrt(1.0 - values))

def finish_vertical(shifted, adjoint):
    result = []
    for member in range(19):
        vertical = VELOCITIES[member][2]
        mirror = adjoint[OPPOSITE[member]]
        if vertical == 1:
            result.append(jnp.concatenate([shifted[member][..., 1:], mirror[..., -1:]], axis=-1))
        elif vertical == -1:
            result.append(jnp.concatenate([mirror[..., :1], shifted[member][..., :-1]], axis=-1))
        else:
            result.append(shifted[member])
    return jnp.stack(result)

def pull_plane(adjoint):
    shifted = []
    for member in range(19):
        shifted.append(jnp.roll(adjoint[member], (-VELOCITIES[member][0], -VELOCITIES[member][1]), axis=(0, 1)))
    return shifted

def block_step(inputs):
    stored, scaling, incoming, thrust_cell = inputs
    populations = decode(stored, scaling)
    _, pullback = jax.vjp(collide, populations, thrust_cell)
    return pullback(incoming)

def reference(fwd_pops, fwd_scale, seed_adjoint, turbine_map, thrust):
    inside = turbine_map >= 0
    ids = jnp.maximum(turbine_map, 0)

    def cell_thrust(values):
        return jnp.where(inside, local_thrust(values)[ids], 0.0)
    thrust_cell, thrust_pull = jax.vjp(cell_thrust, thrust)
    cell_blocks = thrust_cell.reshape(N_GX, CX, NY, NZ)
    adjoint = seed_adjoint
    accumulated = jnp.zeros((NX, NY, NZ), jnp.float32)
    for instant in range(STEPS - 1, -1, -1):
        incoming = finish_vertical(pull_plane(adjoint), adjoint)
        stored = fwd_pops[instant].reshape(19, N_GX, CX, NY, NZ).transpose(1, 0, 2, 3, 4)
        scaling = fwd_scale[instant].reshape(N_GX, CX, NY, NZ)
        moving = incoming.reshape(19, N_GX, CX, NY, NZ).transpose(1, 0, 2, 3, 4)
        new_blocks, cell_grad = lax.map(block_step, (stored, scaling, moving, cell_blocks))
        adjoint = new_blocks.transpose(1, 0, 2, 3, 4).reshape(19, NX, NY, NZ)
        accumulated = accumulated + cell_grad.reshape(NX, NY, NZ)
    thrust_grad = thrust_pull(accumulated)[0]
    return (adjoint, thrust_grad)
```

```python
import jax
import jax.numpy as jnp
from jax import lax
from jax.experimental import pallas as pl
from jax.experimental.pallas import tpu as pltpu
from jax.sharding import PartitionSpec as P

VELOCITIES = (
    (0, 0, 0),
    (1, 0, 0),
    (-1, 0, 0),
    (0, 1, 0),
    (0, -1, 0),
    (0, 0, 1),
    (0, 0, -1),
    (1, 1, 0),
    (-1, -1, 0),
    (1, -1, 0),
    (-1, 1, 0),
    (1, 0, 1),
    (-1, 0, -1),
    (1, 0, -1),
    (-1, 0, 1),
    (0, 1, 1),
    (0, -1, -1),
    (0, 1, -1),
    (0, -1, 1),
)
OPPOSITE = (0, 2, 1, 4, 3, 6, 5, 8, 7, 10, 9, 12, 11, 14, 13, 16, 15, 18, 17)
WEIGHTS = tuple([1.0 / 3.0] + [1.0 / 18.0] * 6 + [1.0 / 36.0] * 12)
MEAN_FLOW = 0.1
TAU_BASE = 0.51
SMAG_COEF = 18.0 * 1.4142135623730951 * 0.17 * 0.17
QUAD_FLOOR = 0.0001

X_UP = (1, 7, 9, 11, 13)
X_DOWN = (2, 8, 10, 12, 14)
Y_UP = (3, 7, 10, 15, 17)
Y_DOWN = (4, 8, 9, 16, 18)

KEEP, MASS, FLUX, UX, UY, UZ, Q1 = 19, 20, 21, 22, 23, 24, 25
RATE, BULK, PX, PY, PZ, DRAG, DRAG_U, GAIN = 34, 35, 36, 37, 38, 39, 40, 41
COEFS = 42

VMEM = pltpu.VMEM


def base_values():
    values = []
    for member in range(19):
        along = float(VELOCITIES[member][0])
        values.append(
            WEIGHTS[member]
            * (
                1.0
                + 3.0 * MEAN_FLOW * along
                + 4.5 * MEAN_FLOW * MEAN_FLOW * along * along
                - 1.5 * MEAN_FLOW * MEAN_FLOW
            )
        )
    return values


def plane_coefs(pops, thrust_cell, slope_cell):
    rho = pops[0]
    for member in range(1, 19):
        rho = rho + pops[member]
    inv_rho = 1.0 / rho
    vel = []
    for axis_id in range(3):
        moment = None
        for member in range(19):
            component = VELOCITIES[member][axis_id]
            if component == 1:
                moment = pops[member] if moment is None else moment + pops[member]
            elif component == -1:
                moment = moment - pops[member]
        vel.append(moment * inv_rho)
    ux, uy, uz = vel
    speed_sq = ux * ux + uy * uy + uz * uz
    rest = 1.0 - 1.5 * speed_sq
    part = []
    for member in range(19):
        if member == 0:
            part.append(pops[0] - (WEIGHTS[0] * rho) * rest)
            continue
        proj = None
        for axis_id in range(3):
            component = VELOCITIES[member][axis_id]
            if component == 1:
                proj = vel[axis_id] if proj is None else proj + vel[axis_id]
            elif component == -1:
                proj = -vel[axis_id] if proj is None else proj - vel[axis_id]
        part.append(pops[member] - (WEIGHTS[member] * rho) * (rest + 3.0 * proj + 4.5 * proj * proj))

    def pair(member):
        return part[member] + part[member + 1]

    in_xy, in_xz, in_yz = pair(7) + pair(9), pair(11) + pair(13), pair(15) + pair(17)
    pxx, pyy, pzz = pair(1) + in_xy + in_xz, pair(3) + in_xy + in_yz, pair(5) + in_xz + in_yz
    pxy, pxz, pyz = pair(7) - pair(9), pair(11) - pair(13), pair(15) - pair(17)
    square = (
        pxx * pxx + pyy * pyy + pzz * pzz + 2.0 * (pxy * pxy + pxz * pxz + pyz * pyz) + QUAD_FLOOR
    )
    size = jnp.sqrt(square)
    root = jnp.sqrt(TAU_BASE * TAU_BASE + SMAG_COEF * size * inv_rho)
    omega = 1.0 / (0.5 * (TAU_BASE + root))
    pux = pxx * ux + pxy * uy + pxz * uz
    puy = pxy * ux + pyy * uy + pyz * uz
    puz = pxz * ux + pyz * uy + pzz * uz
    flux = omega * (3.0 / 36.0)
    drag = (3.0 / 36.0) * thrust_cell * jnp.abs(ux) * inv_rho
    result = list(part)
    result.append(1.0 - omega)
    result.append((omega * (1.0 / 36.0)) * (1.0 + 1.5 * speed_sq))
    result.append(flux)
    result.extend(vel)
    result.extend((pxx, pyy, pzz))
    result.extend((pxx + pyy + 2.0 * pxy, pxx + pyy - 2.0 * pxy))
    result.extend((pxx + pzz + 2.0 * pxz, pxx + pzz - 2.0 * pxz))
    result.extend((pyy + pzz + 2.0 * pyz, pyy + pzz - 2.0 * pyz))
    result.append((0.25 * SMAG_COEF) * omega * omega * inv_rho / (root * size))
    result.append(
        (pux * ux + puy * uy + puz * uz) - (pxx + pyy + pzz) * (1.0 / 3.0) - square * inv_rho
    )
    result.extend((-2.0 * pux, -2.0 * puy, -2.0 * puz))
    result.append(drag)
    result.append(drag * ux)
    result.append((-1.5 / 36.0) * ux * jnp.abs(ux) * slope_cell)
    return result


def plane_adjoint(mu, coef):
    total, diff = {}, {}
    for member in range(1, 19, 2):
        total[member] = mu[member] + mu[member + 1]
        diff[member] = mu[member] - mu[member + 1]
    two_x, two_y, two_z = 2.0 * total[1], 2.0 * total[3], 2.0 * total[5]
    in_xy, in_xz, in_yz = total[7] + total[9], total[11] + total[13], total[15] + total[17]
    mxx, myy, mzz = two_x + in_xy + in_xz, two_y + in_xy + in_yz, two_z + in_xz + in_yz
    mxy, mxz, myz = total[7] - total[9], total[11] - total[13], total[15] - total[17]
    m0 = 12.0 * mu[0] + (two_x + two_y + two_z) + (in_xy + in_xz + in_yz)
    mx = 2.0 * diff[1] + (diff[7] + diff[9]) + (diff[11] + diff[13])
    my = 2.0 * diff[3] + (diff[7] - diff[9]) + (diff[15] + diff[17])
    mz = 2.0 * diff[5] + (diff[11] - diff[13]) + (diff[15] - diff[17])
    ux, uy, uz = coef(UX), coef(UY), coef(UZ)
    vx = mxx * ux + mxy * uy + mxz * uz
    vy = mxy * ux + myy * uy + myz * uz
    vz = mxz * ux + myz * uy + mzz * uz
    along = [mu[member] * coef(member) for member in range(19)]
    while len(along) > 1:
        along = [
            along[k] + along[k + 1] if k + 1 < len(along) else along[k]
            for k in range(0, len(along), 2)
        ]
    gamma = along[0] * coef(RATE)
    flux = coef(FLUX)
    alpha = (
        coef(MASS) * m0
        - 1.5 * flux * (vx * ux + vy * uy + vz * uz)
        + gamma * coef(BULK)
        + mx * coef(DRAG_U)
    )
    beta_x = flux * (mx + 3.0 * vx - ux * m0) + gamma * coef(PX) - mx * coef(DRAG)
    beta_y = flux * (my + 3.0 * vy - uy * m0) + gamma * coef(PY)
    beta_z = flux * (mz + 3.0 * vz - uz * m0) + gamma * coef(PZ)
    keep = coef(KEEP)
    odd = {
        1: beta_x,
        3: beta_y,
        5: beta_z,
        7: beta_x + beta_y,
        9: beta_x - beta_y,
        11: beta_x + beta_z,
        13: beta_x - beta_z,
        15: beta_y + beta_z,
        17: beta_y - beta_z,
    }
    result = [keep * mu[0] + alpha]
    for member in range(1, 19, 2):
        even = alpha + gamma * coef(Q1 + member // 2)
        result.append(keep * mu[member] + (even + odd[member]))
        result.append(keep * mu[member + 1] + (even - odd[member]))
    return result, mx


def coef_kernel(thrust_ref, map_ref, scale_ref, pops_ref, *out_refs):
    steps, width = pops_ref.shape[0], pops_ref.shape[2]
    base = base_values()
    for plane in range(width):
        ids = map_ref[plane]
        ratio = jnp.zeros(ids.shape, jnp.float32)
        for turbine in range(thrust_ref.shape[0]):
            ratio = jnp.where(ids == turbine, thrust_ref[turbine], ratio)
        root = jnp.sqrt(1.0 - ratio)
        square = (1.0 + root) * (1.0 + root)
        inside = ids >= 0
        thrust_cell = jnp.where(inside, 4.0 * ratio / square, 0.0)
        slope_cell = jnp.where(inside, 4.0 / (root * square), 0.0)
        for instant in range(steps):
            scale = scale_ref[instant, plane]
            pops = [
                base[member] * (1.0 + scale * pops_ref[instant, member, plane].astype(jnp.float32))
                for member in range(19)
            ]
            for index, value in enumerate(plane_coefs(pops, thrust_cell, slope_cell)):
                out_refs[instant][index, plane] = value


def write_rows(lam_ref, gain_ref, map_ref, rows_ref):
    width, span = lam_ref.shape[1], lam_ref.shape[2]
    for side, (members, row) in enumerate(((Y_UP, 0), (Y_DOWN, span - 1))):
        for index, member in enumerate(members):
            rows_ref[side, index * width : (index + 1) * width, :] = lam_ref[member, :, row, :]
        if gain_ref is not None:
            start = 5 * width
            rows_ref[side, start : start + width, :] = gain_ref[GAIN, :, row, :]
            rows_ref[side, start + width : start + 2 * width, :] = map_ref[:, row, :].astype(
                jnp.float32
            )


def rows_kernel(lam_ref, rows_ref):
    write_rows(lam_ref, None, None, rows_ref)


def span_shift(value, move, row):
    span = value.shape[0]
    place = lax.broadcasted_iota(jnp.int32, value.shape, 0)
    if move == 1:
        return jnp.where(place == span - 1, row, pltpu.roll(value, span - 1, 0))
    return jnp.where(place == 0, row, pltpu.roll(value, 1, 0))


def moved(lam_ref, rows_ref, member, plane):
    move = VELOCITIES[member][1]
    value = lam_ref[member, plane]
    if move == 0:
        return value
    width = lam_ref.shape[1]
    side, members = (0, Y_UP) if move == 1 else (1, Y_DOWN)
    place = members.index(member) * width + plane
    return span_shift(value, move, rows_ref[side, place : place + 1, :])


def faces_kernel(has_gain, *refs):
    if has_gain:
        lam_ref, rows_ref, coef_ref, map_ref, low_ref, high_ref = refs
    else:
        lam_ref, rows_ref, low_ref, high_ref = refs
    width = lam_ref.shape[1]
    for members, plane, out_ref in ((X_UP, 0, low_ref), (X_DOWN, width - 1, high_ref)):
        for index, member in enumerate(members):
            out_ref[index] = moved(lam_ref, rows_ref, member, plane)
        if has_gain:
            out_ref[5] = coef_ref[GAIN, plane]
            out_ref[6] = map_ref[plane].astype(jnp.float32)
            out_ref[7] = jnp.zeros(out_ref.shape[1:], jnp.float32)
            for side in range(2):
                for field in range(2):
                    place = (5 + field) * width + plane
                    out_ref[7, 2 * field + side : 2 * field + side + 1, :] = rows_ref[
                        side, place : place + 1, :
                    ]


def step_kernel(kind, turbines, *refs):
    lam_ref, rows_ref, above_ref, below_ref, coef_ref = refs[:5]
    width, span, height = lam_ref.shape[1:]
    if kind == 0:
        next_ref, map_ref, out_ref, next_rows_ref, cell_ref = refs[5:]
    elif kind == 1:
        next_ref, map_ref, cell_ref, out_ref, next_rows_ref, sums_ref, pad_ref = refs[5:]
    else:
        (out_ref,) = refs[5:]
    lane = lax.broadcasted_iota(jnp.int32, (span, height), 1)
    first, last = lane == 0, lane == height - 1
    totals = []
    for plane in range(width):
        mu = []
        for member in range(19):
            move_x, _, move_z = VELOCITIES[member]
            source = plane + move_x
            if source < 0:
                value = below_ref[X_DOWN.index(member)]
            elif source >= width:
                value = above_ref[X_UP.index(member)]
            else:
                value = moved(lam_ref, rows_ref, member, source)
            if move_z == 1:
                value = jnp.where(
                    last, lam_ref[OPPOSITE[member], plane], pltpu.roll(value, height - 1, 1)
                )
            elif move_z == -1:
                value = jnp.where(first, lam_ref[OPPOSITE[member], plane], pltpu.roll(value, 1, 1))
            mu.append(value)
        lam, mx = plane_adjoint(mu, lambda index: coef_ref[index, plane])
        for member in range(19):
            out_ref[member, plane] = lam[member]
        if kind == 0:
            cell_ref[plane] = mx * coef_ref[GAIN, plane]
        elif kind == 1:
            totals.append(cell_ref[plane] + mx * coef_ref[GAIN, plane])
    if kind < 2:
        write_rows(
            out_ref, next_ref if kind == 0 else None, map_ref if kind == 0 else None, next_rows_ref
        )
    if kind == 1:
        sum_turbines(
            turbines,
            out_ref,
            next_ref,
            map_ref,
            rows_ref,
            above_ref,
            below_ref,
            totals,
            sums_ref,
            pad_ref,
            first,
            last,
        )


def sum_turbines(
    turbines,
    lam_ref,
    coef_ref,
    map_ref,
    rows_ref,
    above_ref,
    below_ref,
    totals,
    sums_ref,
    pad_ref,
    first,
    last,
):
    width, span, height = lam_ref.shape[1:]

    def roll_z(value, move):
        if move == 1:
            return jnp.where(last, 0.0, pltpu.roll(value, height - 1, 1))
        return jnp.where(first, 0.0, pltpu.roll(value, 1, 1))

    nothing = jnp.zeros((1, height), jnp.float32)
    up, down = [], []
    for plane in range(width):
        up.append(
            2.0 * lam_ref[1, plane]
            + span_shift(lam_ref[7, plane], 1, nothing)
            + span_shift(lam_ref[9, plane], -1, nothing)
            + roll_z(lam_ref[11, plane], 1)
            + roll_z(lam_ref[13, plane], -1)
        )
        down.append(
            2.0 * lam_ref[2, plane]
            + span_shift(lam_ref[8, plane], -1, nothing)
            + span_shift(lam_ref[10, plane], 1, nothing)
            + roll_z(lam_ref[12, plane], -1)
            + roll_z(lam_ref[14, plane], 1)
        )
    tiles = []
    for plane in range(-1, width + 1):
        value = None
        if plane + 1 < width:
            value = up[plane + 1]
        if plane >= 1:
            value = -down[plane - 1] if value is None else value - down[plane - 1]
        if plane < 0:
            tiles.append((below_ref[5] * value, below_ref[6]))
        elif plane >= width:
            tiles.append((above_ref[5] * value, above_ref[6]))
        else:
            value = value + jnp.where(last, lam_ref[12, plane] - lam_ref[13, plane], 0.0)
            value = value + jnp.where(first, lam_ref[14, plane] - lam_ref[11, plane], 0.0)
            tiles.append(
                (
                    totals[plane] + coef_ref[GAIN, plane] * value,
                    map_ref[plane].astype(jnp.float32),
                )
            )
    for side, (upward, downward, row) in enumerate(((9, 8, span - 1), (7, 10, 0))):
        pad_ref[0] = jnp.zeros(pad_ref.shape[1:], jnp.float32)
        pad_ref[1] = jnp.zeros(pad_ref.shape[1:], jnp.float32)
        pad_ref[2] = jnp.zeros(pad_ref.shape[1:], jnp.float32)
        pad_ref[3] = jnp.full(pad_ref.shape[1:], -1.0, jnp.float32)
        pad_ref[0, 0:width, :] = lam_ref[upward, :, row, :]
        pad_ref[1, 2 : width + 2, :] = lam_ref[downward, :, row, :]
        for field in range(2):
            place = (5 + field) * width
            pad_ref[2 + field, 1 : width + 1, :] = rows_ref[side, place : place + width, :]
            pick = 2 * field + side
            pad_ref[2 + field, 0:1, :] = below_ref[7, pick : pick + 1, :]
            pad_ref[2 + field, width + 1 : width + 2, :] = above_ref[7, pick : pick + 1, :]
        tiles.append(((pad_ref[0] - pad_ref[1]) * pad_ref[2], pad_ref[3]))
    sums_ref[...] = jnp.zeros(sums_ref.shape, jnp.float32)
    for turbine in range(turbines):
        row = None
        for value, ids in tiles:
            kept = jnp.sum(jnp.where(ids == float(turbine), value, 0.0), axis=0, keepdims=True)
            row = kept if row is None else row + kept
        sums_ref[turbine : turbine + 1, :] = row


def call(kernel, outs, *args, scratch=(), smem_first=False, micros=1):
    specs = [pl.BlockSpec(memory_space=VMEM)] * len(args)
    if smem_first:
        specs[0] = pl.BlockSpec(memory_space=pltpu.SMEM)
    return pl.pallas_call(
        kernel,
        out_shape=tuple(jax.ShapeDtypeStruct(shape, jnp.float32) for shape in outs),
        in_specs=specs,
        out_specs=tuple(pl.BlockSpec(memory_space=VMEM) for _ in outs),
        scratch_shapes=list(scratch),
        cost_estimate=pl.CostEstimate(
            flops=int(1e6 * micros), bytes_accessed=int(2e6 * micros), transcendentals=0
        ),
        compiler_params=pltpu.CompilerParams(vmem_limit_bytes=32 * 1024 * 1024),
    )(*args)


def ring(axis, step):
    count = lax.axis_size(axis)
    return [(i, (i + step) % count) for i in range(count)]


def swap_rows(rows):
    if lax.axis_size("gy") == 2:
        return lax.ppermute(rows, "gy", ring("gy", 1))
    return jnp.stack(
        [
            lax.ppermute(rows[0], "gy", ring("gy", -1)),
            lax.ppermute(rows[1], "gy", ring("gy", 1)),
        ]
    )


def swap_faces(low, high):
    above = lax.ppermute(low, "gx", ring("gx", -1))
    below = lax.ppermute(high, "gx", ring("gx", 1))
    return above, below


def total(value):
    for axis, stages in (("gx", (1, 1, 2, 2, 2)), ("gy", (1, 1, 1, 1))):
        count = lax.axis_size(axis)
        if count & (count - 1):
            value = lax.psum(value, axis)
            continue
        start = 1
        for bits in stages:
            stop = min(start << bits, count)
            if start >= stop:
                break
            parts = [value]
            for flip in range(start, stop, start):
                parts.append(lax.ppermute(value, axis, [(i, i ^ flip) for i in range(count)]))
            value = sum(parts[1:], parts[0])
            start = stop
        assert start >= count
    return value


def shards(fwd_pops, fwd_scale, seed_adjoint, turbine_map, thrust):
    steps, _, width, span, height = fwd_pops.shape
    turbines = thrust.shape[0]
    whole = (19, width, span, height)
    coefs = call(
        coef_kernel,
        [(COEFS, width, span, height)] * steps,
        thrust,
        turbine_map,
        fwd_scale,
        fwd_pops,
        smem_first=True,
        micros=1.5,
    )
    lam = seed_adjoint
    (rows,) = call(rows_kernel, [(2, 5 * width, height)], lam, micros=0.2)
    cells = None
    sums = None
    for instant in range(steps - 1, -1, -1):
        got_rows = swap_rows(rows)
        has_gain = instant == 1
        static = (coefs[0], turbine_map) if has_gain else ()
        face = ((8 if has_gain else 5), span, height)
        low, high = call(
            lambda *refs, has_gain=has_gain: faces_kernel(has_gain, *refs),
            [face, face],
            lam,
            got_rows,
            *static,
            micros=0.2,
        )
        above, below = swap_faces(low, high)
        common = (lam, got_rows, above, below, coefs[instant])
        if instant == 2:
            lam, rows, cells = call(
                lambda *refs: step_kernel(0, turbines, *refs),
                [whole, (2, 7 * width, height), (width, span, height)],
                *common,
                coefs[0],
                turbine_map,
                micros=0.5,
            )
        elif instant == 1:
            lam, rows, sums = call(
                lambda *refs: step_kernel(1, turbines, *refs),
                [whole, (2, 5 * width, height), (-(-turbines // 8) * 8, height)],
                *common,
                coefs[0],
                turbine_map,
                cells,
                scratch=[pltpu.VMEM((4, -(-(width + 2) // 8) * 8, height), jnp.float32)],
                micros=0.7,
            )
        else:
            (lam,) = call(
                lambda *refs: step_kernel(2, turbines, *refs), [whole], *common, micros=0.5
            )
    thrust_grad = jnp.sum(total(sums), axis=1)[:turbines]
    return (lam, thrust_grad)


def solution(mesh):
    placed = (
        P(None, None, "gx", "gy", None),
        P(None, "gx", "gy", None),
        P(None, "gx", "gy", None),
        P("gx", "gy", None),
        P(),
    )
    return jax.shard_map(
        shards,
        mesh=mesh,
        in_specs=placed,
        out_specs=(P(None, "gx", "gy", None), P()),
        check_vma=False,
    )
```

```python
import jax
import jax.numpy as jnp
from jax import lax
from jax.experimental import pallas as pl
from jax.experimental.pallas import tpu as pltpu
from jax.sharding import PartitionSpec as P

VELOCITIES = (
    (0, 0, 0),
    (1, 0, 0),
    (-1, 0, 0),
    (0, 1, 0),
    (0, -1, 0),
    (0, 0, 1),
    (0, 0, -1),
    (1, 1, 0),
    (-1, -1, 0),
    (1, -1, 0),
    (-1, 1, 0),
    (1, 0, 1),
    (-1, 0, -1),
    (1, 0, -1),
    (-1, 0, 1),
    (0, 1, 1),
    (0, -1, -1),
    (0, 1, -1),
    (0, -1, 1),
)
OPPOSITE = (0, 2, 1, 4, 3, 6, 5, 8, 7, 10, 9, 12, 11, 14, 13, 16, 15, 18, 17)
WEIGHTS = tuple([1.0 / 3.0] + [1.0 / 18.0] * 6 + [1.0 / 36.0] * 12)
MEAN_FLOW = 0.1
TAU_BASE = 0.51
SMAG_COEF = 18.0 * 1.4142135623730951 * 0.17 * 0.17
QUAD_FLOOR = 0.0001

X_UP = (1, 7, 9, 11, 13)
X_DOWN = (2, 8, 10, 12, 14)
Y_UP = (3, 7, 10, 15, 17)
Y_DOWN = (4, 8, 9, 16, 18)

KEEP, MASS, FLUX, UX, UY, UZ, Q1 = 19, 20, 21, 22, 23, 24, 25
RATE, BULK, PX, PY, PZ, DRAG, DRAG_U, GAIN = 34, 35, 36, 37, 38, 39, 40, 41
COEFS = 42

FIELDS = 21

VMEM = pltpu.VMEM


def halo_list(axis, sign):
    near = [
        (1, m) for m in range(19) if VELOCITIES[m][axis] * sign >= 0 or VELOCITIES[m][2] != 0
    ]
    return near + [(2, m) for m in range(19) if VELOCITIES[m][axis] * sign == 1]


SIGNS = (1, -1)
FACE_LIST = [halo_list(0, sign) for sign in SIGNS]
ROW_LIST = [halo_list(1, sign) for sign in SIGNS]
INNER_LIST = [[(0, m) for m in range(19) if VELOCITIES[m][1] * sign == -1] for sign in SIGNS]
PACK_LIST = [ROW_LIST[side] + INNER_LIST[side] for side in range(2)]
CORNER_LIST = [
    [
        [(far_x, far_y, m) for far_x, m in FACE_LIST[x] for far_y in (1, 2) if (far_y, m) in ROW_LIST[y]]
        for y in range(2)
    ]
    for x in range(2)
]
HALO = len(ROW_LIST[0])
CORNER = len(CORNER_LIST[0][0])
FACE_TILES = HALO + FIELDS


def base_values():
    values = []
    for member in range(19):
        along = float(VELOCITIES[member][0])
        values.append(
            WEIGHTS[member]
            * (
                1.0
                + 3.0 * MEAN_FLOW * along
                + 4.5 * MEAN_FLOW * MEAN_FLOW * along * along
                - 1.5 * MEAN_FLOW * MEAN_FLOW
            )
        )
    return values


def plane_coefs(pops, thrust_cell, slope_cell):
    rho = pops[0]
    for member in range(1, 19):
        rho = rho + pops[member]
    inv_rho = 1.0 / rho
    vel = []
    for axis_id in range(3):
        moment = None
        for member in range(19):
            component = VELOCITIES[member][axis_id]
            if component == 1:
                moment = pops[member] if moment is None else moment + pops[member]
            elif component == -1:
                moment = moment - pops[member]
        vel.append(moment * inv_rho)
    ux, uy, uz = vel
    speed_sq = ux * ux + uy * uy + uz * uz
    rest = 1.0 - 1.5 * speed_sq
    part = []
    for member in range(19):
        if member == 0:
            part.append(pops[0] - (WEIGHTS[0] * rho) * rest)
            continue
        proj = None
        for axis_id in range(3):
            component = VELOCITIES[member][axis_id]
            if component == 1:
                proj = vel[axis_id] if proj is None else proj + vel[axis_id]
            elif component == -1:
                proj = -vel[axis_id] if proj is None else proj - vel[axis_id]
        part.append(pops[member] - (WEIGHTS[member] * rho) * (rest + 3.0 * proj + 4.5 * proj * proj))

    def pair(member):
        return part[member] + part[member + 1]

    in_xy, in_xz, in_yz = pair(7) + pair(9), pair(11) + pair(13), pair(15) + pair(17)
    pxx, pyy, pzz = pair(1) + in_xy + in_xz, pair(3) + in_xy + in_yz, pair(5) + in_xz + in_yz
    pxy, pxz, pyz = pair(7) - pair(9), pair(11) - pair(13), pair(15) - pair(17)
    square = (
        pxx * pxx + pyy * pyy + pzz * pzz + 2.0 * (pxy * pxy + pxz * pxz + pyz * pyz) + QUAD_FLOOR
    )
    size = jnp.sqrt(square)
    root = jnp.sqrt(TAU_BASE * TAU_BASE + SMAG_COEF * size * inv_rho)
    omega = 1.0 / (0.5 * (TAU_BASE + root))
    pux = pxx * ux + pxy * uy + pxz * uz
    puy = pxy * ux + pyy * uy + pyz * uz
    puz = pxz * ux + pyz * uy + pzz * uz
    flux = omega * (3.0 / 36.0)
    drag = (3.0 / 36.0) * thrust_cell * jnp.abs(ux) * inv_rho
    result = list(part)
    result.append(1.0 - omega)
    result.append((omega * (1.0 / 36.0)) * (1.0 + 1.5 * speed_sq))
    result.append(flux)
    result.extend(vel)
    result.extend((pxx, pyy, pzz))
    result.extend((pxx + pyy + 2.0 * pxy, pxx + pyy - 2.0 * pxy))
    result.extend((pxx + pzz + 2.0 * pxz, pxx + pzz - 2.0 * pxz))
    result.extend((pyy + pzz + 2.0 * pyz, pyy + pzz - 2.0 * pyz))
    result.append((0.25 * SMAG_COEF) * omega * omega * inv_rho / (root * size))
    result.append(
        (pux * ux + puy * uy + puz * uz) - (pxx + pyy + pzz) * (1.0 / 3.0) - square * inv_rho
    )
    result.extend((-2.0 * pux, -2.0 * puy, -2.0 * puz))
    result.append(drag)
    result.append(drag * ux)
    if slope_cell is not None:
        result.append((-1.5 / 36.0) * ux * jnp.abs(ux) * slope_cell)
    return result


def plane_adjoint(mu, coef, wanted=range(19)):
    total, diff = {}, {}
    for member in range(1, 19, 2):
        total[member] = mu[member] + mu[member + 1]
        diff[member] = mu[member] - mu[member + 1]
    two_x, two_y, two_z = 2.0 * total[1], 2.0 * total[3], 2.0 * total[5]
    in_xy, in_xz, in_yz = total[7] + total[9], total[11] + total[13], total[15] + total[17]
    mxx, myy, mzz = two_x + in_xy + in_xz, two_y + in_xy + in_yz, two_z + in_xz + in_yz
    mxy, mxz, myz = total[7] - total[9], total[11] - total[13], total[15] - total[17]
    m0 = 12.0 * mu[0] + (two_x + two_y + two_z) + (in_xy + in_xz + in_yz)
    mx = 2.0 * diff[1] + (diff[7] + diff[9]) + (diff[11] + diff[13])
    my = 2.0 * diff[3] + (diff[7] - diff[9]) + (diff[15] + diff[17])
    mz = 2.0 * diff[5] + (diff[11] - diff[13]) + (diff[15] - diff[17])
    ux, uy, uz = coef(UX), coef(UY), coef(UZ)
    vx = mxx * ux + mxy * uy + mxz * uz
    vy = mxy * ux + myy * uy + myz * uz
    vz = mxz * ux + myz * uy + mzz * uz
    along = [mu[member] * coef(member) for member in range(19)]
    while len(along) > 1:
        along = [
            along[k] + along[k + 1] if k + 1 < len(along) else along[k]
            for k in range(0, len(along), 2)
        ]
    gamma = along[0] * coef(RATE)
    flux = coef(FLUX)
    alpha = (
        coef(MASS) * m0
        - 1.5 * flux * (vx * ux + vy * uy + vz * uz)
        + gamma * coef(BULK)
        + mx * coef(DRAG_U)
    )
    beta_x = flux * (mx + 3.0 * vx - ux * m0) + gamma * coef(PX) - mx * coef(DRAG)
    beta_y = flux * (my + 3.0 * vy - uy * m0) + gamma * coef(PY)
    beta_z = flux * (mz + 3.0 * vz - uz * m0) + gamma * coef(PZ)
    keep = coef(KEEP)
    odd = {
        1: beta_x,
        3: beta_y,
        5: beta_z,
        7: beta_x + beta_y,
        9: beta_x - beta_y,
        11: beta_x + beta_z,
        13: beta_x - beta_z,
        15: beta_y + beta_z,
        17: beta_y - beta_z,
    }
    result = {}
    for member in wanted:
        if member == 0:
            result[0] = keep * mu[0] + alpha
            continue
        forward = member - 1 + member % 2
        even = alpha + gamma * coef(Q1 + forward // 2)
        if member == forward:
            result[member] = keep * mu[member] + (even + odd[forward])
        else:
            result[member] = keep * mu[member] + (even - odd[forward])
    return result, mx


def turbine_cells(ids, thrust_ref, slope):
    ratio = jnp.zeros(ids.shape, jnp.float32)
    for turbine in range(thrust_ref.shape[0]):
        ratio = jnp.where(ids == jnp.asarray(turbine, ids.dtype), thrust_ref[turbine], ratio)
    root = jnp.sqrt(1.0 - ratio)
    square = (1.0 + root) * (1.0 + root)
    inside = ids >= 0
    thrust_cell = jnp.where(inside, 4.0 * ratio / square, 0.0)
    return thrust_cell, jnp.where(inside, 4.0 / (root * square), 0.0) if slope else None


def decode(scale_ref, pops_ref, instant, plane):
    base = base_values()
    scale = scale_ref[instant, plane]
    return [
        base[member] * (1.0 + scale * pops_ref[instant, member, plane].astype(jnp.float32))
        for member in range(19)
    ]


def coef_kernel(thrust_ref, map_ref, scale_ref, pops_ref, *out_refs):
    for plane in range(pops_ref.shape[2]):
        thrust_cell, slope_cell = turbine_cells(map_ref[plane], thrust_ref, True)
        for instant, out_ref in enumerate(out_refs):
            pops = decode(scale_ref, pops_ref, instant, plane)
            for index, value in enumerate(plane_coefs(pops, thrust_cell, slope_cell)):
                out_ref[index, plane] = value


def pack_kernel(last, thrust_ref, map_ref, scale_ref, pops_ref, lam_ref, fields_ref, rows_ref):
    width, span = lam_ref.shape[1], lam_ref.shape[2]
    for plane in range(width):
        for index, value in enumerate(decode(scale_ref, pops_ref, last, plane)):
            fields_ref[index, plane] = value
        fields_ref[19, plane] = map_ref[plane].astype(jnp.float32)
        _, slope_cell = turbine_cells(map_ref[plane], thrust_ref, True)
        pops = decode(scale_ref, pops_ref, 0, plane)
        rho, momentum = pops[0], None
        for member in range(1, 19):
            rho = rho + pops[member]
        for member in X_UP:
            pair = pops[member] - pops[member + 1]
            momentum = pair if momentum is None else momentum + pair
        ux = momentum / rho
        fields_ref[20, plane] = (-1.5 / 36.0) * ux * jnp.abs(ux) * slope_cell
    for side in range(2):
        for index, (far, member) in enumerate(ROW_LIST[side]):
            row = far - 1 if side == 0 else span - far
            rows_ref[side, index * width : (index + 1) * width, :] = lam_ref[member, :, row, :]
        row = 0 if side == 0 else span - 1
        for field in range(FIELDS):
            start = (HALO + field) * width
            rows_ref[side, start : start + width, :] = fields_ref[field, :, row, :]


def faces_kernel(lam_ref, fields_ref, rows_ref, *out_refs):
    width = lam_ref.shape[1]
    for x_side, out_ref in enumerate(out_refs):

        def plane(far, x_side=x_side):
            return far - 1 if x_side == 0 else width - far

        for index, (far, member) in enumerate(FACE_LIST[x_side]):
            out_ref[index] = lam_ref[member, plane(far)]
        for field in range(FIELDS):
            out_ref[HALO + field] = fields_ref[field, plane(1)]
        slot = 0
        for y_side in range(2):
            picks = [
                ROW_LIST[y_side].index((far_y, member)) * width + plane(far_x)
                for far_x, far_y, member in CORNER_LIST[x_side][y_side]
            ]
            picks += [(HALO + field) * width + plane(1) for field in range(FIELDS)]
            for pick in picks:
                tile, row = FACE_TILES + slot // 8, slot % 8
                out_ref[tile, row : row + 1, :] = rows_ref[y_side, pick : pick + 1, :]
                slot += 1


def span_shift(value, move, row):
    span = value.shape[0]
    place = lax.broadcasted_iota(jnp.int32, value.shape, 0)
    if move == 1:
        return jnp.where(place == span - 1, row, pltpu.roll(value, span - 1, 0))
    return jnp.where(place == 0, row, pltpu.roll(value, 1, 0))


def gather_mu(source, row_of, plane, first, last):
    mu = []
    for member in range(19):
        move_x, move_y, move_z = VELOCITIES[member]
        value = source(plane + move_x, member)
        if move_y != 0:
            side = 0 if move_y == 1 else 1
            value = span_shift(value, move_y, row_of(side, plane + move_x, member))
        mu.append(bounce(value, move_z, source, plane, member, first, last))
    return mu


def bounce(value, move_z, source, plane, member, first, last):
    height = value.shape[1]
    if move_z == 1:
        return jnp.where(
            last, source(plane, OPPOSITE[member]), pltpu.roll(value, height - 1, 1)
        )
    if move_z == -1:
        return jnp.where(first, source(plane, OPPOSITE[member]), pltpu.roll(value, 1, 1))
    return value


def pair_kernel(thrust_ref, lam_ref, rows_ref, above_ref, below_ref, late_ref, early_ref, fields_ref,
                out_ref, next_ref, pack_ref, field_ref, mid_ref, face_ref, edge_ref):
    width, span, height = lam_ref.shape[1:]
    faces = (above_ref, below_ref)
    lane = lax.broadcasted_iota(jnp.int32, (span, height), 1)
    first, last = lane == 0, lane == height - 1
    pack_lane = lax.broadcasted_iota(jnp.int32, pack_ref.shape[2:], 1)
    pack_first, pack_last = pack_lane == 0, pack_lane == height - 1

    def seed(plane, member):
        if plane >= width:
            return above_ref[FACE_LIST[0].index((plane - width + 1, member))]
        if plane < 0:
            return below_ref[FACE_LIST[1].index((-plane, member))]
        return lam_ref[member, plane]

    outside = {0: (width + 2, 1), 1: (1, -1)}
    pack_ref[...] = jnp.zeros(pack_ref.shape, jnp.float32)
    field_ref[...] = jnp.zeros(field_ref.shape, jnp.float32)
    for y_side in range(2):
        inner = span - 1 if y_side == 0 else 0
        for index, (far, member) in enumerate(PACK_LIST[y_side]):
            if far > 0:
                pack_ref[y_side, index, 2 : width + 2, :] = rows_ref[
                    y_side, index * width : (index + 1) * width, :
                ]
                continue
            pack_ref[y_side, index, 2 : width + 2, :] = lam_ref[member, :, inner, :]
            for x_side in range(2):
                start, step = outside[x_side]
                for far_x in (1, 2):
                    if (far_x, member) in FACE_LIST[x_side]:
                        place = start + step * (far_x - 1)
                        tile = FACE_LIST[x_side].index((far_x, member))
                        pack_ref[y_side, index, place : place + 1, :] = faces[x_side][
                            tile, inner : inner + 1, :
                        ]
        for field in range(FIELDS):
            start = (HALO + field) * width
            field_ref[y_side, field, 2 : width + 2, :] = rows_ref[y_side, start : start + width, :]
        for x_side in range(2):
            start, step = outside[x_side]
            slot = y_side * (CORNER + FIELDS)
            for far_x, far_y, member in CORNER_LIST[x_side][y_side]:
                place = start + step * (far_x - 1)
                index = PACK_LIST[y_side].index((far_y, member))
                tile, row = FACE_TILES + slot // 8, slot % 8
                pack_ref[y_side, index, place : place + 1, :] = faces[x_side][tile, row : row + 1, :]
                slot += 1
            for field in range(FIELDS):
                tile, row = FACE_TILES + slot // 8, slot % 8
                field_ref[y_side, field, start : start + 1, :] = faces[x_side][
                    tile, row : row + 1, :
                ]
                slot += 1

    def seed_row(side, plane, member):
        index = PACK_LIST[side].index((1, member))
        return pack_ref[side, index, plane + 2 : plane + 3, :]

    totals = []
    for plane in range(-1, width + 1):
        mu = gather_mu(seed, seed_row, plane, first, last)
        if 0 <= plane < width:
            lam, mx = plane_adjoint(mu, lambda index: late_ref[index, plane])
            for member in range(19):
                mid_ref[member, plane] = lam[member]
            totals.append(mx * late_ref[GAIN, plane])
            continue
        side, wanted = (0, X_UP) if plane >= width else (1, X_DOWN)
        pops = [faces[side][HALO + member] for member in range(19)]
        thrust_cell, _ = turbine_cells(faces[side][HALO + 19], thrust_ref, False)
        coefs = plane_coefs(pops, thrust_cell, None)
        lam, _ = plane_adjoint(mu, lambda index: coefs[index], wanted)
        for index, member in enumerate(wanted):
            face_ref[side, index] = lam[member]
    for side, (sign, wanted) in enumerate(((1, Y_UP), (-1, Y_DOWN))):

        def edge(_, member, side=side):
            return pack_ref[side, PACK_LIST[side].index((1, member))]

        mu = []
        for member in range(19):
            move_x, move_y, move_z = VELOCITIES[member]
            value = pack_ref[side, PACK_LIST[side].index((1 + sign * move_y, member))]
            if move_x != 0:
                value = pltpu.roll(value, (-move_x) % value.shape[0], 0)
            mu.append(bounce(value, move_z, edge, None, member, pack_first, pack_last))
        pops = [field_ref[side, member] for member in range(19)]
        thrust_cell, _ = turbine_cells(field_ref[side, 19], thrust_ref, False)
        coefs = plane_coefs(pops, thrust_cell, None)
        lam, _ = plane_adjoint(mu, lambda index: coefs[index], wanted)
        for index, member in enumerate(wanted):
            edge_ref[side, index] = lam[member]

    def middle(plane, member):
        if plane >= width:
            return face_ref[0, X_UP.index(member)]
        if plane < 0:
            return face_ref[1, X_DOWN.index(member)]
        return mid_ref[member, plane]

    def middle_row(side, plane, member):
        index = (Y_UP, Y_DOWN)[side].index(member)
        return edge_ref[side, index, plane + 2 : plane + 3, :]

    for plane in range(width):
        mu = gather_mu(middle, middle_row, plane, first, last)
        lam, mx = plane_adjoint(mu, lambda index: early_ref[index, plane])
        for member in range(19):
            out_ref[member, plane] = lam[member]
        totals[plane] = totals[plane] + mx * early_ref[GAIN, plane]

    for side, (members, row) in enumerate(((Y_UP, 0), (Y_DOWN, span - 1))):
        for index, member in enumerate(members):
            start = (5 * side + index) * width
            next_ref[start : start + width, :] = out_ref[member, :, row, :]

    def roll_z(value, move):
        if move == 1:
            return jnp.where(last, 0.0, pltpu.roll(value, height - 1, 1))
        return jnp.where(first, 0.0, pltpu.roll(value, 1, 1))

    nothing = jnp.zeros((1, height), jnp.float32)
    up, down = [], []
    for plane in range(width):
        up.append(
            2.0 * out_ref[1, plane]
            + span_shift(out_ref[7, plane], 1, nothing)
            + span_shift(out_ref[9, plane], -1, nothing)
            + roll_z(out_ref[11, plane], 1)
            + roll_z(out_ref[13, plane], -1)
        )
        down.append(
            2.0 * out_ref[2, plane]
            + span_shift(out_ref[8, plane], -1, nothing)
            + span_shift(out_ref[10, plane], 1, nothing)
            + roll_z(out_ref[12, plane], -1)
            + roll_z(out_ref[14, plane], 1)
        )
    tiles = []
    for plane in range(-1, width + 1):
        value = None
        if plane + 1 < width:
            value = up[plane + 1]
        if plane >= 1:
            value = -down[plane - 1] if value is None else value - down[plane - 1]
        if plane < 0 or plane >= width:
            face = below_ref if plane < 0 else above_ref
            tiles.append((face[HALO + 20] * value, face[HALO + 19]))
            continue
        value = value + jnp.where(last, out_ref[12, plane] - out_ref[13, plane], 0.0)
        value = value + jnp.where(first, out_ref[14, plane] - out_ref[11, plane], 0.0)
        tiles.append((totals[plane] + fields_ref[20, plane] * value, fields_ref[19, plane]))
    for side, (upward, downward, row) in enumerate(((9, 8, span - 1), (7, 10, 0))):
        pack_ref[side, 0] = jnp.zeros(pack_ref.shape[2:], jnp.float32)
        pack_ref[side, 1] = jnp.zeros(pack_ref.shape[2:], jnp.float32)
        pack_ref[side, 0, 1 : width + 1, :] = out_ref[upward, :, row, :]
        pack_ref[side, 1, 3 : width + 3, :] = out_ref[downward, :, row, :]
        tiles.append(
            (
                (pack_ref[side, 0] - pack_ref[side, 1]) * field_ref[side, 20],
                field_ref[side, 19],
            )
        )
    start = 10 * width
    next_ref[start:, :] = jnp.zeros((next_ref.shape[0] - start, height), jnp.float32)
    for turbine in range(thrust_ref.shape[0]):
        row = None
        for value, ids in tiles:
            kept = jnp.sum(jnp.where(ids == float(turbine), value, 0.0), axis=0, keepdims=True)
            row = kept if row is None else row + kept
        next_ref[start + turbine : start + turbine + 1, :] = row


def by_parity(even):
    odd = lax.rem(lax.axis_index("gx"), 2) == 1
    pl.when(jnp.logical_not(odd))(lambda: even(True))
    pl.when(odd)(lambda: even(False))


def last_faces_kernel(lam_ref, rows_ref, sums_ref, near_ref, far_ref):
    width = lam_ref.shape[1]

    def row_of(side, plane, member):
        place = (5 * side + (Y_UP, Y_DOWN)[side].index(member)) * width + plane
        return rows_ref[place : place + 1, :]

    def write(even):
        outs = (far_ref, near_ref) if even else (near_ref, far_ref)
        for members, plane, out_ref in ((X_UP, 0, outs[0]), (X_DOWN, width - 1, outs[1])):
            for index, member in enumerate(members):
                move_y = VELOCITIES[member][1]
                value = lam_ref[member, plane]
                if move_y != 0:
                    value = span_shift(
                        value, move_y, row_of(0 if move_y == 1 else 1, plane, member)
                    )
                out_ref[index] = value

    by_parity(write)
    for tile in range(near_ref.shape[0] - 5):
        near_ref[5 + tile] = sums_ref[8 * tile : 8 * tile + 8, :]


def last_far_kernel(far_ref, near_ref, got_ref, out_ref):
    for tile in range(5):
        out_ref[tile] = far_ref[tile]
    for tile in range(5, out_ref.shape[0]):
        out_ref[tile] = near_ref[tile] + got_ref[tile]


def last_kernel(lam_ref, rows_ref, near_ref, far_ref, coef_ref, out_ref):
    width, span, height = lam_ref.shape[1:]
    lane = lax.broadcasted_iota(jnp.int32, (span, height), 1)
    first, last = lane == 0, lane == height - 1
    odd = jnp.full((span, height), lax.rem(lax.axis_index("gx"), 2)) == 1

    def source(plane, member):
        if plane >= width:
            index = X_UP.index(member)
            return jnp.where(odd, far_ref[index], near_ref[index])
        if plane < 0:
            index = X_DOWN.index(member)
            return jnp.where(odd, near_ref[index], far_ref[index])
        value, move_y = lam_ref[member, plane], VELOCITIES[member][1]
        if move_y == 0:
            return value
        side = 0 if move_y == 1 else 1
        place = (5 * side + (Y_UP, Y_DOWN)[side].index(member)) * width + plane
        return span_shift(value, move_y, rows_ref[place : place + 1, :])

    for plane in range(width):
        mu = []
        for member in range(19):
            move_x, _, move_z = VELOCITIES[member]
            value = source(plane + move_x, member)
            if move_z == 1:
                value = jnp.where(
                    last, lam_ref[OPPOSITE[member], plane], pltpu.roll(value, height - 1, 1)
                )
            elif move_z == -1:
                value = jnp.where(first, lam_ref[OPPOSITE[member], plane], pltpu.roll(value, 1, 1))
            mu.append(value)
        lam, _ = plane_adjoint(mu, lambda index: coef_ref[index, plane])
        for member in range(19):
            out_ref[member, plane] = lam[member]


def call(kernel, outs, *args, scratch=(), smem_first=False, micros=1):
    specs = [pl.BlockSpec(memory_space=VMEM)] * len(args)
    if smem_first:
        specs[0] = pl.BlockSpec(memory_space=pltpu.SMEM)
    return pl.pallas_call(
        kernel,
        out_shape=tuple(jax.ShapeDtypeStruct(shape, jnp.float32) for shape in outs),
        in_specs=specs,
        out_specs=tuple(pl.BlockSpec(memory_space=VMEM) for _ in outs),
        scratch_shapes=[pltpu.VMEM(shape, jnp.float32) for shape in scratch],
        cost_estimate=pl.CostEstimate(
            flops=int(1e6 * micros), bytes_accessed=int(2e6 * micros), transcendentals=0
        ),
        compiler_params=pltpu.CompilerParams(vmem_limit_bytes=32 * 1024 * 1024),
    )(*args)


def ring(axis, step):
    count = lax.axis_size(axis)
    return [(i, (i + step) % count) for i in range(count)]


def swap_rows(low, high):
    return lax.ppermute(low, "gy", ring("gy", -1)), lax.ppermute(high, "gy", ring("gy", 1))


def flips(value, axis, flip_list):
    count = lax.axis_size(axis)
    parts = [lax.ppermute(value, axis, [(i, i ^ flip) for i in range(count)]) for flip in flip_list]
    return sum(parts, value)


def sum_bits(value, axis, start):
    count = lax.axis_size(axis)
    while start < count:
        stop = min(4 * start, count)
        value = flips(value, axis, range(start, stop, start))
        start = stop
    return value


def last_exchange(lam, packed, turbine_rows, has_pairs):
    width, height = lam.shape[1], lam.shape[3]
    rows_count = 10 * width
    if lax.axis_size("gy") == 2:
        got = lax.ppermute(packed, "gy", ring("gy", 1))
        rows, sums = got, packed[rows_count:] + got[rows_count:]
    else:
        low, high = swap_rows(packed[: rows_count // 2], packed[rows_count // 2 : rows_count])
        rows = jnp.concatenate([low, high])
        count = lax.axis_size("gy")
        if count & (count - 1):
            sums = lax.psum(packed[rows_count:], "gy")
        else:
            sums = sum_bits(packed[rows_count:], "gy", 1)
    tiles = 5 + turbine_rows // 8
    near, far = call(
        last_faces_kernel,
        [(tiles, lam.shape[2], height), (5, lam.shape[2], height)],
        lam,
        rows,
        sums,
        micros=0.1,
    )
    count = lax.axis_size("gx")
    got_near = lax.ppermute(near, "gx", [(i, i ^ 1) for i in range(count)])
    (far,) = call(last_far_kernel, [near.shape], far, near, got_near, micros=0.1)
    got_far = lax.ppermute(
        far, "gx", [(i, (i + 1 if i % 2 else i - 1) % count) for i in range(count)]
    )
    sums = far[5:] + got_far[5:]
    if count & (count - 1):
        sums = 0.25 * lax.psum(sums, "gx")
    else:
        sums = sum_bits(sums, "gx", 4)
    return rows, got_near, got_far, sums.reshape(turbine_rows, height)


def shards(fwd_pops, fwd_scale, seed_adjoint, turbine_map, thrust):
    steps, _, width, span, height = fwd_pops.shape
    assert steps == 3 and span == 8
    turbines = thrust.shape[0]
    turbine_rows = -(-turbines // 8) * 8
    sublanes = -(-(width + 4) // 8) * 8
    whole = (19, width, span, height)
    static = (thrust, turbine_map, fwd_scale, fwd_pops)
    row_count = (HALO + FIELDS) * width
    fields, rows = call(
        lambda *refs: pack_kernel(steps - 1, *refs),
        [(FIELDS, width, span, height), (2, row_count, height)],
        *static,
        seed_adjoint,
        smem_first=True,
        micros=0.3,
    )
    if lax.axis_size("gy") == 2:
        rows = lax.ppermute(rows, "gy", ring("gy", 1))
    else:
        rows = jnp.stack(swap_rows(rows[0], rows[1]))
    coefs = call(
        coef_kernel,
        [(COEFS, width, span, height)] * steps,
        *static,
        smem_first=True,
        micros=1.5,
    )
    face = (FACE_TILES + -(-2 * (CORNER + FIELDS) // 8), span, height)
    low, high = call(faces_kernel, [face, face], seed_adjoint, fields, rows, micros=0.3)
    above = lax.ppermute(low, "gx", ring("gx", -1))
    below = lax.ppermute(high, "gx", ring("gx", 1))
    lam, packed = call(
        pair_kernel,
        [whole, (10 * width + turbine_rows, height)],
        thrust,
        seed_adjoint,
        rows,
        above,
        below,
        coefs[2],
        coefs[1],
        fields,
        scratch=[
            (2, len(PACK_LIST[0]), sublanes, height),
            (2, FIELDS, sublanes, height),
            whole,
            (2, 5, span, height),
            (2, 5, sublanes, height),
        ],
        smem_first=True,
        micros=1.5,
    )
    rows, near, far, sums = last_exchange(lam, packed, turbine_rows, True)
    (lam,) = call(last_kernel, [whole], lam, rows, near, far, coefs[0], micros=0.5)
    thrust_grad = jnp.sum(sums, axis=1)[:turbines]
    return (lam, thrust_grad)


def solution(mesh):
    placed = (
        P(None, None, "gx", "gy", None),
        P(None, "gx", "gy", None),
        P(None, "gx", "gy", None),
        P("gx", "gy", None),
        P(),
    )
    return jax.shard_map(
        shards,
        mesh=mesh,
        in_specs=placed,
        out_specs=(P(None, "gx", "gy", None), P()),
        check_vma=False,
    )
```

```python
import jax
import jax.numpy as jnp
from jax import lax
from jax.experimental import pallas as pl
from jax.experimental.pallas import tpu as pltpu
from jax.sharding import PartitionSpec as P

VELOCITIES = (
    (0, 0, 0),
    (1, 0, 0),
    (-1, 0, 0),
    (0, 1, 0),
    (0, -1, 0),
    (0, 0, 1),
    (0, 0, -1),
    (1, 1, 0),
    (-1, -1, 0),
    (1, -1, 0),
    (-1, 1, 0),
    (1, 0, 1),
    (-1, 0, -1),
    (1, 0, -1),
    (-1, 0, 1),
    (0, 1, 1),
    (0, -1, -1),
    (0, 1, -1),
    (0, -1, 1),
)
OPPOSITE = (0, 2, 1, 4, 3, 6, 5, 8, 7, 10, 9, 12, 11, 14, 13, 16, 15, 18, 17)
WEIGHTS = tuple([1.0 / 3.0] + [1.0 / 18.0] * 6 + [1.0 / 36.0] * 12)
MEAN_FLOW = 0.1
TAU_BASE = 0.51
SMAG_COEF = 18.0 * 1.4142135623730951 * 0.17 * 0.17
QUAD_FLOOR = 0.0001

X_UP = (1, 7, 9, 11, 13)
X_DOWN = (2, 8, 10, 12, 14)
Y_UP = (3, 7, 10, 15, 17)
Y_DOWN = (4, 8, 9, 16, 18)

KEEP, MASS, FLUX, UX, UY, UZ, Q1 = 19, 20, 21, 22, 23, 24, 25
RATE, BULK, PX, PY, PZ, DRAG, DRAG_U, GAIN = 34, 35, 36, 37, 38, 39, 40, 41
COEFS = 42

FIELDS = 21

VMEM = pltpu.VMEM


def halo_list(axis, sign):
    near = [
        (1, m) for m in range(19) if VELOCITIES[m][axis] * sign >= 0 or VELOCITIES[m][2] != 0
    ]
    return near + [(2, m) for m in range(19) if VELOCITIES[m][axis] * sign == 1]


SIGNS = (1, -1)
ROW_LIST = [halo_list(1, sign) for sign in SIGNS]
INNER_LIST = [[(0, m) for m in range(19) if VELOCITIES[m][1] * sign == -1] for sign in SIGNS]
PACK_LIST = [ROW_LIST[side] + INNER_LIST[side] for side in range(2)]
HALO = len(ROW_LIST[0])
CORNER = 6 + FIELDS
FACE_TILES = 10 + -(-2 * CORNER // 8)


def base_values():
    values = []
    for member in range(19):
        along = float(VELOCITIES[member][0])
        values.append(
            WEIGHTS[member]
            * (
                1.0
                + 3.0 * MEAN_FLOW * along
                + 4.5 * MEAN_FLOW * MEAN_FLOW * along * along
                - 1.5 * MEAN_FLOW * MEAN_FLOW
            )
        )
    return values


def plane_coefs(pops, thrust_cell):
    rho = pops[0]
    for member in range(1, 19):
        rho = rho + pops[member]
    inv_rho = 1.0 / rho
    vel = []
    for axis_id in range(3):
        moment = None
        for member in range(19):
            component = VELOCITIES[member][axis_id]
            if component == 1:
                moment = pops[member] if moment is None else moment + pops[member]
            elif component == -1:
                moment = moment - pops[member]
        vel.append(moment * inv_rho)
    ux, uy, uz = vel
    speed_sq = ux * ux + uy * uy + uz * uz
    rest = 1.0 - 1.5 * speed_sq
    part = []
    for member in range(19):
        if member == 0:
            part.append(pops[0] - (WEIGHTS[0] * rho) * rest)
            continue
        proj = None
        for axis_id in range(3):
            component = VELOCITIES[member][axis_id]
            if component == 1:
                proj = vel[axis_id] if proj is None else proj + vel[axis_id]
            elif component == -1:
                proj = -vel[axis_id] if proj is None else proj - vel[axis_id]
        part.append(pops[member] - (WEIGHTS[member] * rho) * (rest + 3.0 * proj + 4.5 * proj * proj))

    def pair(member):
        return part[member] + part[member + 1]

    in_xy, in_xz, in_yz = pair(7) + pair(9), pair(11) + pair(13), pair(15) + pair(17)
    pxx, pyy, pzz = pair(1) + in_xy + in_xz, pair(3) + in_xy + in_yz, pair(5) + in_xz + in_yz
    pxy, pxz, pyz = pair(7) - pair(9), pair(11) - pair(13), pair(15) - pair(17)
    square = (
        pxx * pxx + pyy * pyy + pzz * pzz + 2.0 * (pxy * pxy + pxz * pxz + pyz * pyz) + QUAD_FLOOR
    )
    size = jnp.sqrt(square)
    root = jnp.sqrt(TAU_BASE * TAU_BASE + SMAG_COEF * size * inv_rho)
    omega = 1.0 / (0.5 * (TAU_BASE + root))
    pux = pxx * ux + pxy * uy + pxz * uz
    puy = pxy * ux + pyy * uy + pyz * uz
    puz = pxz * ux + pyz * uy + pzz * uz
    flux = omega * (3.0 / 36.0)
    drag = (3.0 / 36.0) * thrust_cell * jnp.abs(ux) * inv_rho
    result = list(part)
    result.append(1.0 - omega)
    result.append((omega * (1.0 / 36.0)) * (1.0 + 1.5 * speed_sq))
    result.append(flux)
    result.extend(vel)
    result.extend((pxx, pyy, pzz))
    result.extend((pxx + pyy + 2.0 * pxy, pxx + pyy - 2.0 * pxy))
    result.extend((pxx + pzz + 2.0 * pxz, pxx + pzz - 2.0 * pxz))
    result.extend((pyy + pzz + 2.0 * pyz, pyy + pzz - 2.0 * pyz))
    result.append((0.25 * SMAG_COEF) * omega * omega * inv_rho / (root * size))
    result.append(
        (pux * ux + puy * uy + puz * uz) - (pxx + pyy + pzz) * (1.0 / 3.0) - square * inv_rho
    )
    result.extend((-2.0 * pux, -2.0 * puy, -2.0 * puz))
    result.append(drag)
    result.append(drag * ux)
    result.append((-1.5 / 36.0) * ux * jnp.abs(ux))
    return result


def plus(*values):
    kept = [value for value in values if value is not None]
    return sum(kept[1:], kept[0]) if kept else None


def minus(left, right):
    if right is None:
        return left
    return -right if left is None else left - right


def times(left, right):
    return None if left is None or right is None else left * right


def plane_adjoint(mu, coef, wanted=range(19)):
    total, diff = {}, {}
    for member in range(1, 19, 2):
        total[member] = plus(mu[member], mu[member + 1])
        diff[member] = minus(mu[member], mu[member + 1])
    two_x, two_y, two_z = times(total[1], 2.0), times(total[3], 2.0), times(total[5], 2.0)
    in_xy, in_xz = plus(total[7], total[9]), plus(total[11], total[13])
    in_yz = plus(total[15], total[17])
    mxx, myy, mzz = plus(two_x, in_xy, in_xz), plus(two_y, in_xy, in_yz), plus(two_z, in_xz, in_yz)
    mxy, mxz = minus(total[7], total[9]), minus(total[11], total[13])
    myz = minus(total[15], total[17])
    m0 = plus(times(mu[0], 12.0), plus(two_x, two_y, two_z), plus(in_xy, in_xz, in_yz))
    mx = plus(times(diff[1], 2.0), plus(diff[7], diff[9]), plus(diff[11], diff[13]))
    my = plus(times(diff[3], 2.0), minus(diff[7], diff[9]), plus(diff[15], diff[17]))
    mz = plus(times(diff[5], 2.0), minus(diff[11], diff[13]), minus(diff[15], diff[17]))
    ux, uy, uz = coef(UX), coef(UY), coef(UZ)
    vx = plus(times(mxx, ux), times(mxy, uy), times(mxz, uz))
    vy = plus(times(mxy, ux), times(myy, uy), times(myz, uz))
    vz = plus(times(mxz, ux), times(myz, uy), times(mzz, uz))
    along = [mu[member] * coef(member) for member in range(19) if mu[member] is not None]
    while len(along) > 1:
        along = [
            along[k] + along[k + 1] if k + 1 < len(along) else along[k]
            for k in range(0, len(along), 2)
        ]
    gamma = along[0] * coef(RATE)
    flux = coef(FLUX)
    alpha = (
        coef(MASS) * m0
        - 1.5 * flux * (vx * ux + vy * uy + vz * uz)
        + gamma * coef(BULK)
        + mx * coef(DRAG_U)
    )
    beta_x = flux * (plus(mx, 3.0 * vx) - ux * m0) + gamma * coef(PX) - mx * coef(DRAG)
    beta_y = flux * (plus(my, 3.0 * vy) - uy * m0) + gamma * coef(PY)
    beta_z = flux * (plus(mz, 3.0 * vz) - uz * m0) + gamma * coef(PZ)
    keep = coef(KEEP)
    odd = {
        1: beta_x,
        3: beta_y,
        5: beta_z,
        7: beta_x + beta_y,
        9: beta_x - beta_y,
        11: beta_x + beta_z,
        13: beta_x - beta_z,
        15: beta_y + beta_z,
        17: beta_y - beta_z,
    }
    result = {}
    for member in wanted:
        if member == 0:
            result[0] = plus(times(mu[0], keep), alpha)
            continue
        forward = member - 1 + member % 2
        even = alpha + gamma * coef(Q1 + forward // 2)
        rest = even + odd[forward] if member == forward else even - odd[forward]
        result[member] = plus(times(mu[member], keep), rest)
    return result, mx


def turbine_cells(ids, thrust_ref):
    ratio = jnp.zeros(ids.shape, jnp.float32)
    for turbine in range(thrust_ref.shape[0]):
        ratio = jnp.where(ids == jnp.asarray(turbine, ids.dtype), thrust_ref[turbine], ratio)
    return jnp.where(ids >= 0, local_thrust(ratio), 0.0)


def local_thrust(values):
    return 4.0 * values / jnp.square(1.0 + jnp.sqrt(1.0 - values))


def decode(scale_ref, pops_ref, instant, plane):
    base = base_values()
    scale = scale_ref[instant, plane]
    return [
        base[member] * (1.0 + scale * pops_ref[instant, member, plane].astype(jnp.float32))
        for member in range(19)
    ]


def coef_kernel(thrust_ref, map_ref, scale_ref, pops_ref, _, *out_refs):
    for plane in range(pops_ref.shape[2]):
        thrust_cell = turbine_cells(map_ref[plane], thrust_ref)
        for instant, out_ref in enumerate(out_refs):
            pops = decode(scale_ref, pops_ref, instant, plane)
            for index, value in enumerate(plane_coefs(pops, thrust_cell)):
                out_ref[index, plane] = value


def edge_coef_kernel(thrust_ref, fields_ref, out_ref):
    for index, plane in enumerate((0, fields_ref.shape[1] - 1)):
        pops = [fields_ref[member, plane] for member in range(19)]
        coefs = plane_coefs(pops, turbine_cells(fields_ref[19, plane], thrust_ref))
        for coef, value in enumerate(coefs):
            out_ref[coef, index] = value


def by_parity(even):
    odd = lax.rem(lax.axis_index("gx"), 2) == 1
    pl.when(jnp.logical_not(odd))(lambda: even(True))
    pl.when(odd)(lambda: even(False))


def hand_out(low, high, near_ref, far_ref):
    def write(even):
        for source, out_ref in ((low, far_ref), (high, near_ref)) if even else ((low, near_ref), (high, far_ref)):
            for index in range(out_ref.shape[0]):
                out_ref[index] = source(index)

    by_parity(write)


def take_in(near_ref, far_ref, above_ref, below_ref):
    def write(even):
        for source, out_ref in ((near_ref, above_ref if even else below_ref), (far_ref, below_ref if even else above_ref)):
            for index in range(out_ref.shape[0]):
                out_ref[index] = source[index]

    by_parity(write)


def start_kernel(out_ref):
    out_ref[...] = jnp.zeros(out_ref.shape, jnp.float32)


def pack_kernel(_, map_ref, scale_ref, pops_ref, lam_ref, fields_ref, rows_ref, near_ref, far_ref):
    width, span = lam_ref.shape[1], lam_ref.shape[2]
    for side in range(2):
        for index, (far, member) in enumerate(ROW_LIST[side]):
            row = far - 1 if side == 0 else span - far
            rows_ref[side, index * width : (index + 1) * width, :] = lam_ref[member, :, row, :]
    last = pops_ref.shape[0] - 1
    for plane in range(width):
        for index, value in enumerate(decode(scale_ref, pops_ref, last, plane)):
            fields_ref[index, plane] = value
        fields_ref[19, plane] = map_ref[plane].astype(jnp.float32)
        pops = decode(scale_ref, pops_ref, 0, plane)
        rho, momentum = pops[0], None
        for member in range(1, 19):
            rho = rho + pops[member]
        for member in X_UP:
            pair = pops[member] - pops[member + 1]
            momentum = pair if momentum is None else momentum + pair
        ux = momentum / rho
        fields_ref[20, plane] = (-1.5 / 36.0) * ux * jnp.abs(ux)
    for side in range(2):
        row = 0 if side == 0 else span - 1
        for field in range(FIELDS):
            start = (HALO + field) * width
            rows_ref[side, start : start + width, :] = fields_ref[field, :, row, :]
    hand_out(
        lambda field: fields_ref[field, 0],
        lambda field: fields_ref[field, width - 1],
        near_ref,
        far_ref,
    )


def span_shift(value, move, row):
    span = value.shape[0]
    place = lax.broadcasted_iota(jnp.int32, value.shape, 0)
    if move == 1:
        return jnp.where(place == span - 1, row, pltpu.roll(value, span - 1, 0))
    return jnp.where(place == 0, row, pltpu.roll(value, 1, 0))


def roll_z(value, move, edges, walls=None):
    height = value.shape[1]
    if move == 0:
        return value
    shift, edge = (height - 1, edges[1]) if move == 1 else (1, edges[0])
    return jnp.where(edge, 0.0 if walls is None else walls, pltpu.roll(value, shift, 1))


def wall_masks(shape):
    lane = lax.broadcasted_iota(jnp.int32, shape, 1)
    return lane == 0, lane == shape[1] - 1


def gather_mu(source, row_of, plane, edges):
    mu = []
    for member in range(19):
        move_x, move_y, move_z = VELOCITIES[member]
        value = source(plane + move_x, member)
        if value is not None and move_y != 0:
            side = 0 if move_y == 1 else 1
            value = span_shift(value, move_y, row_of(side, plane + move_x, member))
        if move_z != 0:
            walls = source(plane, OPPOSITE[member])
            if value is None:
                value = jnp.where(edges[1 if move_z == 1 else 0], walls, 0.0)
            else:
                value = roll_z(value, move_z, edges, walls)
        mu.append(value)
    return mu


def own_lam(lam_ref):
    def source(plane, member):
        return lam_ref[member, plane] if 0 <= plane < lam_ref.shape[1] else None

    return source


def got_row(rows_ref, width):
    def row_of(side, plane, member):
        place = ROW_LIST[side].index((1, member)) * width + plane
        return rows_ref[side, place : place + 1, :]

    return row_of


def corner_row(face_ref, side, index):
    slot = side * CORNER + index
    return face_ref[10 + slot // 8, slot % 8 : slot % 8 + 1, :]


def faces_kernel(thrust_ref, lam_ref, rows_ref, coef_ref, near_ref, far_ref, field_ref, part_ref, pack_ref, low_ref, high_ref):
    width, span = lam_ref.shape[1], lam_ref.shape[2]
    edges = wall_masks(lam_ref.shape[2:])
    source, row_of = own_lam(lam_ref), got_row(rows_ref, width)
    pack_ref[...] = jnp.zeros(pack_ref.shape, jnp.float32)
    field_ref[...] = jnp.zeros(field_ref.shape, jnp.float32)
    for side in range(2):
        for index, (far, member) in enumerate(PACK_LIST[side]):
            if far > 0:
                rows = rows_ref[side, index * width : (index + 1) * width, :]
            else:
                rows = lam_ref[member, :, span - 1 if side == 0 else 0, :]
            pack_ref[side, index, 2 : width + 2, :] = rows
        for field in range(FIELDS):
            start = (HALO + field) * width
            field_ref[side, field, 2 : width + 2, :] = rows_ref[side, start : start + width, :]
    place = lax.broadcasted_iota(jnp.int32, pack_ref.shape[2:], 0)
    inside = jnp.logical_and(place >= 2, place < width + 2)
    pack_edges = wall_masks(pack_ref.shape[2:])
    for side, (sign, wanted) in enumerate(((1, Y_UP), (-1, Y_DOWN))):
        mu = []
        for member in range(19):
            move_x, move_y, move_z = VELOCITIES[member]
            value = pack_ref[side, PACK_LIST[side].index((1 + sign * move_y, member))]
            if move_x != 0:
                value = pltpu.roll(value, (-move_x) % value.shape[0], 0)
            if move_z != 0:
                walls = pack_ref[side, PACK_LIST[side].index((1, OPPOSITE[member]))]
                value = roll_z(value, move_z, pack_edges, walls)
            mu.append(value)
        pops = [field_ref[side, member] for member in range(19)]
        coefs = plane_coefs(pops, turbine_cells(field_ref[side, 19], thrust_ref))
        lam, _ = plane_adjoint(mu, lambda index: coefs[index], wanted)
        for index, member in enumerate(wanted):
            part_ref[side, index] = jnp.where(inside, lam[member], 0.0)
    for out_ref, plane, members in ((low_ref, 0, X_UP), (high_ref, width - 1, X_DOWN)):
        lam, _ = plane_adjoint(
            gather_mu(source, row_of, plane, edges),
            lambda index: coef_ref[index, min(plane, 1)],
            members,
        )
        for index, member in enumerate(members):
            value, move_y = lam_ref[member, plane], VELOCITIES[member][1]
            if move_y != 0:
                value = span_shift(value, move_y, row_of(0 if move_y == 1 else 1, plane, member))
            out_ref[index] = value
            out_ref[5 + index] = lam[member]
        for side, (sign, wanted) in enumerate(((1, Y_UP), (-1, Y_DOWN))):
            sources = [
                pack_ref.at[side, PACK_LIST[side].index((1 + sign * VELOCITIES[member][1], member))]
                for member in members
            ]
            corner = VELOCITIES.index((VELOCITIES[members[0]][0], sign, 0))
            sources.append(part_ref.at[side, wanted.index(corner)])
            sources += [field_ref.at[side, field] for field in range(FIELDS)]
            for index, ref in enumerate(sources):
                slot = side * CORNER + index
                out_ref[10 + slot // 8, slot % 8 : slot % 8 + 1, :] = ref[plane + 2 : plane + 3, :]
    hand_out(lambda index: low_ref[index], lambda index: high_ref[index], near_ref, far_ref)


def middle_kernel(thrust_ref, lam_ref, rows_ref, coef_ref, near_ref, far_ref, mid_ref, cell_ref, face_ref, ids_ref, gains_ref, above_ref, below_ref):
    width = lam_ref.shape[1]
    edges = wall_masks(lam_ref.shape[2:])
    source, row_of = own_lam(lam_ref), got_row(rows_ref, width)
    take_in(near_ref, far_ref, above_ref, below_ref)
    for side, fields_ref in enumerate((above_ref, below_ref)):
        ids_ref[side], gains_ref[side] = fields_ref[19], fields_ref[20]
    for plane in range(width):
        mu = gather_mu(source, row_of, plane, edges)
        lam, mx = plane_adjoint(mu, lambda index: coef_ref[index, plane])
        for member in range(19):
            mid_ref[member, plane] = lam[member]
        cell_ref[plane] = mx * coef_ref[GAIN, plane]
    for side, (fields_ref, plane, members, wanted) in enumerate(
        ((above_ref, width - 1, X_DOWN, X_UP), (below_ref, 0, X_UP, X_DOWN))
    ):
        mu = [None] * 19
        for member in members:
            value, (_, move_y, move_z) = lam_ref[member, plane], VELOCITIES[member]
            if move_y != 0:
                value = span_shift(value, move_y, row_of(0 if move_y == 1 else 1, plane, member))
            mu[member] = roll_z(value, move_z, edges)
        pops = [fields_ref[member] for member in range(19)]
        coefs = plane_coefs(pops, turbine_cells(fields_ref[19], thrust_ref))
        lam, _ = plane_adjoint(mu, lambda index: coefs[index], wanted)
        for index, member in enumerate(wanted):
            face_ref[side, index] = lam[member]


def pair_kernel(thrust_ref, lam_ref, rows_ref, near_ref, far_ref, late_ref, early_ref, fields_ref,
                part_mid_ref, part_cell_ref, part_face_ref, ids_ref, gains_ref, part_edge_ref, pack_ref,
                out_ref, next_ref, mid_ref, edge_ref, line_ref, above_ref, below_ref):
    width, span, height = lam_ref.shape[1:]
    take_in(near_ref, far_ref, above_ref, below_ref)
    edges = wall_masks((span, height))
    pack_shape = pack_ref.shape[2:]
    pack_edges = wall_masks(pack_shape)
    place = lax.broadcasted_iota(jnp.int32, pack_shape, 0)
    totals = [part_cell_ref[plane] for plane in range(width)]
    for face_ref, plane, members in ((above_ref, width - 1, X_UP), (below_ref, 0, X_DOWN)):
        mu = [None] * 19
        for index, member in enumerate(members):
            mu[member] = roll_z(face_ref[index], VELOCITIES[member][2], edges)
        lam, mx = plane_adjoint(mu, lambda index: late_ref[index, plane])
        for member in range(19):
            mid_ref[member, 0 if plane == 0 else 1] = part_mid_ref[member, plane] + lam[member]
        totals[plane] = totals[plane] + mx * late_ref[GAIN, plane]

    def beyond(below, above, rest):
        return jnp.where(place == 1, below, jnp.where(place == width + 2, above, rest))

    halo_tiles = []
    for side, (sign, wanted) in enumerate(((1, Y_UP), (-1, Y_DOWN))):
        mu = [None] * 19
        for members, got_ref, got_place, own_place in (
            (X_UP, above_ref, width + 1, 1),
            (X_DOWN, below_ref, 2, width + 2),
        ):
            plane = 0 if own_place == 1 else width - 1
            for index, member in enumerate(members):
                far = 1 + sign * VELOCITIES[member][1]
                if far > 0:
                    start = ROW_LIST[side].index((far, member)) * width + plane
                    own = rows_ref[side, start : start + 1, :]
                else:
                    inner = span - 1 if side == 0 else 0
                    own = lam_ref[member, plane, inner : inner + 1, :]
                value = jnp.where(
                    place == got_place,
                    corner_row(got_ref, side, index),
                    jnp.where(place == own_place, own, 0.0),
                )
                mu[member] = roll_z(value, VELOCITIES[member][2], pack_edges)
        fields = [
            beyond(
                corner_row(below_ref, side, 6 + field),
                corner_row(above_ref, side, 6 + field),
                pack_ref[side, field],
            )
            for field in range(FIELDS)
        ]
        coefs = plane_coefs(fields[:19], turbine_cells(fields[19], thrust_ref))
        lam, _ = plane_adjoint(mu, lambda index: coefs[index], wanted)
        for index, member in enumerate(wanted):
            value = part_edge_ref[side, index] + lam[member]
            if VELOCITIES[member][0] == 1:
                value = value + jnp.where(place == width + 2, corner_row(above_ref, side, 5), 0.0)
            elif VELOCITIES[member][0] == -1:
                value = value + jnp.where(place == 1, corner_row(below_ref, side, 5), 0.0)
            edge_ref[side, index] = value
        halo_tiles.append((fields[20], fields[19]))

    def middle(plane, member):
        if plane >= width:
            index = X_UP.index(member)
            return above_ref[5 + index] + part_face_ref[0, index]
        if plane < 0:
            index = X_DOWN.index(member)
            return below_ref[5 + index] + part_face_ref[1, index]
        if plane in (0, width - 1):
            return mid_ref[member, 0 if plane == 0 else 1]
        return part_mid_ref[member, plane]

    def middle_row(side, plane, member):
        index = (Y_UP, Y_DOWN)[side].index(member)
        return edge_ref[side, index, plane + 2 : plane + 3, :]

    for plane in range(width):
        mu = gather_mu(middle, middle_row, plane, edges)
        lam, mx = plane_adjoint(mu, lambda index: early_ref[index, plane])
        for member in range(19):
            out_ref[member, plane] = lam[member]
        totals[plane] = totals[plane] + mx * early_ref[GAIN, plane]

    for side, (members, row) in enumerate(((Y_UP, 0), (Y_DOWN, span - 1))):
        for index, member in enumerate(members):
            start = (5 * side + index) * width
            next_ref[start : start + width, :] = out_ref[member, :, row, :]

    nothing = jnp.zeros((1, height), jnp.float32)
    up, down = [], []
    for plane in range(width):
        up.append(
            2.0 * out_ref[1, plane]
            + span_shift(out_ref[7, plane], 1, nothing)
            + span_shift(out_ref[9, plane], -1, nothing)
            + roll_z(out_ref[11, plane], 1, edges)
            + roll_z(out_ref[13, plane], -1, edges)
        )
        down.append(
            2.0 * out_ref[2, plane]
            + span_shift(out_ref[8, plane], -1, nothing)
            + span_shift(out_ref[10, plane], 1, nothing)
            + roll_z(out_ref[12, plane], -1, edges)
            + roll_z(out_ref[14, plane], 1, edges)
        )
    tiles = []
    for plane in range(-1, width + 1):
        value = None
        if plane + 1 < width:
            value = up[plane + 1]
        if plane >= 1:
            value = -down[plane - 1] if value is None else value - down[plane - 1]
        if plane < 0 or plane >= width:
            side = 1 if plane < 0 else 0
            tiles.append((gains_ref[side] * value, ids_ref[side]))
            continue
        value = value + jnp.where(edges[1], out_ref[12, plane] - out_ref[13, plane], 0.0)
        value = value + jnp.where(edges[0], out_ref[14, plane] - out_ref[11, plane], 0.0)
        tiles.append((totals[plane] + fields_ref[20, plane] * value, fields_ref[19, plane]))
    line_ref[...] = jnp.zeros(line_ref.shape, jnp.float32)
    for side, (upward, downward, row) in enumerate(((9, 8, span - 1), (7, 10, 0))):
        line_ref[side, 0, 1 : width + 1, :] = out_ref[upward, :, row, :]
        line_ref[side, 1, 3 : width + 3, :] = out_ref[downward, :, row, :]
        gain, ids = halo_tiles[side]
        tiles.append(((line_ref[side, 0] - line_ref[side, 1]) * gain, ids))
    start = 10 * width
    next_ref[start:, :] = jnp.zeros((next_ref.shape[0] - start, height), jnp.float32)
    for turbine in range(thrust_ref.shape[0]):
        row = None
        for value, ids in tiles:
            kept = jnp.sum(jnp.where(ids == float(turbine), value, 0.0), axis=0, keepdims=True)
            row = kept if row is None else row + kept
        next_ref[start + turbine : start + turbine + 1, :] = row


def last_faces_kernel(lam_ref, rows_ref, sums_ref, near_ref, far_ref):
    width = lam_ref.shape[1]

    def row_of(side, plane, member):
        place = (5 * side + (Y_UP, Y_DOWN)[side].index(member)) * width + plane
        return rows_ref[place : place + 1, :]

    def moved(members, plane):
        def tile(index):
            member = members[index]
            value, move_y = lam_ref[member, plane], VELOCITIES[member][1]
            if move_y == 0:
                return value
            return span_shift(value, move_y, row_of(0 if move_y == 1 else 1, plane, member))

        return tile

    hand_out(moved(X_UP, 0), moved(X_DOWN, width - 1), near_ref.at[0:5], far_ref)
    for tile in range(near_ref.shape[0] - 5):
        near_ref[5 + tile] = sums_ref[8 * tile : 8 * tile + 8, :]


def last_kernel(lam_ref, rows_ref, near_ref, far_ref, coef_ref, out_ref):
    width, span, height = lam_ref.shape[1:]
    lane = lax.broadcasted_iota(jnp.int32, (span, height), 1)
    first, last = lane == 0, lane == height - 1
    odd = jnp.full((span, height), lax.rem(lax.axis_index("gx"), 2)) == 1

    def source(plane, member):
        if plane >= width:
            index = X_UP.index(member)
            return jnp.where(odd, far_ref[index], near_ref[index])
        if plane < 0:
            index = X_DOWN.index(member)
            return jnp.where(odd, near_ref[index], far_ref[index])
        value, move_y = lam_ref[member, plane], VELOCITIES[member][1]
        if move_y == 0:
            return value
        side = 0 if move_y == 1 else 1
        place = (5 * side + (Y_UP, Y_DOWN)[side].index(member)) * width + plane
        return span_shift(value, move_y, rows_ref[place : place + 1, :])

    for plane in range(width):
        mu = []
        for member in range(19):
            move_x, _, move_z = VELOCITIES[member]
            value = source(plane + move_x, member)
            if move_z == 1:
                value = jnp.where(
                    last, lam_ref[OPPOSITE[member], plane], pltpu.roll(value, height - 1, 1)
                )
            elif move_z == -1:
                value = jnp.where(first, lam_ref[OPPOSITE[member], plane], pltpu.roll(value, 1, 1))
            mu.append(value)
        lam, _ = plane_adjoint(mu, lambda index: coef_ref[index, plane])
        for member in range(19):
            out_ref[member, plane] = lam[member]


def call(kernel, outs, *args, scratch=(), smem_first=False, micros=1):
    specs = [pl.BlockSpec(memory_space=VMEM)] * len(args)
    if smem_first:
        specs[0] = pl.BlockSpec(memory_space=pltpu.SMEM)
    return pl.pallas_call(
        kernel,
        out_shape=tuple(jax.ShapeDtypeStruct(shape, jnp.float32) for shape in outs),
        in_specs=specs,
        out_specs=tuple(pl.BlockSpec(memory_space=VMEM) for _ in outs),
        scratch_shapes=[pltpu.VMEM(shape, jnp.float32) for shape in scratch],
        cost_estimate=pl.CostEstimate(
            flops=int(1e6 * micros), bytes_accessed=int(2e6 * micros), transcendentals=0
        ),
        compiler_params=pltpu.CompilerParams(vmem_limit_bytes=32 * 1024 * 1024),
    )(*args)


def ring(axis, step):
    count = lax.axis_size(axis)
    return [(i, (i + step) % count) for i in range(count)]


def swap_rows(low, high):
    return lax.ppermute(low, "gy", ring("gy", -1)), lax.ppermute(high, "gy", ring("gy", 1))


def swap_planes(near, far):
    count = lax.axis_size("gx")
    assert count % 2 == 0
    got_near = lax.ppermute(near, "gx", [(i, i ^ 1) for i in range(count)])
    got_far = lax.ppermute(
        far, "gx", [(i, (i + 1 if i % 2 else i - 1) % count) for i in range(count)]
    )
    return got_near, got_far


def flips(value, axis, flip_list):
    count = lax.axis_size(axis)
    parts = [lax.ppermute(value, axis, [(i, i ^ flip) for i in range(count)]) for flip in flip_list]
    return sum(parts, value)


def sum_bits(value, axis, start):
    count = lax.axis_size(axis)
    while start < count:
        stop = min(4 * start, count)
        value = flips(value, axis, range(start, stop, start))
        start = stop
    return value


def last_exchange(lam, packed, turbine_rows):
    width, height = lam.shape[1], lam.shape[3]
    rows_count = 10 * width
    if lax.axis_size("gy") == 2:
        got = lax.ppermute(packed, "gy", ring("gy", 1))
        rows, sums = got, packed[rows_count:] + got[rows_count:]
    else:
        low, high = swap_rows(packed[: rows_count // 2], packed[rows_count // 2 : rows_count])
        rows = jnp.concatenate([low, high])
        count = lax.axis_size("gy")
        if count & (count - 1):
            sums = lax.psum(packed[rows_count:], "gy")
        else:
            sums = sum_bits(packed[rows_count:], "gy", 1)
    tiles = 5 + turbine_rows // 8
    near, far = call(
        last_faces_kernel,
        [(tiles, lam.shape[2], height), (5, lam.shape[2], height)],
        lam,
        rows,
        sums,
        micros=0.1,
    )
    got_near, got_far = swap_planes(near, far)
    count = lax.axis_size("gx")
    if count & (count - 1):
        sums = lax.psum(sums, "gx")
    else:
        sums = near[5:] + got_near[5:]
        if count > 2:
            sums = sum_bits(flips(sums, "gx", [2]), "gx", 4)
    return rows, got_near, got_far, sums.reshape(turbine_rows, height)


def shards(fwd_pops, fwd_scale, seed_adjoint, turbine_map, thrust):
    steps, _, width, span, height = fwd_pops.shape
    assert steps == 3 and span == 8
    turbines = thrust.shape[0]
    turbine_rows = -(-turbines // 8) * 8
    sublanes = -(-(width + 4) // 8) * 8
    whole = (19, width, span, height)
    static = (thrust, turbine_map, fwd_scale, fwd_pops)
    (begun,) = call(start_kernel, [(8, height)], micros=400)
    fields, rows, near_fields, far_fields = call(
        pack_kernel,
        [
            (FIELDS, width, span, height),
            (2, (HALO + FIELDS) * width, height),
            (FIELDS, span, height),
            (FIELDS, span, height),
        ],
        begun,
        *static[1:],
        seed_adjoint,
        micros=0.6,
    )
    if lax.axis_size("gy") == 2:
        rows = lax.ppermute(rows, "gy", ring("gy", 1))
    else:
        rows = jnp.stack(swap_rows(rows[0], rows[1]))
    near_fields, far_fields = swap_planes(near_fields, far_fields)
    (edge_coefs,) = call(
        edge_coef_kernel, [(COEFS, 2, span, height)], thrust, fields, smem_first=True, micros=0.3
    )
    face, edge = (FACE_TILES, span, height), (2, 5, sublanes, height)
    near, far, pack, part_edge = call(
        faces_kernel,
        [face, face, (2, FIELDS, sublanes, height), edge],
        thrust,
        seed_adjoint,
        rows,
        edge_coefs,
        scratch=[(2, len(PACK_LIST[0]), sublanes, height), face, face],
        smem_first=True,
        micros=0.6,
    )
    near, far = swap_planes(near, far)
    coefs = call(
        coef_kernel,
        [(COEFS, width, span, height)] * steps,
        *static,
        rows,
        smem_first=True,
        micros=1.5,
    )
    halo = (FIELDS, span, height)
    parts = call(
        middle_kernel,
        [whole, (width, span, height), (2, 5, span, height), (2, span, height), (2, span, height)],
        thrust,
        seed_adjoint,
        rows,
        coefs[2],
        near_fields,
        far_fields,
        scratch=[halo, halo],
        smem_first=True,
        micros=0.6,
    )
    lam, packed = call(
        pair_kernel,
        [whole, (10 * width + turbine_rows, height)],
        thrust,
        seed_adjoint,
        rows,
        near,
        far,
        coefs[2],
        coefs[1],
        fields,
        *parts,
        part_edge,
        pack,
        scratch=[(19, 2, span, height), edge, (2, 2, sublanes, height), face, face],
        smem_first=True,
        micros=0.8,
    )
    rows, near, far, sums = last_exchange(lam, packed, turbine_rows)
    (lam,) = call(last_kernel, [whole], lam, rows, near, far, coefs[0], micros=0.5)
    _, slope = jax.vjp(local_thrust, thrust)
    thrust_grad = slope(jnp.sum(sums[:turbines], axis=1))[0]
    return (lam, thrust_grad)


def solution(mesh):
    placed = (
        P(None, None, "gx", "gy", None),
        P(None, "gx", "gy", None),
        P(None, "gx", "gy", None),
        P("gx", "gy", None),
        P(),
    )
    return jax.shard_map(
        shards,
        mesh=mesh,
        in_specs=placed,
        out_specs=(P(None, "gx", "gy", None), P()),
        check_vma=False,
    )
```

```python
import jax
import jax.numpy as jnp
from jax import lax
from jax.experimental import pallas as pl
from jax.experimental.pallas import tpu as pltpu
from jax.sharding import PartitionSpec as P

VELOCITIES = (
    (0, 0, 0),
    (1, 0, 0),
    (-1, 0, 0),
    (0, 1, 0),
    (0, -1, 0),
    (0, 0, 1),
    (0, 0, -1),
    (1, 1, 0),
    (-1, -1, 0),
    (1, -1, 0),
    (-1, 1, 0),
    (1, 0, 1),
    (-1, 0, -1),
    (1, 0, -1),
    (-1, 0, 1),
    (0, 1, 1),
    (0, -1, -1),
    (0, 1, -1),
    (0, -1, 1),
)
OPPOSITE = (0, 2, 1, 4, 3, 6, 5, 8, 7, 10, 9, 12, 11, 14, 13, 16, 15, 18, 17)
WEIGHTS = tuple([1.0 / 3.0] + [1.0 / 18.0] * 6 + [1.0 / 36.0] * 12)
MEAN_FLOW = 0.1
TAU_BASE = 0.51
SMAG_COEF = 18.0 * 1.4142135623730951 * 0.17 * 0.17
QUAD_FLOOR = 0.0001

X_UP = (1, 7, 9, 11, 13)
X_DOWN = (2, 8, 10, 12, 14)
Y_UP = (3, 7, 10, 15, 17)
Y_DOWN = (4, 8, 9, 16, 18)

KEEP, MASS, FLUX, UX, UY, UZ, Q1 = 19, 20, 21, 22, 23, 24, 25
RATE, BULK, PX, PY, PZ, DRAG, DRAG_U, GAIN = 34, 35, 36, 37, 38, 39, 40, 41
COEFS = 42

FIELDS = 21

VMEM = pltpu.VMEM


def halo_list(axis, sign):
    near = [
        (1, m) for m in range(19) if VELOCITIES[m][axis] * sign >= 0 or VELOCITIES[m][2] != 0
    ]
    return near + [(2, m) for m in range(19) if VELOCITIES[m][axis] * sign == 1]


SIGNS = (1, -1)
ROW_LIST = [halo_list(1, sign) for sign in SIGNS]
INNER_LIST = [[(0, m) for m in range(19) if VELOCITIES[m][1] * sign == -1] for sign in SIGNS]
PACK_LIST = [ROW_LIST[side] + INNER_LIST[side] for side in range(2)]
HALO = len(ROW_LIST[0])
CORNER = 6 + FIELDS
FACE_TILES = 10 + -(-2 * CORNER // 8)


def base_values():
    values = []
    for member in range(19):
        along = float(VELOCITIES[member][0])
        values.append(
            WEIGHTS[member]
            * (
                1.0
                + 3.0 * MEAN_FLOW * along
                + 4.5 * MEAN_FLOW * MEAN_FLOW * along * along
                - 1.5 * MEAN_FLOW * MEAN_FLOW
            )
        )
    return values


def plane_coefs(pops, thrust_cell):
    rho = pops[0]
    for member in range(1, 19):
        rho = rho + pops[member]
    inv_rho = 1.0 / rho
    vel = []
    for axis_id in range(3):
        moment = None
        for member in range(19):
            component = VELOCITIES[member][axis_id]
            if component == 1:
                moment = pops[member] if moment is None else moment + pops[member]
            elif component == -1:
                moment = moment - pops[member]
        vel.append(moment * inv_rho)
    ux, uy, uz = vel
    speed_sq = ux * ux + uy * uy + uz * uz
    rest = 1.0 - 1.5 * speed_sq
    part = []
    for member in range(19):
        if member == 0:
            part.append(pops[0] - (WEIGHTS[0] * rho) * rest)
            continue
        proj = None
        for axis_id in range(3):
            component = VELOCITIES[member][axis_id]
            if component == 1:
                proj = vel[axis_id] if proj is None else proj + vel[axis_id]
            elif component == -1:
                proj = -vel[axis_id] if proj is None else proj - vel[axis_id]
        part.append(pops[member] - (WEIGHTS[member] * rho) * (rest + 3.0 * proj + 4.5 * proj * proj))

    def pair(member):
        return part[member] + part[member + 1]

    in_xy, in_xz, in_yz = pair(7) + pair(9), pair(11) + pair(13), pair(15) + pair(17)
    pxx, pyy, pzz = pair(1) + in_xy + in_xz, pair(3) + in_xy + in_yz, pair(5) + in_xz + in_yz
    pxy, pxz, pyz = pair(7) - pair(9), pair(11) - pair(13), pair(15) - pair(17)
    square = (
        pxx * pxx + pyy * pyy + pzz * pzz + 2.0 * (pxy * pxy + pxz * pxz + pyz * pyz) + QUAD_FLOOR
    )
    size = jnp.sqrt(square)
    root = jnp.sqrt(TAU_BASE * TAU_BASE + SMAG_COEF * size * inv_rho)
    omega = 1.0 / (0.5 * (TAU_BASE + root))
    pux = pxx * ux + pxy * uy + pxz * uz
    puy = pxy * ux + pyy * uy + pyz * uz
    puz = pxz * ux + pyz * uy + pzz * uz
    flux = omega * (3.0 / 36.0)
    drag = (3.0 / 36.0) * thrust_cell * jnp.abs(ux) * inv_rho
    result = list(part)
    result.append(1.0 - omega)
    result.append((omega * (1.0 / 36.0)) * (1.0 + 1.5 * speed_sq))
    result.append(flux)
    result.extend(vel)
    result.extend((pxx, pyy, pzz))
    result.extend((pxx + pyy + 2.0 * pxy, pxx + pyy - 2.0 * pxy))
    result.extend((pxx + pzz + 2.0 * pxz, pxx + pzz - 2.0 * pxz))
    result.extend((pyy + pzz + 2.0 * pyz, pyy + pzz - 2.0 * pyz))
    result.append((0.25 * SMAG_COEF) * omega * omega * inv_rho / (root * size))
    result.append(
        (pux * ux + puy * uy + puz * uz) - (pxx + pyy + pzz) * (1.0 / 3.0) - square * inv_rho
    )
    result.extend((-2.0 * pux, -2.0 * puy, -2.0 * puz))
    result.append(drag)
    result.append(drag * ux)
    result.append((-1.5 / 36.0) * ux * jnp.abs(ux))
    return result


def plus(*values):
    kept = [value for value in values if value is not None]
    return sum(kept[1:], kept[0]) if kept else None


def minus(left, right):
    if right is None:
        return left
    return -right if left is None else left - right


def times(left, right):
    return None if left is None or right is None else left * right


def plane_adjoint(mu, coef, wanted=range(19)):
    total, diff = {}, {}
    for member in range(1, 19, 2):
        total[member] = plus(mu[member], mu[member + 1])
        diff[member] = minus(mu[member], mu[member + 1])
    two_x, two_y, two_z = times(total[1], 2.0), times(total[3], 2.0), times(total[5], 2.0)
    in_xy, in_xz = plus(total[7], total[9]), plus(total[11], total[13])
    in_yz = plus(total[15], total[17])
    mxx, myy, mzz = plus(two_x, in_xy, in_xz), plus(two_y, in_xy, in_yz), plus(two_z, in_xz, in_yz)
    mxy, mxz = minus(total[7], total[9]), minus(total[11], total[13])
    myz = minus(total[15], total[17])
    m0 = plus(times(mu[0], 12.0), plus(two_x, two_y, two_z), plus(in_xy, in_xz, in_yz))
    mx = plus(times(diff[1], 2.0), plus(diff[7], diff[9]), plus(diff[11], diff[13]))
    my = plus(times(diff[3], 2.0), minus(diff[7], diff[9]), plus(diff[15], diff[17]))
    mz = plus(times(diff[5], 2.0), minus(diff[11], diff[13]), minus(diff[15], diff[17]))
    ux, uy, uz = coef(UX), coef(UY), coef(UZ)
    vx = plus(times(mxx, ux), times(mxy, uy), times(mxz, uz))
    vy = plus(times(mxy, ux), times(myy, uy), times(myz, uz))
    vz = plus(times(mxz, ux), times(myz, uy), times(mzz, uz))
    along = [mu[member] * coef(member) for member in range(19) if mu[member] is not None]
    while len(along) > 1:
        along = [
            along[k] + along[k + 1] if k + 1 < len(along) else along[k]
            for k in range(0, len(along), 2)
        ]
    gamma = along[0] * coef(RATE)
    flux = coef(FLUX)
    alpha = (
        coef(MASS) * m0
        - 1.5 * flux * (vx * ux + vy * uy + vz * uz)
        + gamma * coef(BULK)
        + mx * coef(DRAG_U)
    )
    beta_x = flux * (plus(mx, 3.0 * vx) - ux * m0) + gamma * coef(PX) - mx * coef(DRAG)
    beta_y = flux * (plus(my, 3.0 * vy) - uy * m0) + gamma * coef(PY)
    beta_z = flux * (plus(mz, 3.0 * vz) - uz * m0) + gamma * coef(PZ)
    keep = coef(KEEP)
    odd = {
        1: beta_x,
        3: beta_y,
        5: beta_z,
        7: beta_x + beta_y,
        9: beta_x - beta_y,
        11: beta_x + beta_z,
        13: beta_x - beta_z,
        15: beta_y + beta_z,
        17: beta_y - beta_z,
    }
    result = {}
    for member in wanted:
        if member == 0:
            result[0] = plus(times(mu[0], keep), alpha)
            continue
        forward = member - 1 + member % 2
        even = alpha + gamma * coef(Q1 + forward // 2)
        rest = even + odd[forward] if member == forward else even - odd[forward]
        result[member] = plus(times(mu[member], keep), rest)
    return result, mx


def turbine_cells(ids, thrust_ref):
    ratio = jnp.zeros(ids.shape, jnp.float32)
    for turbine in range(thrust_ref.shape[0]):
        row = thrust_ref[turbine : turbine + 1, :]
        ratio = jnp.where(ids == jnp.asarray(turbine, ids.dtype), row, ratio)
    return jnp.where(ids >= 0, local_thrust(ratio), 0.0)


def local_thrust(values):
    return 4.0 * values / jnp.square(1.0 + jnp.sqrt(1.0 - values))


def decode(scale_ref, pops_ref, instant, plane):
    base = base_values()
    scale = scale_ref[instant, plane]
    return [
        base[member] * (1.0 + scale * pops_ref[instant, member, plane].astype(jnp.float32))
        for member in range(19)
    ]


def coef_kernel(thrust_ref, map_ref, scale_ref, pops_ref, near_ref, pass_ref, *out_refs):
    pass_ref[...] = near_ref[...]
    for plane in range(pops_ref.shape[2]):
        thrust_cell = turbine_cells(map_ref[plane], thrust_ref)
        for instant, out_ref in enumerate(out_refs):
            pops = decode(scale_ref, pops_ref, instant, plane)
            for index, value in enumerate(plane_coefs(pops, thrust_cell)):
                out_ref[index, plane] = value


def edge_coef_kernel(thrust_ref, fields_ref, near_ref, out_ref, pass_ref):
    for index, plane in enumerate((0, fields_ref.shape[1] - 1)):
        pops = [fields_ref[member, plane] for member in range(19)]
        coefs = plane_coefs(pops, turbine_cells(fields_ref[19, plane], thrust_ref))
        for coef, value in enumerate(coefs):
            out_ref[coef, index] = value
    pass_ref[...] = near_ref[...]


def by_parity(even):
    odd = lax.rem(lax.axis_index("gx"), 2) == 1
    pl.when(jnp.logical_not(odd))(lambda: even(True))
    pl.when(odd)(lambda: even(False))


def hand_out(low, high, near_ref, far_ref):
    def write(even):
        for source, out_ref in ((low, far_ref), (high, near_ref)) if even else ((low, near_ref), (high, far_ref)):
            for index in range(out_ref.shape[0]):
                out_ref[index] = source(index)

    by_parity(write)


def take_in(near_ref, far_ref, above_ref, below_ref):
    def write(even):
        for source, out_ref in ((near_ref, above_ref if even else below_ref), (far_ref, below_ref if even else above_ref)):
            for index in range(out_ref.shape[0]):
                out_ref[index] = source[index]

    by_parity(write)


def start_kernel(out_ref):
    out_ref[...] = jnp.zeros(out_ref.shape, jnp.float32)


def thrust_kernel(thrust_ref, _, thrust_rows_ref, slope_rows_ref):
    thrust_rows_ref[...] = jnp.zeros(thrust_rows_ref.shape, jnp.float32)
    for turbine in range(thrust_ref.shape[0]):
        thrust_rows_ref[turbine : turbine + 1, :] = jnp.full(
            (1, thrust_rows_ref.shape[1]), thrust_ref[turbine], jnp.float32
        )
    root = jnp.sqrt(1.0 - thrust_rows_ref[...])
    slope_rows_ref[...] = 4.0 / (root * jnp.square(1.0 + root))


def pack_kernel(_, map_ref, scale_ref, pops_ref, lam_ref, fields_ref, rows_ref, near_ref, far_ref):
    width, span = lam_ref.shape[1], lam_ref.shape[2]
    for side in range(2):
        for index, (far, member) in enumerate(ROW_LIST[side]):
            row = far - 1 if side == 0 else span - far
            rows_ref[side, index * width : (index + 1) * width, :] = lam_ref[member, :, row, :]
    last = pops_ref.shape[0] - 1
    for plane in range(width):
        for index, value in enumerate(decode(scale_ref, pops_ref, last, plane)):
            fields_ref[index, plane] = value
        fields_ref[19, plane] = map_ref[plane].astype(jnp.float32)
        pops = decode(scale_ref, pops_ref, 0, plane)
        rho, momentum = pops[0], None
        for member in range(1, 19):
            rho = rho + pops[member]
        for member in X_UP:
            pair = pops[member] - pops[member + 1]
            momentum = pair if momentum is None else momentum + pair
        ux = momentum / rho
        fields_ref[20, plane] = (-1.5 / 36.0) * ux * jnp.abs(ux)
    for side in range(2):
        row = 0 if side == 0 else span - 1
        for field in range(FIELDS):
            start = (HALO + field) * width
            rows_ref[side, start : start + width, :] = fields_ref[field, :, row, :]
    hand_out(
        lambda field: fields_ref[field, 0],
        lambda field: fields_ref[field, width - 1],
        near_ref,
        far_ref,
    )


def span_shift(value, move, row):
    span = value.shape[0]
    place = lax.broadcasted_iota(jnp.int32, value.shape, 0)
    if move == 1:
        return jnp.where(place == span - 1, row, pltpu.roll(value, span - 1, 0))
    return jnp.where(place == 0, row, pltpu.roll(value, 1, 0))


def roll_z(value, move, edges, walls=None):
    height = value.shape[1]
    if move == 0:
        return value
    shift, edge = (height - 1, edges[1]) if move == 1 else (1, edges[0])
    return jnp.where(edge, 0.0 if walls is None else walls, pltpu.roll(value, shift, 1))


def wall_masks(shape):
    lane = lax.broadcasted_iota(jnp.int32, shape, 1)
    return lane == 0, lane == shape[1] - 1


def gather_mu(source, row_of, plane, edges):
    mu = []
    for member in range(19):
        move_x, move_y, move_z = VELOCITIES[member]
        value = source(plane + move_x, member)
        if value is not None and move_y != 0:
            side = 0 if move_y == 1 else 1
            value = span_shift(value, move_y, row_of(side, plane + move_x, member))
        if move_z != 0:
            walls = source(plane, OPPOSITE[member])
            if value is None:
                value = jnp.where(edges[1 if move_z == 1 else 0], walls, 0.0)
            else:
                value = roll_z(value, move_z, edges, walls)
        mu.append(value)
    return mu


def own_lam(lam_ref):
    def source(plane, member):
        return lam_ref[member, plane] if 0 <= plane < lam_ref.shape[1] else None

    return source


def got_row(rows_ref, width):
    def row_of(side, plane, member):
        place = ROW_LIST[side].index((1, member)) * width + plane
        return rows_ref[side, place : place + 1, :]

    return row_of


def corner_row(face_ref, side, index):
    slot = side * CORNER + index
    return face_ref[10 + slot // 8, slot % 8 : slot % 8 + 1, :]


def faces_kernel(thrust_ref, lam_ref, rows_ref, coef_ref, near_ref, far_ref, field_ref, part_ref, pack_ref, low_ref, high_ref):
    width, span = lam_ref.shape[1], lam_ref.shape[2]
    edges = wall_masks(lam_ref.shape[2:])
    source, row_of = own_lam(lam_ref), got_row(rows_ref, width)
    pack_ref[...] = jnp.zeros(pack_ref.shape, jnp.float32)
    field_ref[...] = jnp.zeros(field_ref.shape, jnp.float32)
    for side in range(2):
        for index, (far, member) in enumerate(PACK_LIST[side]):
            if far > 0:
                rows = rows_ref[side, index * width : (index + 1) * width, :]
            else:
                rows = lam_ref[member, :, span - 1 if side == 0 else 0, :]
            pack_ref[side, index, 2 : width + 2, :] = rows
        for field in range(FIELDS):
            start = (HALO + field) * width
            field_ref[side, field, 2 : width + 2, :] = rows_ref[side, start : start + width, :]
    place = lax.broadcasted_iota(jnp.int32, pack_ref.shape[2:], 0)
    inside = jnp.logical_and(place >= 2, place < width + 2)
    pack_edges = wall_masks(pack_ref.shape[2:])
    for side, (sign, wanted) in enumerate(((1, Y_UP), (-1, Y_DOWN))):
        mu = []
        for member in range(19):
            move_x, move_y, move_z = VELOCITIES[member]
            value = pack_ref[side, PACK_LIST[side].index((1 + sign * move_y, member))]
            if move_x != 0:
                value = pltpu.roll(value, (-move_x) % value.shape[0], 0)
            if move_z != 0:
                walls = pack_ref[side, PACK_LIST[side].index((1, OPPOSITE[member]))]
                value = roll_z(value, move_z, pack_edges, walls)
            mu.append(value)
        pops = [field_ref[side, member] for member in range(19)]
        coefs = plane_coefs(pops, turbine_cells(field_ref[side, 19], thrust_ref))
        lam, _ = plane_adjoint(mu, lambda index: coefs[index], wanted)
        for index, member in enumerate(wanted):
            part_ref[side, index] = jnp.where(inside, lam[member], 0.0)
    for out_ref, plane, members in ((low_ref, 0, X_UP), (high_ref, width - 1, X_DOWN)):
        lam, _ = plane_adjoint(
            gather_mu(source, row_of, plane, edges),
            lambda index: coef_ref[index, min(plane, 1)],
            members,
        )
        for index, member in enumerate(members):
            value, move_y = lam_ref[member, plane], VELOCITIES[member][1]
            if move_y != 0:
                value = span_shift(value, move_y, row_of(0 if move_y == 1 else 1, plane, member))
            out_ref[index] = value
            out_ref[5 + index] = lam[member]
        for side, (sign, wanted) in enumerate(((1, Y_UP), (-1, Y_DOWN))):
            sources = [
                pack_ref.at[side, PACK_LIST[side].index((1 + sign * VELOCITIES[member][1], member))]
                for member in members
            ]
            corner = VELOCITIES.index((VELOCITIES[members[0]][0], sign, 0))
            sources.append(part_ref.at[side, wanted.index(corner)])
            sources += [field_ref.at[side, field] for field in range(FIELDS)]
            for index, ref in enumerate(sources):
                slot = side * CORNER + index
                out_ref[10 + slot // 8, slot % 8 : slot % 8 + 1, :] = ref[plane + 2 : plane + 3, :]
    hand_out(lambda index: low_ref[index], lambda index: high_ref[index], near_ref, far_ref)


def middle_kernel(thrust_ref, lam_ref, rows_ref, coef_ref, near_ref, far_ref, mid_ref, cell_ref, face_ref, ids_ref, gains_ref, above_ref, below_ref):
    width = lam_ref.shape[1]
    edges = wall_masks(lam_ref.shape[2:])
    source, row_of = own_lam(lam_ref), got_row(rows_ref, width)
    take_in(near_ref, far_ref, above_ref, below_ref)
    for side, fields_ref in enumerate((above_ref, below_ref)):
        ids_ref[side], gains_ref[side] = fields_ref[19], fields_ref[20]
    for plane in range(width):
        mu = gather_mu(source, row_of, plane, edges)
        lam, mx = plane_adjoint(mu, lambda index: coef_ref[index, plane])
        for member in range(19):
            mid_ref[member, plane] = lam[member]
        cell_ref[plane] = mx * coef_ref[GAIN, plane]
    for side, (fields_ref, plane, members, wanted) in enumerate(
        ((above_ref, width - 1, X_DOWN, X_UP), (below_ref, 0, X_UP, X_DOWN))
    ):
        mu = [None] * 19
        for member in members:
            value, (_, move_y, move_z) = lam_ref[member, plane], VELOCITIES[member]
            if move_y != 0:
                value = span_shift(value, move_y, row_of(0 if move_y == 1 else 1, plane, member))
            mu[member] = roll_z(value, move_z, edges)
        pops = [fields_ref[member] for member in range(19)]
        coefs = plane_coefs(pops, turbine_cells(fields_ref[19], thrust_ref))
        lam, _ = plane_adjoint(mu, lambda index: coefs[index], wanted)
        for index, member in enumerate(wanted):
            face_ref[side, index] = lam[member]


def pair_kernel(turbines, thrust_ref, lam_ref, rows_ref, near_ref, far_ref, late_ref, early_ref, fields_ref,
                part_mid_ref, part_cell_ref, part_face_ref, ids_ref, gains_ref, part_edge_ref, pack_ref,
                out_ref, next_ref, mid_ref, edge_ref, line_ref, above_ref, below_ref):
    width, span, height = lam_ref.shape[1:]
    take_in(near_ref, far_ref, above_ref, below_ref)
    edges = wall_masks((span, height))
    pack_shape = pack_ref.shape[2:]
    pack_edges = wall_masks(pack_shape)
    place = lax.broadcasted_iota(jnp.int32, pack_shape, 0)
    totals = [part_cell_ref[plane] for plane in range(width)]
    for face_ref, plane, members in ((above_ref, width - 1, X_UP), (below_ref, 0, X_DOWN)):
        mu = [None] * 19
        for index, member in enumerate(members):
            mu[member] = roll_z(face_ref[index], VELOCITIES[member][2], edges)
        lam, mx = plane_adjoint(mu, lambda index: late_ref[index, plane])
        for member in range(19):
            mid_ref[member, 0 if plane == 0 else 1] = part_mid_ref[member, plane] + lam[member]
        totals[plane] = totals[plane] + mx * late_ref[GAIN, plane]

    def beyond(below, above, rest):
        return jnp.where(place == 1, below, jnp.where(place == width + 2, above, rest))

    halo_tiles = []
    for side, (sign, wanted) in enumerate(((1, Y_UP), (-1, Y_DOWN))):
        mu = [None] * 19
        for members, got_ref, got_place, own_place in (
            (X_UP, above_ref, width + 1, 1),
            (X_DOWN, below_ref, 2, width + 2),
        ):
            plane = 0 if own_place == 1 else width - 1
            for index, member in enumerate(members):
                far = 1 + sign * VELOCITIES[member][1]
                if far > 0:
                    start = ROW_LIST[side].index((far, member)) * width + plane
                    own = rows_ref[side, start : start + 1, :]
                else:
                    inner = span - 1 if side == 0 else 0
                    own = lam_ref[member, plane, inner : inner + 1, :]
                value = jnp.where(
                    place == got_place,
                    corner_row(got_ref, side, index),
                    jnp.where(place == own_place, own, 0.0),
                )
                mu[member] = roll_z(value, VELOCITIES[member][2], pack_edges)
        fields = [
            beyond(
                corner_row(below_ref, side, 6 + field),
                corner_row(above_ref, side, 6 + field),
                pack_ref[side, field],
            )
            for field in range(FIELDS)
        ]
        coefs = plane_coefs(fields[:19], turbine_cells(fields[19], thrust_ref))
        lam, _ = plane_adjoint(mu, lambda index: coefs[index], wanted)
        for index, member in enumerate(wanted):
            value = part_edge_ref[side, index] + lam[member]
            if VELOCITIES[member][0] == 1:
                value = value + jnp.where(place == width + 2, corner_row(above_ref, side, 5), 0.0)
            elif VELOCITIES[member][0] == -1:
                value = value + jnp.where(place == 1, corner_row(below_ref, side, 5), 0.0)
            edge_ref[side, index] = value
        halo_tiles.append((fields[20], fields[19]))

    def middle(plane, member):
        if plane >= width:
            index = X_UP.index(member)
            return above_ref[5 + index] + part_face_ref[0, index]
        if plane < 0:
            index = X_DOWN.index(member)
            return below_ref[5 + index] + part_face_ref[1, index]
        if plane in (0, width - 1):
            return mid_ref[member, 0 if plane == 0 else 1]
        return part_mid_ref[member, plane]

    def middle_row(side, plane, member):
        index = (Y_UP, Y_DOWN)[side].index(member)
        return edge_ref[side, index, plane + 2 : plane + 3, :]

    for plane in range(width):
        mu = gather_mu(middle, middle_row, plane, edges)
        lam, mx = plane_adjoint(mu, lambda index: early_ref[index, plane])
        for member in range(19):
            out_ref[member, plane] = lam[member]
        totals[plane] = totals[plane] + mx * early_ref[GAIN, plane]

    for side, (members, row) in enumerate(((Y_UP, 0), (Y_DOWN, span - 1))):
        for index, member in enumerate(members):
            start = (5 * side + index) * width
            next_ref[start : start + width, :] = out_ref[member, :, row, :]

    nothing = jnp.zeros((1, height), jnp.float32)
    up, down = [], []
    for plane in range(width):
        up.append(
            2.0 * out_ref[1, plane]
            + span_shift(out_ref[7, plane], 1, nothing)
            + span_shift(out_ref[9, plane], -1, nothing)
            + roll_z(out_ref[11, plane], 1, edges)
            + roll_z(out_ref[13, plane], -1, edges)
        )
        down.append(
            2.0 * out_ref[2, plane]
            + span_shift(out_ref[8, plane], -1, nothing)
            + span_shift(out_ref[10, plane], 1, nothing)
            + roll_z(out_ref[12, plane], -1, edges)
            + roll_z(out_ref[14, plane], 1, edges)
        )
    tiles = []
    for plane in range(-1, width + 1):
        value = None
        if plane + 1 < width:
            value = up[plane + 1]
        if plane >= 1:
            value = -down[plane - 1] if value is None else value - down[plane - 1]
        if plane < 0 or plane >= width:
            side = 1 if plane < 0 else 0
            tiles.append((gains_ref[side] * value, ids_ref[side]))
            continue
        value = value + jnp.where(edges[1], out_ref[12, plane] - out_ref[13, plane], 0.0)
        value = value + jnp.where(edges[0], out_ref[14, plane] - out_ref[11, plane], 0.0)
        tiles.append((totals[plane] + fields_ref[20, plane] * value, fields_ref[19, plane]))
    line_ref[...] = jnp.zeros(line_ref.shape, jnp.float32)
    for side, (upward, downward, row) in enumerate(((9, 8, span - 1), (7, 10, 0))):
        line_ref[side, 0, 1 : width + 1, :] = out_ref[upward, :, row, :]
        line_ref[side, 1, 3 : width + 3, :] = out_ref[downward, :, row, :]
        gain, ids = halo_tiles[side]
        tiles.append(((line_ref[side, 0] - line_ref[side, 1]) * gain, ids))
    start = 10 * width
    next_ref[start:, :] = jnp.zeros((next_ref.shape[0] - start, height), jnp.float32)
    for turbine in range(turbines):
        row = None
        for value, ids in tiles:
            kept = jnp.sum(jnp.where(ids == float(turbine), value, 0.0), axis=0, keepdims=True)
            row = kept if row is None else row + kept
        next_ref[start + turbine : start + turbine + 1, :] = row


def last_faces_kernel(lam_ref, rows_ref, sums_ref, got_ref, near_ref, far_ref, total_ref):
    width = lam_ref.shape[1]

    def row_of(side, plane, member):
        place = (5 * side + (Y_UP, Y_DOWN)[side].index(member)) * width + plane
        return rows_ref[place : place + 1, :]

    def moved(members, plane):
        def tile(index):
            member = members[index]
            value, move_y = lam_ref[member, plane], VELOCITIES[member][1]
            if move_y == 0:
                return value
            return span_shift(value, move_y, row_of(0 if move_y == 1 else 1, plane, member))

        return tile

    total_ref[...] = sums_ref[...] + got_ref[...]
    hand_out(moved(X_UP, 0), moved(X_DOWN, width - 1), near_ref, far_ref)


def last_kernel(lam_ref, rows_ref, near_ref, far_ref, coef_ref, out_ref):
    width, span, height = lam_ref.shape[1:]
    lane = lax.broadcasted_iota(jnp.int32, (span, height), 1)
    first, last = lane == 0, lane == height - 1
    odd = jnp.full((span, height), lax.rem(lax.axis_index("gx"), 2)) == 1

    def source(plane, member):
        if plane >= width:
            index = X_UP.index(member)
            return jnp.where(odd, far_ref[index], near_ref[index])
        if plane < 0:
            index = X_DOWN.index(member)
            return jnp.where(odd, near_ref[index], far_ref[index])
        value, move_y = lam_ref[member, plane], VELOCITIES[member][1]
        if move_y == 0:
            return value
        side = 0 if move_y == 1 else 1
        place = (5 * side + (Y_UP, Y_DOWN)[side].index(member)) * width + plane
        return span_shift(value, move_y, rows_ref[place : place + 1, :])

    for plane in range(width):
        mu = []
        for member in range(19):
            move_x, _, move_z = VELOCITIES[member]
            value = source(plane + move_x, member)
            if move_z == 1:
                value = jnp.where(
                    last, lam_ref[OPPOSITE[member], plane], pltpu.roll(value, height - 1, 1)
                )
            elif move_z == -1:
                value = jnp.where(first, lam_ref[OPPOSITE[member], plane], pltpu.roll(value, 1, 1))
            mu.append(value)
        lam, _ = plane_adjoint(mu, lambda index: coef_ref[index, plane])
        for member in range(19):
            out_ref[member, plane] = lam[member]


def call(kernel, outs, *args, scratch=(), smem_first=False, micros=1):
    specs = [pl.BlockSpec(memory_space=VMEM)] * len(args)
    if smem_first:
        specs[0] = pl.BlockSpec(memory_space=pltpu.SMEM)
    return pl.pallas_call(
        kernel,
        out_shape=tuple(jax.ShapeDtypeStruct(shape, jnp.float32) for shape in outs),
        in_specs=specs,
        out_specs=tuple(pl.BlockSpec(memory_space=VMEM) for _ in outs),
        scratch_shapes=[pltpu.VMEM(shape, jnp.float32) for shape in scratch],
        cost_estimate=pl.CostEstimate(
            flops=int(1e6 * micros), bytes_accessed=int(2e6 * micros), transcendentals=0
        ),
        compiler_params=pltpu.CompilerParams(vmem_limit_bytes=32 * 1024 * 1024),
    )(*args)


def ring(axis, step):
    count = lax.axis_size(axis)
    return [(i, (i + step) % count) for i in range(count)]


def swap_rows(low, high):
    return lax.ppermute(low, "gy", ring("gy", -1)), lax.ppermute(high, "gy", ring("gy", 1))


def swap_near(near):
    count = lax.axis_size("gx")
    assert count % 2 == 0
    return lax.ppermute(near, "gx", [(i, i ^ 1) for i in range(count)])


def swap_far(far):
    count = lax.axis_size("gx")
    return lax.ppermute(
        far, "gx", [(i, (i + 1 if i % 2 else i - 1) % count) for i in range(count)]
    )


def flips(value, axis, flip_list):
    count = lax.axis_size(axis)
    parts = [lax.ppermute(value, axis, [(i, i ^ flip) for i in range(count)]) for flip in flip_list]
    return sum(parts, value)


def sum_bits(value, axis, start):
    count = lax.axis_size(axis)
    while start < count:
        stop = min(4 * start, count)
        value = flips(value, axis, range(start, stop, start))
        start = stop
    return value


def last_exchange(lam, packed):
    width, height = lam.shape[1], lam.shape[3]
    rows_count = 10 * width
    sums = packed[rows_count:]
    if lax.axis_size("gy") == 2:
        got = lax.ppermute(packed, "gy", ring("gy", 1))
        rows, got = got[:rows_count], got[rows_count:]
    else:
        rows = jnp.concatenate(
            swap_rows(packed[: rows_count // 2], packed[rows_count // 2 : rows_count])
        )
        count = lax.axis_size("gy")
        got = (lax.psum(sums, "gy") if count & (count - 1) else sum_bits(sums, "gy", 1)) - sums
    near, far, sums = call(
        last_faces_kernel,
        [(5, lam.shape[2], height), (5, lam.shape[2], height), sums.shape],
        lam,
        rows,
        sums,
        got,
        micros=0.1,
    )
    count = lax.axis_size("gx")
    apart = count & (count - 1) == 0 and count > 2
    if apart:
        sums = flips(sums, "gx", [2])
    got_near, got_far = swap_near(near), swap_far(far)
    if apart:
        sums = sum_bits(flips(sums, "gx", [1]), "gx", 4)
    else:
        sums = lax.psum(sums, "gx")
    return rows, got_near, got_far, sums


def shards(fwd_pops, fwd_scale, seed_adjoint, turbine_map, thrust):
    steps, _, width, span, height = fwd_pops.shape
    assert steps == 3 and span == 8
    turbines = thrust.shape[0]
    turbine_rows = -(-turbines // 8) * 8
    sublanes = -(-(width + 4) // 8) * 8
    whole = (19, width, span, height)
    (begun,) = call(start_kernel, [(8, height)], micros=400)
    fields, rows, near_fields, far_fields = call(
        pack_kernel,
        [
            (FIELDS, width, span, height),
            (2, (HALO + FIELDS) * width, height),
            (FIELDS, span, height),
            (FIELDS, span, height),
        ],
        begun,
        turbine_map,
        fwd_scale,
        fwd_pops,
        seed_adjoint,
        micros=0.6,
    )
    thrust_rows, slope_rows = call(
        thrust_kernel,
        [(turbine_rows, height)] * 2,
        thrust,
        fields,
        smem_first=True,
        micros=0.3,
    )
    if lax.axis_size("gy") == 2:
        rows = lax.ppermute(rows, "gy", ring("gy", 1))
    else:
        rows = jnp.stack(swap_rows(rows[0], rows[1]))
    far_fields = swap_far(far_fields)
    edge_coefs, near_fields = call(
        edge_coef_kernel,
        [(COEFS, 2, span, height), near_fields.shape],
        thrust_rows,
        fields,
        near_fields,
        micros=0.3,
    )
    near_fields = swap_near(near_fields)
    face, edge = (FACE_TILES, span, height), (2, 5, sublanes, height)
    near, far, pack, part_edge = call(
        faces_kernel,
        [face, face, (2, FIELDS, sublanes, height), edge],
        thrust_rows,
        seed_adjoint,
        rows,
        edge_coefs,
        scratch=[(2, len(PACK_LIST[0]), sublanes, height), face, face],
        micros=0.6,
    )
    far = swap_far(far)
    near, *coefs = call(
        coef_kernel,
        [near.shape] + [(COEFS, width, span, height)] * steps,
        thrust_rows,
        turbine_map,
        fwd_scale,
        fwd_pops,
        near,
        micros=1.5,
    )
    near = swap_near(near)
    halo = (FIELDS, span, height)
    parts = call(
        middle_kernel,
        [whole, (width, span, height), (2, 5, span, height), (2, span, height), (2, span, height)],
        thrust_rows,
        seed_adjoint,
        rows,
        coefs[2],
        near_fields,
        far_fields,
        scratch=[halo, halo],
        micros=0.6,
    )
    lam, packed = call(
        lambda *refs: pair_kernel(turbines, *refs),
        [whole, (10 * width + turbine_rows, height)],
        thrust_rows,
        seed_adjoint,
        rows,
        near,
        far,
        coefs[2],
        coefs[1],
        fields,
        *parts,
        part_edge,
        pack,
        scratch=[(19, 2, span, height), edge, (2, 2, sublanes, height), face, face],
        micros=0.8,
    )
    rows, near, far, sums = last_exchange(lam, packed)
    (lam,) = call(last_kernel, [whole], lam, rows, near, far, coefs[0], micros=0.5)
    thrust_grad = jnp.sum((slope_rows * sums)[:turbines], axis=1)
    return (lam, thrust_grad)


def solution(mesh):
    placed = (
        P(None, None, "gx", "gy", None),
        P(None, "gx", "gy", None),
        P(None, "gx", "gy", None),
        P("gx", "gy", None),
        P(),
    )
    return jax.shard_map(
        shards,
        mesh=mesh,
        in_specs=placed,
        out_specs=(P(None, "gx", "gy", None), P()),
        check_vma=False,
    )
```

```python
import jax
import jax.numpy as jnp
from jax import lax
from jax.experimental import pallas as pl
from jax.experimental.pallas import tpu as pltpu
from jax.sharding import PartitionSpec as P

VELOCITIES = (
    (0, 0, 0),
    (1, 0, 0),
    (-1, 0, 0),
    (0, 1, 0),
    (0, -1, 0),
    (0, 0, 1),
    (0, 0, -1),
    (1, 1, 0),
    (-1, -1, 0),
    (1, -1, 0),
    (-1, 1, 0),
    (1, 0, 1),
    (-1, 0, -1),
    (1, 0, -1),
    (-1, 0, 1),
    (0, 1, 1),
    (0, -1, -1),
    (0, 1, -1),
    (0, -1, 1),
)
OPPOSITE = (0, 2, 1, 4, 3, 6, 5, 8, 7, 10, 9, 12, 11, 14, 13, 16, 15, 18, 17)
WEIGHTS = tuple([1.0 / 3.0] + [1.0 / 18.0] * 6 + [1.0 / 36.0] * 12)
MEAN_FLOW = 0.1
TAU_BASE = 0.51
SMAG_COEF = 18.0 * 1.4142135623730951 * 0.17 * 0.17
QUAD_FLOOR = 0.0001

X_UP = (1, 7, 9, 11, 13)
X_DOWN = (2, 8, 10, 12, 14)
Y_UP = (3, 7, 10, 15, 17)
Y_DOWN = (4, 8, 9, 16, 18)

KEEP, MASS, FLUX, UX, UY, UZ, Q1 = 19, 20, 21, 22, 23, 24, 25
RATE, BULK, PX, PY, PZ, DRAG, DRAG_U, GAIN = 34, 35, 36, 37, 38, 39, 40, 41
COEFS = 42

FIELDS = 21

VMEM = pltpu.VMEM


def halo_list(axis, sign):
    near = [
        (1, m) for m in range(19) if VELOCITIES[m][axis] * sign >= 0 or VELOCITIES[m][2] != 0
    ]
    return near + [(2, m) for m in range(19) if VELOCITIES[m][axis] * sign == 1]


SIGNS = (1, -1)
ROW_LIST = [halo_list(1, sign) for sign in SIGNS]
INNER_LIST = [[(0, m) for m in range(19) if VELOCITIES[m][1] * sign == -1] for sign in SIGNS]
PACK_LIST = [ROW_LIST[side] + INNER_LIST[side] for side in range(2)]
HALO = len(ROW_LIST[0])
CORNER = 6 + FIELDS
NEXT_LIST = [
    [[(far, m) for far, m in ROW_LIST[y] if VELOCITIES[m][0] == sign] for y in range(2)]
    for sign in SIGNS
]
FIRST_ROWS = -(-(HALO + len(NEXT_LIST[0][0]) + FIELDS) // 8) * 8
MIRROR = [VELOCITIES.index((a, -b, c)) for a, b, c in VELOCITIES]
STATIC = 10 + -(-2 * CORNER // 8)
FACE_TILES = STATIC + FIELDS


def base_values():
    values = []
    for member in range(19):
        along = float(VELOCITIES[member][0])
        values.append(
            WEIGHTS[member]
            * (
                1.0
                + 3.0 * MEAN_FLOW * along
                + 4.5 * MEAN_FLOW * MEAN_FLOW * along * along
                - 1.5 * MEAN_FLOW * MEAN_FLOW
            )
        )
    return values


def plane_coefs(pops, thrust_cell):
    rho = pops[0]
    for member in range(1, 19):
        rho = rho + pops[member]
    inv_rho = 1.0 / rho
    vel = []
    for axis_id in range(3):
        moment = None
        for member in range(19):
            component = VELOCITIES[member][axis_id]
            if component == 1:
                moment = pops[member] if moment is None else moment + pops[member]
            elif component == -1:
                moment = moment - pops[member]
        vel.append(moment * inv_rho)
    ux, uy, uz = vel
    speed_sq = ux * ux + uy * uy + uz * uz
    rest = 1.0 - 1.5 * speed_sq
    part = []
    for member in range(19):
        if member == 0:
            part.append(pops[0] - (WEIGHTS[0] * rho) * rest)
            continue
        proj = None
        for axis_id in range(3):
            component = VELOCITIES[member][axis_id]
            if component == 1:
                proj = vel[axis_id] if proj is None else proj + vel[axis_id]
            elif component == -1:
                proj = -vel[axis_id] if proj is None else proj - vel[axis_id]
        part.append(pops[member] - (WEIGHTS[member] * rho) * (rest + 3.0 * proj + 4.5 * proj * proj))

    def pair(member):
        return part[member] + part[member + 1]

    in_xy, in_xz, in_yz = pair(7) + pair(9), pair(11) + pair(13), pair(15) + pair(17)
    pxx, pyy, pzz = pair(1) + in_xy + in_xz, pair(3) + in_xy + in_yz, pair(5) + in_xz + in_yz
    pxy, pxz, pyz = pair(7) - pair(9), pair(11) - pair(13), pair(15) - pair(17)
    square = (
        pxx * pxx + pyy * pyy + pzz * pzz + 2.0 * (pxy * pxy + pxz * pxz + pyz * pyz) + QUAD_FLOOR
    )
    size = jnp.sqrt(square)
    root = jnp.sqrt(TAU_BASE * TAU_BASE + SMAG_COEF * size * inv_rho)
    omega = 1.0 / (0.5 * (TAU_BASE + root))
    pux = pxx * ux + pxy * uy + pxz * uz
    puy = pxy * ux + pyy * uy + pyz * uz
    puz = pxz * ux + pyz * uy + pzz * uz
    flux = omega * (3.0 / 36.0)
    drag = (3.0 / 36.0) * thrust_cell * jnp.abs(ux) * inv_rho
    result = list(part)
    result.append(1.0 - omega)
    result.append((omega * (1.0 / 36.0)) * (1.0 + 1.5 * speed_sq))
    result.append(flux)
    result.extend(vel)
    result.extend((pxx, pyy, pzz))
    result.extend((pxx + pyy + 2.0 * pxy, pxx + pyy - 2.0 * pxy))
    result.extend((pxx + pzz + 2.0 * pxz, pxx + pzz - 2.0 * pxz))
    result.extend((pyy + pzz + 2.0 * pyz, pyy + pzz - 2.0 * pyz))
    result.append((0.25 * SMAG_COEF) * omega * omega * inv_rho / (root * size))
    result.append(
        (pux * ux + puy * uy + puz * uz) - (pxx + pyy + pzz) * (1.0 / 3.0) - square * inv_rho
    )
    result.extend((-2.0 * pux, -2.0 * puy, -2.0 * puz))
    result.append(drag)
    result.append(drag * ux)
    result.append((-1.5 / 36.0) * ux * jnp.abs(ux))
    return result


def plus(*values):
    kept = [value for value in values if value is not None]
    return sum(kept[1:], kept[0]) if kept else None


def minus(left, right):
    if right is None:
        return left
    return -right if left is None else left - right


def times(left, right):
    return None if left is None or right is None else left * right


def plane_adjoint(mu, coef, wanted=range(19)):
    total, diff = {}, {}
    for member in range(1, 19, 2):
        total[member] = plus(mu[member], mu[member + 1])
        diff[member] = minus(mu[member], mu[member + 1])
    two_x, two_y, two_z = times(total[1], 2.0), times(total[3], 2.0), times(total[5], 2.0)
    in_xy, in_xz = plus(total[7], total[9]), plus(total[11], total[13])
    in_yz = plus(total[15], total[17])
    mxx, myy, mzz = plus(two_x, in_xy, in_xz), plus(two_y, in_xy, in_yz), plus(two_z, in_xz, in_yz)
    mxy, mxz = minus(total[7], total[9]), minus(total[11], total[13])
    myz = minus(total[15], total[17])
    m0 = plus(times(mu[0], 12.0), plus(two_x, two_y, two_z), plus(in_xy, in_xz, in_yz))
    mx = plus(times(diff[1], 2.0), plus(diff[7], diff[9]), plus(diff[11], diff[13]))
    my = plus(times(diff[3], 2.0), minus(diff[7], diff[9]), plus(diff[15], diff[17]))
    mz = plus(times(diff[5], 2.0), minus(diff[11], diff[13]), minus(diff[15], diff[17]))
    ux, uy, uz = coef(UX), coef(UY), coef(UZ)
    vx = plus(times(mxx, ux), times(mxy, uy), times(mxz, uz))
    vy = plus(times(mxy, ux), times(myy, uy), times(myz, uz))
    vz = plus(times(mxz, ux), times(myz, uy), times(mzz, uz))
    along = [mu[member] * coef(member) for member in range(19) if mu[member] is not None]
    while len(along) > 1:
        along = [
            along[k] + along[k + 1] if k + 1 < len(along) else along[k]
            for k in range(0, len(along), 2)
        ]
    gamma = along[0] * coef(RATE)
    flux = coef(FLUX)
    alpha = (
        coef(MASS) * m0
        - 1.5 * flux * (vx * ux + vy * uy + vz * uz)
        + gamma * coef(BULK)
        + mx * coef(DRAG_U)
    )
    beta_x = flux * (plus(mx, 3.0 * vx) - ux * m0) + gamma * coef(PX) - mx * coef(DRAG)
    beta_y = flux * (plus(my, 3.0 * vy) - uy * m0) + gamma * coef(PY)
    beta_z = flux * (plus(mz, 3.0 * vz) - uz * m0) + gamma * coef(PZ)
    keep = coef(KEEP)
    odd = {
        1: beta_x,
        3: beta_y,
        5: beta_z,
        7: beta_x + beta_y,
        9: beta_x - beta_y,
        11: beta_x + beta_z,
        13: beta_x - beta_z,
        15: beta_y + beta_z,
        17: beta_y - beta_z,
    }
    result = {}
    for member in wanted:
        if member == 0:
            result[0] = plus(times(mu[0], keep), alpha)
            continue
        forward = member - 1 + member % 2
        even = alpha + gamma * coef(Q1 + forward // 2)
        rest = even + odd[forward] if member == forward else even - odd[forward]
        result[member] = plus(times(mu[member], keep), rest)
    return result, mx


def turbine_cells(ids, thrust_ref):
    ratio = jnp.zeros(ids.shape, jnp.float32)
    for turbine in range(thrust_ref.shape[0]):
        row = thrust_ref[turbine : turbine + 1, :]
        ratio = jnp.where(ids == jnp.asarray(turbine, ids.dtype), row, ratio)
    return jnp.where(ids >= 0, local_thrust(ratio), 0.0)


def local_thrust(values):
    return 4.0 * values / jnp.square(1.0 + jnp.sqrt(1.0 - values))


def decode(scale_ref, pops_ref, instant, plane):
    base = base_values()
    scale = scale_ref[instant, plane]
    return [
        base[member] * (1.0 + scale * pops_ref[instant, member, plane].astype(jnp.float32))
        for member in range(19)
    ]


def coef_kernel(thrust_ref, map_ref, scale_ref, pops_ref, *out_refs):
    for plane in range(pops_ref.shape[2]):
        thrust_cell = turbine_cells(map_ref[plane], thrust_ref)
        for instant, out_ref in enumerate(out_refs):
            pops = decode(scale_ref, pops_ref, instant, plane)
            for index, value in enumerate(plane_coefs(pops, thrust_cell)):
                out_ref[index, plane] = value


def by_parity(even):
    odd = lax.rem(lax.axis_index("gx"), 2) == 1
    pl.when(jnp.logical_not(odd))(lambda: even(True))
    pl.when(odd)(lambda: even(False))


def hand_out(low, high, near_ref, far_ref):
    def write(even):
        for source, out_ref in ((low, far_ref), (high, near_ref)) if even else ((low, near_ref), (high, far_ref)):
            for index in range(out_ref.shape[0]):
                out_ref[index] = source(index)

    by_parity(write)


def take_in(near_ref, far_ref, above_ref, below_ref):
    def write(even):
        for source, out_ref in ((near_ref, above_ref if even else below_ref), (far_ref, below_ref if even else above_ref)):
            for index in range(out_ref.shape[0]):
                out_ref[index] = source[index]

    by_parity(write)


def start_kernel(out_ref):
    out_ref[...] = jnp.zeros(out_ref.shape, jnp.float32)


def write_thrust(thrust_ref, thrust_rows_ref, slope_rows_ref):
    thrust_rows_ref[...] = jnp.zeros(thrust_rows_ref.shape, jnp.float32)
    for turbine in range(thrust_ref.shape[1]):
        thrust_rows_ref[turbine : turbine + 1, :] = jnp.broadcast_to(
            thrust_ref[0:1, turbine : turbine + 1], (1, thrust_rows_ref.shape[1])
        )
    root = jnp.sqrt(1.0 - thrust_rows_ref[...])
    slope_rows_ref[...] = 4.0 / (root * jnp.square(1.0 + root))


def pack_kernel(_, thrust_ref, map_ref, scale_ref, pops_ref, lam_ref, fields_ref, first_ref, thrust_rows_ref, slope_rows_ref):
    width, span = lam_ref.shape[1], lam_ref.shape[2]
    write_thrust(thrust_ref, thrust_rows_ref, slope_rows_ref)
    last = pops_ref.shape[0] - 1
    for plane in range(width):
        for index, value in enumerate(decode(scale_ref, pops_ref, last, plane)):
            fields_ref[index, plane] = value
        fields_ref[19, plane] = map_ref[plane].astype(jnp.float32)
        pops = decode(scale_ref, pops_ref, 0, plane)
        rho, momentum = pops[0], None
        for member in range(1, 19):
            rho = rho + pops[member]
        for member in X_UP:
            pair = pops[member] - pops[member + 1]
            momentum = pair if momentum is None else momentum + pair
        ux = momentum / rho
        fields_ref[20, plane] = (-1.5 / 36.0) * ux * jnp.abs(ux)
    first_ref[...] = jnp.zeros(first_ref.shape, jnp.float32)

    def write(even):
        plane, inner = (0, 1) if even else (width - 1, width - 2)
        for side in range(2):
            picks = [(lam_ref, m, plane, far) for far, m in ROW_LIST[side]]
            picks += [(lam_ref, m, inner, far) for far, m in NEXT_LIST[0 if even else 1][side]]
            picks += [(fields_ref, field, plane, 1) for field in range(FIELDS)]
            for index, (ref, member, at, far) in enumerate(picks):
                row = far - 1 if side == 0 else span - far
                first_ref[side, index : index + 1, :] = ref[member, at, row : row + 1, :]

    by_parity(write)


def rows_kernel(lam_ref, fields_ref, _, rows_ref):
    width, span = lam_ref.shape[1], lam_ref.shape[2]
    for side in range(2):
        for index, (far, member) in enumerate(ROW_LIST[side]):
            row = far - 1 if side == 0 else span - far
            rows_ref[side, index * width : (index + 1) * width, :] = lam_ref[member, :, row, :]
        row = 0 if side == 0 else span - 1
        for field in range(FIELDS):
            start = (HALO + field) * width
            rows_ref[side, start : start + width, :] = fields_ref[field, :, row, :]


def span_shift(value, move, row):
    span = value.shape[0]
    place = lax.broadcasted_iota(jnp.int32, value.shape, 0)
    if move == 1:
        return jnp.where(place == span - 1, row, pltpu.roll(value, span - 1, 0))
    return jnp.where(place == 0, row, pltpu.roll(value, 1, 0))


def roll_z(value, move, edges, walls=None):
    height = value.shape[1]
    if move == 0:
        return value
    shift, edge = (height - 1, edges[1]) if move == 1 else (1, edges[0])
    return jnp.where(edge, 0.0 if walls is None else walls, pltpu.roll(value, shift, 1))


def wall_masks(shape):
    lane = lax.broadcasted_iota(jnp.int32, shape, 1)
    return lane == 0, lane == shape[1] - 1


def gather_mu(source, row_of, plane, edges):
    mu = []
    for member in range(19):
        move_x, move_y, move_z = VELOCITIES[member]
        value = source(plane + move_x, member)
        if value is not None and move_y != 0:
            side = 0 if move_y == 1 else 1
            value = span_shift(value, move_y, row_of(side, plane + move_x, member))
        if move_z != 0:
            walls = source(plane, OPPOSITE[member])
            if value is None:
                value = jnp.where(edges[1 if move_z == 1 else 0], walls, 0.0)
            else:
                value = roll_z(value, move_z, edges, walls)
        mu.append(value)
    return mu


def own_lam(lam_ref):
    def source(plane, member):
        return lam_ref[member, plane] if 0 <= plane < lam_ref.shape[1] else None

    return source


def got_row(rows_ref, width):
    def row_of(side, plane, member):
        place = ROW_LIST[side].index((1, member)) * width + plane
        return rows_ref[side, place : place + 1, :]

    return row_of


def corner_row(face_ref, side, index):
    slot = side * CORNER + index
    return face_ref[10 + slot // 8, slot % 8 : slot % 8 + 1, :]


def far_kernel(thrust_ref, lam_ref, fields_ref, first_ref, coef_ref, out_ref, pop_ref, mu_ref, wall_ref):
    width, span = lam_ref.shape[1], lam_ref.shape[2]
    edges = wall_masks(lam_ref.shape[2:])
    source = own_lam(lam_ref)
    pop_ref[...] = jnp.ones(pop_ref.shape, jnp.float32)

    def write(even):
        x_side, plane, inner, members = (0, 0, 1, X_UP) if even else (1, width - 1, width - 2, X_DOWN)
        inward = SIGNS[x_side]

        def row(side, far, member, at):
            if far == 0:
                last = span - 1 if side == 0 else 0
                return lam_ref[member, at, last : last + 1, :]
            place = (
                ROW_LIST[side].index((far, member))
                if at == plane
                else HALO + NEXT_LIST[x_side][side].index((far, member))
            )
            return first_ref[side, place : place + 1, :]

        def field(side, index):
            place = HALO + len(NEXT_LIST[0][0]) + index
            return first_ref[side, place : place + 1, :]

        def row_of(side, at, member):
            return row(side, 1, member, at)

        for member in range(19):
            move_x, move_y, move_z = VELOCITIES[member]
            for side in range(2):
                same = (member, MIRROR[member])[side]
                wall = (OPPOSITE[member], MIRROR[OPPOSITE[member]])[side]
                pop_ref[member, side : side + 1, :] = field(side, same)
                if move_x != -inward:
                    mu_ref[member, side : side + 1, :] = row(
                        side, 1 + move_y, same, plane if move_x == 0 else inner
                    )
                if move_z != 0:
                    wall_ref[member, side : side + 1, :] = row(side, 1, wall, plane)
        for side in range(2):
            pop_ref[19, side : side + 1, :] = field(side, 19)
        mu = []
        for member in range(19):
            move_x, _, move_z = VELOCITIES[member]
            if move_z == 0:
                mu.append(None if move_x == -inward else mu_ref[member])
            elif move_x == -inward:
                mu.append(jnp.where(edges[1 if move_z == 1 else 0], wall_ref[member], 0.0))
            else:
                mu.append(roll_z(mu_ref[member], move_z, edges, wall_ref[member]))
        coefs = plane_coefs(
            [pop_ref[member] for member in range(19)], turbine_cells(pop_ref[19], thrust_ref)
        )
        corner = VELOCITIES.index((inward, 1, 0))
        corners, _ = plane_adjoint(mu, lambda index: coefs[index], (corner,))
        mu_ref[0] = corners[corner]
        lam, _ = plane_adjoint(
            gather_mu(source, row_of, plane, edges),
            lambda index: coef_ref[index, plane],
            members,
        )
        for index, member in enumerate(members):
            value, move_y = lam_ref[member, plane], VELOCITIES[member][1]
            if move_y != 0:
                value = span_shift(value, move_y, row_of(0 if move_y == 1 else 1, plane, member))
            out_ref[index] = value
            out_ref[5 + index] = lam[member]
        for side, sign in enumerate(SIGNS):
            rows = [row(side, 1 + sign * VELOCITIES[m][1], m, plane) for m in members]
            rows.append(mu_ref[0, side : side + 1, :])
            rows += [field(side, index) for index in range(FIELDS)]
            for index, value in enumerate(rows):
                slot = side * CORNER + index
                out_ref[10 + slot // 8, slot % 8 : slot % 8 + 1, :] = value
        for index in range(FIELDS):
            out_ref[STATIC + index] = fields_ref[index, plane]

    by_parity(write)


def faces_kernel(thrust_ref, lam_ref, fields_ref, rows_ref, coef_ref, near_ref, field_ref, part_ref, pack_ref, low_ref, high_ref):
    width, span = lam_ref.shape[1], lam_ref.shape[2]
    edges = wall_masks(lam_ref.shape[2:])
    source, row_of = own_lam(lam_ref), got_row(rows_ref, width)
    pack_ref[...] = jnp.zeros(pack_ref.shape, jnp.float32)
    field_ref[...] = jnp.zeros(field_ref.shape, jnp.float32)
    for side in range(2):
        for index, (far, member) in enumerate(PACK_LIST[side]):
            if far > 0:
                rows = rows_ref[side, index * width : (index + 1) * width, :]
            else:
                rows = lam_ref[member, :, span - 1 if side == 0 else 0, :]
            pack_ref[side, index, 2 : width + 2, :] = rows
        for field in range(FIELDS):
            start = (HALO + field) * width
            field_ref[side, field, 2 : width + 2, :] = rows_ref[side, start : start + width, :]
    place = lax.broadcasted_iota(jnp.int32, pack_ref.shape[2:], 0)
    inside = jnp.logical_and(place >= 2, place < width + 2)
    pack_edges = wall_masks(pack_ref.shape[2:])
    for side, (sign, wanted) in enumerate(((1, Y_UP), (-1, Y_DOWN))):
        mu = []
        for member in range(19):
            move_x, move_y, move_z = VELOCITIES[member]
            value = pack_ref[side, PACK_LIST[side].index((1 + sign * move_y, member))]
            if move_x != 0:
                value = pltpu.roll(value, (-move_x) % value.shape[0], 0)
            if move_z != 0:
                walls = pack_ref[side, PACK_LIST[side].index((1, OPPOSITE[member]))]
                value = roll_z(value, move_z, pack_edges, walls)
            mu.append(value)
        pops = [field_ref[side, member] for member in range(19)]
        coefs = plane_coefs(pops, turbine_cells(field_ref[side, 19], thrust_ref))
        lam, _ = plane_adjoint(mu, lambda index: coefs[index], wanted)
        for index, member in enumerate(wanted):
            part_ref[side, index] = jnp.where(inside, lam[member], 0.0)
    for out_ref, plane, members in ((low_ref, 0, X_UP), (high_ref, width - 1, X_DOWN)):
        lam, _ = plane_adjoint(
            gather_mu(source, row_of, plane, edges),
            lambda index: coef_ref[index, plane],
            members,
        )
        for index, member in enumerate(members):
            value, move_y = lam_ref[member, plane], VELOCITIES[member][1]
            if move_y != 0:
                value = span_shift(value, move_y, row_of(0 if move_y == 1 else 1, plane, member))
            out_ref[index] = value
            out_ref[5 + index] = lam[member]
        for side, (sign, wanted) in enumerate(((1, Y_UP), (-1, Y_DOWN))):
            sources = [
                pack_ref.at[side, PACK_LIST[side].index((1 + sign * VELOCITIES[member][1], member))]
                for member in members
            ]
            corner = VELOCITIES.index((VELOCITIES[members[0]][0], sign, 0))
            sources.append(part_ref.at[side, wanted.index(corner)])
            sources += [field_ref.at[side, field] for field in range(FIELDS)]
            for index, ref in enumerate(sources):
                slot = side * CORNER + index
                out_ref[10 + slot // 8, slot % 8 : slot % 8 + 1, :] = ref[plane + 2 : plane + 3, :]

    def write(even):
        near_ref[0:STATIC] = (high_ref if even else low_ref)[0:STATIC]
        for index in range(FIELDS):
            near_ref[STATIC + index] = fields_ref[index, width - 1 if even else 0]

    by_parity(write)


def middle_kernel(lam_ref, rows_ref, coef_ref, mid_ref, cell_ref):
    width = lam_ref.shape[1]
    edges = wall_masks(lam_ref.shape[2:])
    source, row_of = own_lam(lam_ref), got_row(rows_ref, width)
    for plane in range(width):
        mu = gather_mu(source, row_of, plane, edges)
        lam, mx = plane_adjoint(mu, lambda index: coef_ref[index, plane])
        for member in range(19):
            mid_ref[member, plane] = lam[member]
        cell_ref[plane] = mx * coef_ref[GAIN, plane]


def pair_kernel(turbines, thrust_ref, lam_ref, rows_ref, near_ref, far_ref, late_ref, early_ref, fields_ref,
                part_mid_ref, part_cell_ref, part_edge_ref, pack_ref,
                out_ref, next_ref, mid_ref, edge_ref, line_ref, above_ref, below_ref, part_face_ref):
    width, span, height = lam_ref.shape[1:]
    take_in(near_ref, far_ref, above_ref, below_ref)
    edges = wall_masks((span, height))
    pack_shape = pack_ref.shape[2:]
    pack_edges = wall_masks(pack_shape)
    place = lax.broadcasted_iota(jnp.int32, pack_shape, 0)
    totals = [part_cell_ref[plane] for plane in range(width)]
    for face_ref, plane, members in ((above_ref, width - 1, X_UP), (below_ref, 0, X_DOWN)):
        mu = [None] * 19
        for index, member in enumerate(members):
            mu[member] = roll_z(face_ref[index], VELOCITIES[member][2], edges)
        lam, mx = plane_adjoint(mu, lambda index: late_ref[index, plane])
        for member in range(19):
            mid_ref[member, 0 if plane == 0 else 1] = part_mid_ref[member, plane] + lam[member]
        totals[plane] = totals[plane] + mx * late_ref[GAIN, plane]

    for side, (static_ref, plane, members, wanted) in enumerate(
        ((above_ref, width - 1, X_DOWN, X_UP), (below_ref, 0, X_UP, X_DOWN))
    ):
        mu = [None] * 19
        for member in members:
            value, (_, move_y, move_z) = lam_ref[member, plane], VELOCITIES[member]
            if move_y != 0:
                value = span_shift(value, move_y, got_row(rows_ref, width)(0 if move_y == 1 else 1, plane, member))
            mu[member] = roll_z(value, move_z, edges)
        pops = [static_ref[STATIC + member] for member in range(19)]
        coefs = plane_coefs(pops, turbine_cells(static_ref[STATIC + 19], thrust_ref))
        lam, _ = plane_adjoint(mu, lambda index: coefs[index], wanted)
        for index, member in enumerate(wanted):
            part_face_ref[side, index] = lam[member]

    def beyond(below, above, rest):
        return jnp.where(place == 1, below, jnp.where(place == width + 2, above, rest))

    halo_tiles = []
    for side, (sign, wanted) in enumerate(((1, Y_UP), (-1, Y_DOWN))):
        mu = [None] * 19
        for members, got_ref, got_place, own_place in (
            (X_UP, above_ref, width + 1, 1),
            (X_DOWN, below_ref, 2, width + 2),
        ):
            plane = 0 if own_place == 1 else width - 1
            for index, member in enumerate(members):
                far = 1 + sign * VELOCITIES[member][1]
                if far > 0:
                    start = ROW_LIST[side].index((far, member)) * width + plane
                    own = rows_ref[side, start : start + 1, :]
                else:
                    inner = span - 1 if side == 0 else 0
                    own = lam_ref[member, plane, inner : inner + 1, :]
                value = jnp.where(
                    place == got_place,
                    corner_row(got_ref, side, index),
                    jnp.where(place == own_place, own, 0.0),
                )
                mu[member] = roll_z(value, VELOCITIES[member][2], pack_edges)
        fields = [
            beyond(
                corner_row(below_ref, side, 6 + field),
                corner_row(above_ref, side, 6 + field),
                pack_ref[side, field],
            )
            for field in range(FIELDS)
        ]
        coefs = plane_coefs(fields[:19], turbine_cells(fields[19], thrust_ref))
        lam, _ = plane_adjoint(mu, lambda index: coefs[index], wanted)
        for index, member in enumerate(wanted):
            value = part_edge_ref[side, index] + lam[member]
            if VELOCITIES[member][0] == 1:
                value = value + jnp.where(place == width + 2, corner_row(above_ref, side, 5), 0.0)
            elif VELOCITIES[member][0] == -1:
                value = value + jnp.where(place == 1, corner_row(below_ref, side, 5), 0.0)
            edge_ref[side, index] = value
        halo_tiles.append((fields[20], fields[19]))

    def middle(plane, member):
        if plane >= width:
            index = X_UP.index(member)
            return above_ref[5 + index] + part_face_ref[0, index]
        if plane < 0:
            index = X_DOWN.index(member)
            return below_ref[5 + index] + part_face_ref[1, index]
        if plane in (0, width - 1):
            return mid_ref[member, 0 if plane == 0 else 1]
        return part_mid_ref[member, plane]

    def middle_row(side, plane, member):
        index = (Y_UP, Y_DOWN)[side].index(member)
        return edge_ref[side, index, plane + 2 : plane + 3, :]

    for plane in range(width):
        mu = gather_mu(middle, middle_row, plane, edges)
        lam, mx = plane_adjoint(mu, lambda index: early_ref[index, plane])
        for member in range(19):
            out_ref[member, plane] = lam[member]
        totals[plane] = totals[plane] + mx * early_ref[GAIN, plane]

    for side, (members, row) in enumerate(((Y_UP, 0), (Y_DOWN, span - 1))):
        for index, member in enumerate(members):
            start = (5 * side + index) * width
            next_ref[start : start + width, :] = out_ref[member, :, row, :]

    nothing = jnp.zeros((1, height), jnp.float32)
    up, down = [], []
    for plane in range(width):
        up.append(
            2.0 * out_ref[1, plane]
            + span_shift(out_ref[7, plane], 1, nothing)
            + span_shift(out_ref[9, plane], -1, nothing)
            + roll_z(out_ref[11, plane], 1, edges)
            + roll_z(out_ref[13, plane], -1, edges)
        )
        down.append(
            2.0 * out_ref[2, plane]
            + span_shift(out_ref[8, plane], -1, nothing)
            + span_shift(out_ref[10, plane], 1, nothing)
            + roll_z(out_ref[12, plane], -1, edges)
            + roll_z(out_ref[14, plane], 1, edges)
        )
    tiles = []
    for plane in range(-1, width + 1):
        value = None
        if plane + 1 < width:
            value = up[plane + 1]
        if plane >= 1:
            value = -down[plane - 1] if value is None else value - down[plane - 1]
        if plane < 0 or plane >= width:
            face_ref = below_ref if plane < 0 else above_ref
            tiles.append((face_ref[STATIC + 20] * value, face_ref[STATIC + 19]))
            continue
        value = value + jnp.where(edges[1], out_ref[12, plane] - out_ref[13, plane], 0.0)
        value = value + jnp.where(edges[0], out_ref[14, plane] - out_ref[11, plane], 0.0)
        tiles.append((totals[plane] + fields_ref[20, plane] * value, fields_ref[19, plane]))
    line_ref[...] = jnp.zeros(line_ref.shape, jnp.float32)
    for side, (upward, downward, row) in enumerate(((9, 8, span - 1), (7, 10, 0))):
        line_ref[side, 0, 1 : width + 1, :] = out_ref[upward, :, row, :]
        line_ref[side, 1, 3 : width + 3, :] = out_ref[downward, :, row, :]
        gain, ids = halo_tiles[side]
        tiles.append(((line_ref[side, 0] - line_ref[side, 1]) * gain, ids))
    start = 10 * width
    next_ref[start:, :] = jnp.zeros((next_ref.shape[0] - start, height), jnp.float32)
    for turbine in range(turbines):
        row = None
        for value, ids in tiles:
            kept = jnp.sum(jnp.where(ids == float(turbine), value, 0.0), axis=0, keepdims=True)
            row = kept if row is None else row + kept
        next_ref[start + turbine : start + turbine + 1, :] = row


def last_faces_kernel(lam_ref, rows_ref, sums_ref, got_ref, near_ref, far_ref, total_ref):
    width = lam_ref.shape[1]

    def row_of(side, plane, member):
        place = (5 * side + (Y_UP, Y_DOWN)[side].index(member)) * width + plane
        return rows_ref[place : place + 1, :]

    def moved(members, plane):
        def tile(index):
            member = members[index]
            value, move_y = lam_ref[member, plane], VELOCITIES[member][1]
            if move_y == 0:
                return value
            return span_shift(value, move_y, row_of(0 if move_y == 1 else 1, plane, member))

        return tile

    total_ref[...] = sums_ref[...] + got_ref[...]
    far_ref[5:] = jnp.zeros((far_ref.shape[0] - 5,) + far_ref.shape[1:], jnp.float32)
    hand_out(moved(X_UP, 0), moved(X_DOWN, width - 1), near_ref, far_ref.at[0:5])


def last_kernel(lam_ref, rows_ref, near_ref, far_ref, coef_ref, out_ref):
    width, span, height = lam_ref.shape[1:]
    lane = lax.broadcasted_iota(jnp.int32, (span, height), 1)
    first, last = lane == 0, lane == height - 1
    odd = jnp.full((span, height), lax.rem(lax.axis_index("gx"), 2)) == 1

    def source(plane, member):
        if plane >= width:
            index = X_UP.index(member)
            return jnp.where(odd, far_ref[index], near_ref[index])
        if plane < 0:
            index = X_DOWN.index(member)
            return jnp.where(odd, near_ref[index], far_ref[index])
        value, move_y = lam_ref[member, plane], VELOCITIES[member][1]
        if move_y == 0:
            return value
        side = 0 if move_y == 1 else 1
        place = (5 * side + (Y_UP, Y_DOWN)[side].index(member)) * width + plane
        return span_shift(value, move_y, rows_ref[place : place + 1, :])

    for plane in range(width):
        mu = []
        for member in range(19):
            move_x, _, move_z = VELOCITIES[member]
            value = source(plane + move_x, member)
            if move_z == 1:
                value = jnp.where(
                    last, lam_ref[OPPOSITE[member], plane], pltpu.roll(value, height - 1, 1)
                )
            elif move_z == -1:
                value = jnp.where(first, lam_ref[OPPOSITE[member], plane], pltpu.roll(value, 1, 1))
            mu.append(value)
        lam, _ = plane_adjoint(mu, lambda index: coef_ref[index, plane])
        for member in range(19):
            out_ref[member, plane] = lam[member]


def call(kernel, outs, *args, scratch=(), micros=1):
    return pl.pallas_call(
        kernel,
        out_shape=tuple(jax.ShapeDtypeStruct(shape, jnp.float32) for shape in outs),
        in_specs=[pl.BlockSpec(memory_space=VMEM)] * len(args),
        out_specs=tuple(pl.BlockSpec(memory_space=VMEM) for _ in outs),
        scratch_shapes=[pltpu.VMEM(shape, jnp.float32) for shape in scratch],
        cost_estimate=pl.CostEstimate(
            flops=int(1e6 * micros), bytes_accessed=int(2e6 * micros), transcendentals=0
        ),
        compiler_params=pltpu.CompilerParams(vmem_limit_bytes=32 * 1024 * 1024),
    )(*args)


def ring(axis, step):
    count = lax.axis_size(axis)
    return [(i, (i + step) % count) for i in range(count)]


def swap_rows(rows):
    if lax.axis_size("gy") == 2:
        return lax.ppermute(rows, "gy", ring("gy", 1))
    return jnp.stack(
        [
            lax.ppermute(rows[0], "gy", ring("gy", -1)),
            lax.ppermute(rows[1], "gy", ring("gy", 1)),
        ]
    )


def swap_near(near):
    count = lax.axis_size("gx")
    assert count % 2 == 0
    return lax.ppermute(near, "gx", [(i, i ^ 1) for i in range(count)])


def swap_far(far):
    count = lax.axis_size("gx")
    return lax.ppermute(
        far, "gx", [(i, (i + 1 if i % 2 else i - 1) % count) for i in range(count)]
    )


def flips(value, axis, flip_list):
    count = lax.axis_size(axis)
    parts = [lax.ppermute(value, axis, [(i, i ^ flip) for i in range(count)]) for flip in flip_list]
    return sum(parts, value)


def sum_bits(value, axis, start):
    count = lax.axis_size(axis)
    while start < count:
        stop = min(4 * start, count)
        value = flips(value, axis, range(start, stop, start))
        start = stop
    return value


def last_exchange(lam, packed):
    width, height = lam.shape[1], lam.shape[3]
    rows_count = 10 * width
    sums = packed[rows_count:]
    if lax.axis_size("gy") == 2:
        got = lax.ppermute(packed, "gy", ring("gy", 1))
        rows, got = got[:rows_count], got[rows_count:]
    else:
        rows = swap_rows(packed[:rows_count].reshape(2, rows_count // 2, -1))
        rows = rows.reshape(rows_count, -1)
        count = lax.axis_size("gy")
        got = (lax.psum(sums, "gy") if count & (count - 1) else sum_bits(sums, "gy", 1)) - sums
    near, far, sums = call(
        last_faces_kernel,
        [(5, lam.shape[2], height), (6, lam.shape[2], height), sums.shape],
        lam,
        rows,
        sums,
        got,
        micros=0.1,
    )
    count = lax.axis_size("gx")
    apart = count & (count - 1) == 0 and count > 2
    if apart:
        sums = flips(sums, "gx", [2])
    got_near, got_far = swap_near(near), swap_far(far)
    if apart:
        sums = sum_bits(flips(sums, "gx", [1]), "gx", 4)
    else:
        sums = lax.psum(sums, "gx")
    return rows, got_near, got_far, sums


def shards(fwd_pops, fwd_scale, seed_adjoint, turbine_map, thrust):
    steps, _, width, span, height = fwd_pops.shape
    assert steps == 3 and span == 8
    turbines = thrust.shape[0]
    turbine_rows = -(-turbines // 8) * 8
    sublanes = -(-(width + 4) // 8) * 8
    whole = (19, width, span, height)
    (begun,) = call(start_kernel, [(8, height)], micros=400)
    fields, first, thrust_rows, slope_rows = call(
        pack_kernel,
        [
            (FIELDS, width, span, height),
            (2, FIRST_ROWS, height),
            (turbine_rows, height),
            (turbine_rows, height),
        ],
        begun,
        thrust.reshape(1, turbines),
        turbine_map,
        fwd_scale,
        fwd_pops,
        seed_adjoint,
        micros=0.6,
    )
    first = swap_rows(first)
    coefs = call(
        coef_kernel,
        [(COEFS, width, span, height)] * steps,
        thrust_rows,
        turbine_map,
        fwd_scale,
        fwd_pops,
        micros=0.8,
    )
    (rows,) = call(
        rows_kernel,
        [(2, (HALO + FIELDS) * width, height)],
        seed_adjoint,
        fields,
        coefs[2],
        micros=0.1,
    )
    rows = swap_rows(rows)
    face, edge = (FACE_TILES, span, height), (2, 5, sublanes, height)
    tile = (19, span, height)
    (far,) = call(
        far_kernel,
        [face],
        thrust_rows,
        seed_adjoint,
        fields,
        first,
        coefs[2],
        scratch=[(20, span, height), tile, tile],
        micros=2000,
    )
    far = swap_far(far)
    near, pack, part_edge = call(
        faces_kernel,
        [face, (2, FIELDS, sublanes, height), edge],
        thrust_rows,
        seed_adjoint,
        fields,
        rows,
        coefs[2],
        scratch=[(2, len(PACK_LIST[0]), sublanes, height), face, face],
        micros=0.4,
    )
    near = swap_near(near)
    parts = call(
        middle_kernel,
        [whole, (width, span, height)],
        seed_adjoint,
        rows,
        coefs[2],
        micros=0.6,
    )
    lam, packed = call(
        lambda *refs: pair_kernel(turbines, *refs),
        [whole, (10 * width + turbine_rows, height)],
        thrust_rows,
        seed_adjoint,
        rows,
        near,
        far,
        coefs[2],
        coefs[1],
        fields,
        *parts,
        part_edge,
        pack,
        scratch=[
            (19, 2, span, height),
            edge,
            (2, 2, sublanes, height),
            face,
            face,
            (2, 5, span, height),
        ],
        micros=0.8,
    )
    rows, near, far, sums = last_exchange(lam, packed)
    (lam,) = call(last_kernel, [whole], lam, rows, near, far, coefs[0], micros=0.5)
    thrust_grad = jnp.sum((slope_rows * sums)[:turbines], axis=1)
    return (lam, thrust_grad)


def solution(mesh):
    placed = (
        P(None, None, "gx", "gy", None),
        P(None, "gx", "gy", None),
        P(None, "gx", "gy", None),
        P("gx", "gy", None),
        P(),
    )
    return jax.shard_map(
        shards,
        mesh=mesh,
        in_specs=placed,
        out_specs=(P(None, "gx", "gy", None), P()),
        check_vma=False,
    )
```

```python
import jax
import jax.numpy as jnp
from jax import lax
from jax.experimental import pallas as pl
from jax.experimental.pallas import tpu as pltpu
from jax.sharding import PartitionSpec as P

VELOCITIES = (
    (0, 0, 0),
    (1, 0, 0),
    (-1, 0, 0),
    (0, 1, 0),
    (0, -1, 0),
    (0, 0, 1),
    (0, 0, -1),
    (1, 1, 0),
    (-1, -1, 0),
    (1, -1, 0),
    (-1, 1, 0),
    (1, 0, 1),
    (-1, 0, -1),
    (1, 0, -1),
    (-1, 0, 1),
    (0, 1, 1),
    (0, -1, -1),
    (0, 1, -1),
    (0, -1, 1),
)
OPPOSITE = (0, 2, 1, 4, 3, 6, 5, 8, 7, 10, 9, 12, 11, 14, 13, 16, 15, 18, 17)
WEIGHTS = tuple([1.0 / 3.0] + [1.0 / 18.0] * 6 + [1.0 / 36.0] * 12)
MEAN_FLOW = 0.1
TAU_BASE = 0.51
SMAG_COEF = 18.0 * 1.4142135623730951 * 0.17 * 0.17
QUAD_FLOOR = 0.0001

X_UP = (1, 7, 9, 11, 13)
X_DOWN = (2, 8, 10, 12, 14)
Y_UP = (3, 7, 10, 15, 17)
Y_DOWN = (4, 8, 9, 16, 18)

KEEP, MASS, FLUX, UX, UY, UZ, Q1 = 19, 20, 21, 22, 23, 24, 25
RATE, BULK, PX, PY, PZ, DRAG, DRAG_U, GAIN = 34, 35, 36, 37, 38, 39, 40, 41
COEFS = 42

FIELDS = 21

VMEM = pltpu.VMEM


def halo_list(axis, sign):
    near = [
        (1, m) for m in range(19) if VELOCITIES[m][axis] * sign >= 0 or VELOCITIES[m][2] != 0
    ]
    return near + [(2, m) for m in range(19) if VELOCITIES[m][axis] * sign == 1]


SIGNS = (1, -1)
ROW_LIST = [halo_list(1, sign) for sign in SIGNS]
INNER_LIST = [[(0, m) for m in range(19) if VELOCITIES[m][1] * sign == -1] for sign in SIGNS]
PACK_LIST = [ROW_LIST[side] + INNER_LIST[side] for side in range(2)]
HALO = len(ROW_LIST[0])
CORNER = 6 + FIELDS
NEXT_LIST = [
    [[(far, m) for far, m in ROW_LIST[y] if VELOCITIES[m][0] == sign] for y in range(2)]
    for sign in SIGNS
]
FIRST_ROWS = -(-(HALO + len(NEXT_LIST[0][0]) + FIELDS) // 8) * 8
MIRROR = [VELOCITIES.index((a, -b, c)) for a, b, c in VELOCITIES]
STATIC = 10 + -(-2 * CORNER // 8)
FACE_TILES = STATIC + FIELDS


def base_values():
    values = []
    for member in range(19):
        along = float(VELOCITIES[member][0])
        values.append(
            WEIGHTS[member]
            * (
                1.0
                + 3.0 * MEAN_FLOW * along
                + 4.5 * MEAN_FLOW * MEAN_FLOW * along * along
                - 1.5 * MEAN_FLOW * MEAN_FLOW
            )
        )
    return values


def plane_coefs(pops, thrust_cell):
    rho = pops[0]
    for member in range(1, 19):
        rho = rho + pops[member]
    inv_rho = 1.0 / rho
    vel = []
    for axis_id in range(3):
        moment = None
        for member in range(19):
            component = VELOCITIES[member][axis_id]
            if component == 1:
                moment = pops[member] if moment is None else moment + pops[member]
            elif component == -1:
                moment = moment - pops[member]
        vel.append(moment * inv_rho)
    ux, uy, uz = vel
    speed_sq = ux * ux + uy * uy + uz * uz
    rest = 1.0 - 1.5 * speed_sq
    part = []
    for member in range(19):
        if member == 0:
            part.append(pops[0] - (WEIGHTS[0] * rho) * rest)
            continue
        proj = None
        for axis_id in range(3):
            component = VELOCITIES[member][axis_id]
            if component == 1:
                proj = vel[axis_id] if proj is None else proj + vel[axis_id]
            elif component == -1:
                proj = -vel[axis_id] if proj is None else proj - vel[axis_id]
        part.append(pops[member] - (WEIGHTS[member] * rho) * (rest + 3.0 * proj + 4.5 * proj * proj))

    def pair(member):
        return part[member] + part[member + 1]

    in_xy, in_xz, in_yz = pair(7) + pair(9), pair(11) + pair(13), pair(15) + pair(17)
    pxx, pyy, pzz = pair(1) + in_xy + in_xz, pair(3) + in_xy + in_yz, pair(5) + in_xz + in_yz
    pxy, pxz, pyz = pair(7) - pair(9), pair(11) - pair(13), pair(15) - pair(17)
    square = (
        pxx * pxx + pyy * pyy + pzz * pzz + 2.0 * (pxy * pxy + pxz * pxz + pyz * pyz) + QUAD_FLOOR
    )
    size = jnp.sqrt(square)
    root = jnp.sqrt(TAU_BASE * TAU_BASE + SMAG_COEF * size * inv_rho)
    omega = 1.0 / (0.5 * (TAU_BASE + root))
    pux = pxx * ux + pxy * uy + pxz * uz
    puy = pxy * ux + pyy * uy + pyz * uz
    puz = pxz * ux + pyz * uy + pzz * uz
    flux = omega * (3.0 / 36.0)
    drag = (3.0 / 36.0) * thrust_cell * jnp.abs(ux) * inv_rho
    result = list(part)
    result.append(1.0 - omega)
    result.append((omega * (1.0 / 36.0)) * (1.0 + 1.5 * speed_sq))
    result.append(flux)
    result.extend(vel)
    result.extend((pxx, pyy, pzz))
    result.extend((pxx + pyy + 2.0 * pxy, pxx + pyy - 2.0 * pxy))
    result.extend((pxx + pzz + 2.0 * pxz, pxx + pzz - 2.0 * pxz))
    result.extend((pyy + pzz + 2.0 * pyz, pyy + pzz - 2.0 * pyz))
    result.append((0.25 * SMAG_COEF) * omega * omega * inv_rho / (root * size))
    result.append(
        (pux * ux + puy * uy + puz * uz) - (pxx + pyy + pzz) * (1.0 / 3.0) - square * inv_rho
    )
    result.extend((-2.0 * pux, -2.0 * puy, -2.0 * puz))
    result.append(drag)
    result.append(drag * ux)
    result.append((-1.5 / 36.0) * ux * jnp.abs(ux))
    return result


def plus(*values):
    kept = [value for value in values if value is not None]
    return sum(kept[1:], kept[0]) if kept else None


def minus(left, right):
    if right is None:
        return left
    return -right if left is None else left - right


def times(left, right):
    return None if left is None or right is None else left * right


def plane_adjoint(mu, coef, wanted=range(19)):
    total, diff = {}, {}
    for member in range(1, 19, 2):
        total[member] = plus(mu[member], mu[member + 1])
        diff[member] = minus(mu[member], mu[member + 1])
    two_x, two_y, two_z = times(total[1], 2.0), times(total[3], 2.0), times(total[5], 2.0)
    in_xy, in_xz = plus(total[7], total[9]), plus(total[11], total[13])
    in_yz = plus(total[15], total[17])
    mxx, myy, mzz = plus(two_x, in_xy, in_xz), plus(two_y, in_xy, in_yz), plus(two_z, in_xz, in_yz)
    mxy, mxz = minus(total[7], total[9]), minus(total[11], total[13])
    myz = minus(total[15], total[17])
    m0 = plus(times(mu[0], 12.0), plus(two_x, two_y, two_z), plus(in_xy, in_xz, in_yz))
    mx = plus(times(diff[1], 2.0), plus(diff[7], diff[9]), plus(diff[11], diff[13]))
    my = plus(times(diff[3], 2.0), minus(diff[7], diff[9]), plus(diff[15], diff[17]))
    mz = plus(times(diff[5], 2.0), minus(diff[11], diff[13]), minus(diff[15], diff[17]))
    ux, uy, uz = coef(UX), coef(UY), coef(UZ)
    vx = plus(times(mxx, ux), times(mxy, uy), times(mxz, uz))
    vy = plus(times(mxy, ux), times(myy, uy), times(myz, uz))
    vz = plus(times(mxz, ux), times(myz, uy), times(mzz, uz))
    along = [mu[member] * coef(member) for member in range(19) if mu[member] is not None]
    while len(along) > 1:
        along = [
            along[k] + along[k + 1] if k + 1 < len(along) else along[k]
            for k in range(0, len(along), 2)
        ]
    gamma = along[0] * coef(RATE)
    flux = coef(FLUX)
    alpha = (
        coef(MASS) * m0
        - 1.5 * flux * (vx * ux + vy * uy + vz * uz)
        + gamma * coef(BULK)
        + mx * coef(DRAG_U)
    )
    beta_x = flux * (plus(mx, 3.0 * vx) - ux * m0) + gamma * coef(PX) - mx * coef(DRAG)
    beta_y = flux * (plus(my, 3.0 * vy) - uy * m0) + gamma * coef(PY)
    beta_z = flux * (plus(mz, 3.0 * vz) - uz * m0) + gamma * coef(PZ)
    keep = coef(KEEP)
    odd = {
        1: beta_x,
        3: beta_y,
        5: beta_z,
        7: beta_x + beta_y,
        9: beta_x - beta_y,
        11: beta_x + beta_z,
        13: beta_x - beta_z,
        15: beta_y + beta_z,
        17: beta_y - beta_z,
    }
    result = {}
    for member in wanted:
        if member == 0:
            result[0] = plus(times(mu[0], keep), alpha)
            continue
        forward = member - 1 + member % 2
        even = alpha + gamma * coef(Q1 + forward // 2)
        rest = even + odd[forward] if member == forward else even - odd[forward]
        result[member] = plus(times(mu[member], keep), rest)
    return result, mx


def turbine_cells(ids, thrust_ref):
    ratio = jnp.zeros(ids.shape, jnp.float32)
    for turbine in range(thrust_ref.shape[0]):
        row = thrust_ref[turbine : turbine + 1, :]
        ratio = jnp.where(ids == jnp.asarray(turbine, ids.dtype), row, ratio)
    return jnp.where(ids >= 0, local_thrust(ratio), 0.0)


def local_thrust(values):
    return 4.0 * values / jnp.square(1.0 + jnp.sqrt(1.0 - values))


def decode(scale_ref, pops_ref, instant, plane):
    base = base_values()
    scale = scale_ref[instant, plane]
    return [
        base[member] * (1.0 + scale * pops_ref[instant, member, plane].astype(jnp.float32))
        for member in range(19)
    ]


def coef_kernel(thrust_ref, map_ref, scale_ref, pops_ref, *out_refs):
    for plane in range(pops_ref.shape[2]):
        thrust_cell = turbine_cells(map_ref[plane], thrust_ref)
        for instant, out_ref in enumerate(out_refs):
            pops = decode(scale_ref, pops_ref, instant, plane)
            for index, value in enumerate(plane_coefs(pops, thrust_cell)):
                out_ref[index, plane] = value


def by_parity(even):
    odd = lax.rem(lax.axis_index("gx"), 2) == 1
    pl.when(jnp.logical_not(odd))(lambda: even(True))
    pl.when(odd)(lambda: even(False))


def hand_out(low, high, near_ref, far_ref):
    def write(even):
        for source, out_ref in ((low, far_ref), (high, near_ref)) if even else ((low, near_ref), (high, far_ref)):
            for index in range(out_ref.shape[0]):
                out_ref[index] = source(index)

    by_parity(write)


def take_in(near_ref, far_ref, above_ref, below_ref):
    def write(even):
        for source, out_ref in ((near_ref, above_ref if even else below_ref), (far_ref, below_ref if even else above_ref)):
            for index in range(out_ref.shape[0]):
                out_ref[index] = source[index]

    by_parity(write)


def start_kernel(out_ref):
    out_ref[...] = jnp.zeros(out_ref.shape, jnp.float32)


def write_thrust(thrust_ref, thrust_rows_ref, slope_rows_ref):
    thrust_rows_ref[...] = jnp.zeros(thrust_rows_ref.shape, jnp.float32)
    for turbine in range(thrust_ref.shape[1]):
        thrust_rows_ref[turbine : turbine + 1, :] = jnp.broadcast_to(
            thrust_ref[0:1, turbine : turbine + 1], (1, thrust_rows_ref.shape[1])
        )
    root = jnp.sqrt(1.0 - thrust_rows_ref[...])
    slope_rows_ref[...] = 4.0 / (root * jnp.square(1.0 + root))


def pack_kernel(_, thrust_ref, map_ref, scale_ref, pops_ref, lam_ref, fields_ref, first_ref, thrust_rows_ref, slope_rows_ref):
    width, span = lam_ref.shape[1], lam_ref.shape[2]
    write_thrust(thrust_ref, thrust_rows_ref, slope_rows_ref)
    last = pops_ref.shape[0] - 1
    for plane in range(width):
        for index, value in enumerate(decode(scale_ref, pops_ref, last, plane)):
            fields_ref[index, plane] = value
        fields_ref[19, plane] = map_ref[plane].astype(jnp.float32)
        pops = decode(scale_ref, pops_ref, 0, plane)
        rho, momentum = pops[0], None
        for member in range(1, 19):
            rho = rho + pops[member]
        for member in X_UP:
            pair = pops[member] - pops[member + 1]
            momentum = pair if momentum is None else momentum + pair
        ux = momentum / rho
        fields_ref[20, plane] = (-1.5 / 36.0) * ux * jnp.abs(ux)
    first_ref[...] = jnp.zeros(first_ref.shape, jnp.float32)

    def write(even):
        plane, inner = (0, 1) if even else (width - 1, width - 2)
        for side in range(2):
            picks = [(lam_ref, m, plane, far) for far, m in ROW_LIST[side]]
            picks += [(lam_ref, m, inner, far) for far, m in NEXT_LIST[0 if even else 1][side]]
            picks += [(fields_ref, field, plane, 1) for field in range(FIELDS)]
            for index, (ref, member, at, far) in enumerate(picks):
                row = far - 1 if side == 0 else span - far
                first_ref[side, index : index + 1, :] = ref[member, at, row : row + 1, :]

    by_parity(write)


def rows_kernel(lam_ref, fields_ref, _, rows_ref):
    width, span = lam_ref.shape[1], lam_ref.shape[2]
    for side in range(2):
        for index, (far, member) in enumerate(ROW_LIST[side]):
            row = far - 1 if side == 0 else span - far
            rows_ref[side, index * width : (index + 1) * width, :] = lam_ref[member, :, row, :]
        row = 0 if side == 0 else span - 1
        for field in range(FIELDS):
            start = (HALO + field) * width
            rows_ref[side, start : start + width, :] = fields_ref[field, :, row, :]


def span_shift(value, move, row):
    span = value.shape[0]
    place = lax.broadcasted_iota(jnp.int32, value.shape, 0)
    if move == 1:
        return jnp.where(place == span - 1, row, pltpu.roll(value, span - 1, 0))
    return jnp.where(place == 0, row, pltpu.roll(value, 1, 0))


def roll_z(value, move, edges, walls=None):
    height = value.shape[1]
    if move == 0:
        return value
    shift, edge = (height - 1, edges[1]) if move == 1 else (1, edges[0])
    return jnp.where(edge, 0.0 if walls is None else walls, pltpu.roll(value, shift, 1))


def wall_masks(shape):
    lane = lax.broadcasted_iota(jnp.int32, shape, 1)
    return lane == 0, lane == shape[1] - 1


def gather_mu(source, row_of, plane, edges):
    mu = []
    for member in range(19):
        move_x, move_y, move_z = VELOCITIES[member]
        value = source(plane + move_x, member)
        if value is not None and move_y != 0:
            side = 0 if move_y == 1 else 1
            value = span_shift(value, move_y, row_of(side, plane + move_x, member))
        if move_z != 0:
            walls = source(plane, OPPOSITE[member])
            if value is None:
                value = jnp.where(edges[1 if move_z == 1 else 0], walls, 0.0)
            else:
                value = roll_z(value, move_z, edges, walls)
        mu.append(value)
    return mu


def own_lam(lam_ref):
    def source(plane, member):
        return lam_ref[member, plane] if 0 <= plane < lam_ref.shape[1] else None

    return source


def got_row(rows_ref, width):
    def row_of(side, plane, member):
        place = ROW_LIST[side].index((1, member)) * width + plane
        return rows_ref[side, place : place + 1, :]

    return row_of


def corner_row(face_ref, side, index):
    slot = side * CORNER + index
    return face_ref[10 + slot // 8, slot % 8 : slot % 8 + 1, :]


def far_kernel(thrust_ref, lam_ref, fields_ref, first_ref, coef_ref, out_ref, pop_ref, mu_ref, wall_ref):
    width, span = lam_ref.shape[1], lam_ref.shape[2]
    edges = wall_masks(lam_ref.shape[2:])
    source = own_lam(lam_ref)
    pop_ref[...] = jnp.ones(pop_ref.shape, jnp.float32)

    def write(even):
        x_side, plane, inner, members = (0, 0, 1, X_UP) if even else (1, width - 1, width - 2, X_DOWN)
        inward = SIGNS[x_side]

        def row(side, far, member, at):
            if far == 0:
                last = span - 1 if side == 0 else 0
                return lam_ref[member, at, last : last + 1, :]
            place = (
                ROW_LIST[side].index((far, member))
                if at == plane
                else HALO + NEXT_LIST[x_side][side].index((far, member))
            )
            return first_ref[side, place : place + 1, :]

        def field(side, index):
            place = HALO + len(NEXT_LIST[0][0]) + index
            return first_ref[side, place : place + 1, :]

        def row_of(side, at, member):
            return row(side, 1, member, at)

        for member in range(19):
            move_x, move_y, move_z = VELOCITIES[member]
            for side in range(2):
                same = (member, MIRROR[member])[side]
                wall = (OPPOSITE[member], MIRROR[OPPOSITE[member]])[side]
                pop_ref[member, side : side + 1, :] = field(side, same)
                if move_x != -inward:
                    mu_ref[member, side : side + 1, :] = row(
                        side, 1 + move_y, same, plane if move_x == 0 else inner
                    )
                if move_z != 0:
                    wall_ref[member, side : side + 1, :] = row(side, 1, wall, plane)
        for side in range(2):
            pop_ref[19, side : side + 1, :] = field(side, 19)
        mu = []
        for member in range(19):
            move_x, _, move_z = VELOCITIES[member]
            if move_z == 0:
                mu.append(None if move_x == -inward else mu_ref[member])
            elif move_x == -inward:
                mu.append(jnp.where(edges[1 if move_z == 1 else 0], wall_ref[member], 0.0))
            else:
                mu.append(roll_z(mu_ref[member], move_z, edges, wall_ref[member]))
        coefs = plane_coefs(
            [pop_ref[member] for member in range(19)], turbine_cells(pop_ref[19], thrust_ref)
        )
        corner = VELOCITIES.index((inward, 1, 0))
        corners, _ = plane_adjoint(mu, lambda index: coefs[index], (corner,))
        mu_ref[0] = corners[corner]
        lam, _ = plane_adjoint(
            gather_mu(source, row_of, plane, edges),
            lambda index: coef_ref[index, plane],
            members,
        )
        for index, member in enumerate(members):
            value, move_y = lam_ref[member, plane], VELOCITIES[member][1]
            if move_y != 0:
                value = span_shift(value, move_y, row_of(0 if move_y == 1 else 1, plane, member))
            out_ref[index] = value
            out_ref[5 + index] = lam[member]
        for side, sign in enumerate(SIGNS):
            rows = [row(side, 1 + sign * VELOCITIES[m][1], m, plane) for m in members]
            rows.append(mu_ref[0, side : side + 1, :])
            rows += [field(side, index) for index in range(FIELDS)]
            for index, value in enumerate(rows):
                slot = side * CORNER + index
                out_ref[10 + slot // 8, slot % 8 : slot % 8 + 1, :] = value
        for index in range(FIELDS):
            out_ref[STATIC + index] = fields_ref[index, plane]

    by_parity(write)


def faces_kernel(thrust_ref, lam_ref, fields_ref, rows_ref, coef_ref, near_ref, field_ref, part_ref, pack_ref, low_ref, high_ref):
    width, span = lam_ref.shape[1], lam_ref.shape[2]
    edges = wall_masks(lam_ref.shape[2:])
    source, row_of = own_lam(lam_ref), got_row(rows_ref, width)
    pack_ref[...] = jnp.zeros(pack_ref.shape, jnp.float32)
    field_ref[...] = jnp.zeros(field_ref.shape, jnp.float32)
    for side in range(2):
        for index, (far, member) in enumerate(PACK_LIST[side]):
            if far > 0:
                rows = rows_ref[side, index * width : (index + 1) * width, :]
            else:
                rows = lam_ref[member, :, span - 1 if side == 0 else 0, :]
            pack_ref[side, index, 2 : width + 2, :] = rows
        for field in range(FIELDS):
            start = (HALO + field) * width
            field_ref[side, field, 2 : width + 2, :] = rows_ref[side, start : start + width, :]
    place = lax.broadcasted_iota(jnp.int32, pack_ref.shape[2:], 0)
    inside = jnp.logical_and(place >= 2, place < width + 2)
    pack_edges = wall_masks(pack_ref.shape[2:])
    for side, (sign, wanted) in enumerate(((1, Y_UP), (-1, Y_DOWN))):
        mu = []
        for member in range(19):
            move_x, move_y, move_z = VELOCITIES[member]
            value = pack_ref[side, PACK_LIST[side].index((1 + sign * move_y, member))]
            if move_x != 0:
                value = pltpu.roll(value, (-move_x) % value.shape[0], 0)
            if move_z != 0:
                walls = pack_ref[side, PACK_LIST[side].index((1, OPPOSITE[member]))]
                value = roll_z(value, move_z, pack_edges, walls)
            mu.append(value)
        pops = [field_ref[side, member] for member in range(19)]
        coefs = plane_coefs(pops, turbine_cells(field_ref[side, 19], thrust_ref))
        lam, _ = plane_adjoint(mu, lambda index: coefs[index], wanted)
        for index, member in enumerate(wanted):
            part_ref[side, index] = jnp.where(inside, lam[member], 0.0)
    for out_ref, plane, members in ((low_ref, 0, X_UP), (high_ref, width - 1, X_DOWN)):
        lam, _ = plane_adjoint(
            gather_mu(source, row_of, plane, edges),
            lambda index: coef_ref[index, plane],
            members,
        )
        for index, member in enumerate(members):
            value, move_y = lam_ref[member, plane], VELOCITIES[member][1]
            if move_y != 0:
                value = span_shift(value, move_y, row_of(0 if move_y == 1 else 1, plane, member))
            out_ref[index] = value
            out_ref[5 + index] = lam[member]
        for side, (sign, wanted) in enumerate(((1, Y_UP), (-1, Y_DOWN))):
            sources = [
                pack_ref.at[side, PACK_LIST[side].index((1 + sign * VELOCITIES[member][1], member))]
                for member in members
            ]
            corner = VELOCITIES.index((VELOCITIES[members[0]][0], sign, 0))
            sources.append(part_ref.at[side, wanted.index(corner)])
            sources += [field_ref.at[side, field] for field in range(FIELDS)]
            for index, ref in enumerate(sources):
                slot = side * CORNER + index
                out_ref[10 + slot // 8, slot % 8 : slot % 8 + 1, :] = ref[plane + 2 : plane + 3, :]

    def write(even):
        near_ref[0:STATIC] = (high_ref if even else low_ref)[0:STATIC]
        for index in range(FIELDS):
            near_ref[STATIC + index] = fields_ref[index, width - 1 if even else 0]

    by_parity(write)


def middle_kernel(lam_ref, rows_ref, coef_ref, mid_ref, cell_ref):
    width = lam_ref.shape[1]
    edges = wall_masks(lam_ref.shape[2:])
    source, row_of = own_lam(lam_ref), got_row(rows_ref, width)
    for plane in range(width):
        mu = gather_mu(source, row_of, plane, edges)
        lam, mx = plane_adjoint(mu, lambda index: coef_ref[index, plane])
        for member in range(19):
            mid_ref[member, plane] = lam[member]
        cell_ref[plane] = mx * coef_ref[GAIN, plane]


def pair_kernel(turbines, thrust_ref, lam_ref, rows_ref, near_ref, far_ref, late_ref, early_ref, fields_ref,
                part_mid_ref, part_cell_ref, part_edge_ref, pack_ref,
                out_ref, next_ref, mid_ref, edge_ref, line_ref, above_ref, below_ref, part_face_ref):
    width, span, height = lam_ref.shape[1:]
    take_in(near_ref, far_ref, above_ref, below_ref)
    edges = wall_masks((span, height))
    pack_shape = pack_ref.shape[2:]
    pack_edges = wall_masks(pack_shape)
    place = lax.broadcasted_iota(jnp.int32, pack_shape, 0)
    totals = [part_cell_ref[plane] for plane in range(width)]
    for face_ref, plane, members in ((above_ref, width - 1, X_UP), (below_ref, 0, X_DOWN)):
        mu = [None] * 19
        for index, member in enumerate(members):
            mu[member] = roll_z(face_ref[index], VELOCITIES[member][2], edges)
        lam, mx = plane_adjoint(mu, lambda index: late_ref[index, plane])
        for member in range(19):
            mid_ref[member, 0 if plane == 0 else 1] = part_mid_ref[member, plane] + lam[member]
        totals[plane] = totals[plane] + mx * late_ref[GAIN, plane]

    for side, (static_ref, plane, members, wanted) in enumerate(
        ((above_ref, width - 1, X_DOWN, X_UP), (below_ref, 0, X_UP, X_DOWN))
    ):
        mu = [None] * 19
        for member in members:
            value, (_, move_y, move_z) = lam_ref[member, plane], VELOCITIES[member]
            if move_y != 0:
                value = span_shift(value, move_y, got_row(rows_ref, width)(0 if move_y == 1 else 1, plane, member))
            mu[member] = roll_z(value, move_z, edges)
        pops = [static_ref[STATIC + member] for member in range(19)]
        coefs = plane_coefs(pops, turbine_cells(static_ref[STATIC + 19], thrust_ref))
        lam, _ = plane_adjoint(mu, lambda index: coefs[index], wanted)
        for index, member in enumerate(wanted):
            part_face_ref[side, index] = lam[member]

    def beyond(below, above, rest):
        return jnp.where(place == 1, below, jnp.where(place == width + 2, above, rest))

    halo_tiles = []
    for side, (sign, wanted) in enumerate(((1, Y_UP), (-1, Y_DOWN))):
        mu = [None] * 19
        for members, got_ref, got_place, own_place in (
            (X_UP, above_ref, width + 1, 1),
            (X_DOWN, below_ref, 2, width + 2),
        ):
            plane = 0 if own_place == 1 else width - 1
            for index, member in enumerate(members):
                far = 1 + sign * VELOCITIES[member][1]
                if far > 0:
                    start = ROW_LIST[side].index((far, member)) * width + plane
                    own = rows_ref[side, start : start + 1, :]
                else:
                    inner = span - 1 if side == 0 else 0
                    own = lam_ref[member, plane, inner : inner + 1, :]
                value = jnp.where(
                    place == got_place,
                    corner_row(got_ref, side, index),
                    jnp.where(place == own_place, own, 0.0),
                )
                mu[member] = roll_z(value, VELOCITIES[member][2], pack_edges)
        fields = [
            beyond(
                corner_row(below_ref, side, 6 + field),
                corner_row(above_ref, side, 6 + field),
                pack_ref[side, field],
            )
            for field in range(FIELDS)
        ]
        coefs = plane_coefs(fields[:19], turbine_cells(fields[19], thrust_ref))
        lam, _ = plane_adjoint(mu, lambda index: coefs[index], wanted)
        for index, member in enumerate(wanted):
            value = part_edge_ref[side, index] + lam[member]
            if VELOCITIES[member][0] == 1:
                value = value + jnp.where(place == width + 2, corner_row(above_ref, side, 5), 0.0)
            elif VELOCITIES[member][0] == -1:
                value = value + jnp.where(place == 1, corner_row(below_ref, side, 5), 0.0)
            edge_ref[side, index] = value
        halo_tiles.append((fields[20], fields[19]))

    def middle(plane, member):
        if plane >= width:
            index = X_UP.index(member)
            return above_ref[5 + index] + part_face_ref[0, index]
        if plane < 0:
            index = X_DOWN.index(member)
            return below_ref[5 + index] + part_face_ref[1, index]
        if plane in (0, width - 1):
            return mid_ref[member, 0 if plane == 0 else 1]
        return part_mid_ref[member, plane]

    def middle_row(side, plane, member):
        index = (Y_UP, Y_DOWN)[side].index(member)
        return edge_ref[side, index, plane + 2 : plane + 3, :]

    for plane in range(width):
        mu = gather_mu(middle, middle_row, plane, edges)
        lam, mx = plane_adjoint(mu, lambda index: early_ref[index, plane])
        for member in range(19):
            out_ref[member, plane] = lam[member]
        totals[plane] = totals[plane] + mx * early_ref[GAIN, plane]

    for side, (members, row) in enumerate(((Y_UP, 0), (Y_DOWN, span - 1))):
        for index, member in enumerate(members):
            start = (5 * side + index) * width
            next_ref[start : start + width, :] = out_ref[member, :, row, :]

    nothing = jnp.zeros((1, height), jnp.float32)
    up, down = [], []
    for plane in range(width):
        up.append(
            2.0 * out_ref[1, plane]
            + span_shift(out_ref[7, plane], 1, nothing)
            + span_shift(out_ref[9, plane], -1, nothing)
            + roll_z(out_ref[11, plane], 1, edges)
            + roll_z(out_ref[13, plane], -1, edges)
        )
        down.append(
            2.0 * out_ref[2, plane]
            + span_shift(out_ref[8, plane], -1, nothing)
            + span_shift(out_ref[10, plane], 1, nothing)
            + roll_z(out_ref[12, plane], -1, edges)
            + roll_z(out_ref[14, plane], 1, edges)
        )
    tiles = []
    for plane in range(-1, width + 1):
        value = None
        if plane + 1 < width:
            value = up[plane + 1]
        if plane >= 1:
            value = -down[plane - 1] if value is None else value - down[plane - 1]
        if plane < 0 or plane >= width:
            face_ref = below_ref if plane < 0 else above_ref
            tiles.append((face_ref[STATIC + 20] * value, face_ref[STATIC + 19]))
            continue
        value = value + jnp.where(edges[1], out_ref[12, plane] - out_ref[13, plane], 0.0)
        value = value + jnp.where(edges[0], out_ref[14, plane] - out_ref[11, plane], 0.0)
        tiles.append((totals[plane] + fields_ref[20, plane] * value, fields_ref[19, plane]))
    line_ref[...] = jnp.zeros(line_ref.shape, jnp.float32)
    for side, (upward, downward, row) in enumerate(((9, 8, span - 1), (7, 10, 0))):
        line_ref[side, 0, 1 : width + 1, :] = out_ref[upward, :, row, :]
        line_ref[side, 1, 3 : width + 3, :] = out_ref[downward, :, row, :]
        gain, ids = halo_tiles[side]
        tiles.append(((line_ref[side, 0] - line_ref[side, 1]) * gain, ids))
    start = 10 * width
    next_ref[start:, :] = jnp.zeros((next_ref.shape[0] - start, height), jnp.float32)
    for turbine in range(turbines):
        row = None
        for value, ids in tiles:
            kept = jnp.sum(jnp.where(ids == float(turbine), value, 0.0), axis=0, keepdims=True)
            row = kept if row is None else row + kept
        next_ref[start + turbine : start + turbine + 1, :] = row


def last_faces_kernel(lam_ref, rows_ref, near_ref, far_ref):
    width = lam_ref.shape[1]

    def row_of(side, plane, member):
        place = (5 * side + (Y_UP, Y_DOWN)[side].index(member)) * width + plane
        return rows_ref[place : place + 1, :]

    def moved(members, plane):
        def tile(index):
            member = members[index]
            value, move_y = lam_ref[member, plane], VELOCITIES[member][1]
            if move_y == 0:
                return value
            return span_shift(value, move_y, row_of(0 if move_y == 1 else 1, plane, member))

        return tile

    far_ref[5:] = jnp.zeros((far_ref.shape[0] - 5,) + far_ref.shape[1:], jnp.float32)
    hand_out(moved(X_UP, 0), moved(X_DOWN, width - 1), near_ref, far_ref.at[0:5])


def pass_kernel(value_ref, _, out_ref):
    out_ref[...] = value_ref[...]


def last_kernel(lam_ref, rows_ref, near_ref, far_ref, coef_ref, out_ref):
    width, span, height = lam_ref.shape[1:]
    lane = lax.broadcasted_iota(jnp.int32, (span, height), 1)
    first, last = lane == 0, lane == height - 1
    odd = jnp.full((span, height), lax.rem(lax.axis_index("gx"), 2)) == 1

    def source(plane, member):
        if plane >= width:
            index = X_UP.index(member)
            return jnp.where(odd, far_ref[index], near_ref[index])
        if plane < 0:
            index = X_DOWN.index(member)
            return jnp.where(odd, near_ref[index], far_ref[index])
        value, move_y = lam_ref[member, plane], VELOCITIES[member][1]
        if move_y == 0:
            return value
        side = 0 if move_y == 1 else 1
        place = (5 * side + (Y_UP, Y_DOWN)[side].index(member)) * width + plane
        return span_shift(value, move_y, rows_ref[place : place + 1, :])

    for plane in range(width):
        mu = []
        for member in range(19):
            move_x, _, move_z = VELOCITIES[member]
            value = source(plane + move_x, member)
            if move_z == 1:
                value = jnp.where(
                    last, lam_ref[OPPOSITE[member], plane], pltpu.roll(value, height - 1, 1)
                )
            elif move_z == -1:
                value = jnp.where(first, lam_ref[OPPOSITE[member], plane], pltpu.roll(value, 1, 1))
            mu.append(value)
        lam, _ = plane_adjoint(mu, lambda index: coef_ref[index, plane])
        for member in range(19):
            out_ref[member, plane] = lam[member]


def call(kernel, outs, *args, scratch=(), micros=1):
    return pl.pallas_call(
        kernel,
        out_shape=tuple(jax.ShapeDtypeStruct(shape, jnp.float32) for shape in outs),
        in_specs=[pl.BlockSpec(memory_space=VMEM)] * len(args),
        out_specs=tuple(pl.BlockSpec(memory_space=VMEM) for _ in outs),
        scratch_shapes=[pltpu.VMEM(shape, jnp.float32) for shape in scratch],
        cost_estimate=pl.CostEstimate(
            flops=int(1e6 * micros), bytes_accessed=int(2e6 * micros), transcendentals=0
        ),
        compiler_params=pltpu.CompilerParams(vmem_limit_bytes=32 * 1024 * 1024),
    )(*args)


def ring(axis, step):
    count = lax.axis_size(axis)
    return [(i, (i + step) % count) for i in range(count)]


def swap_rows(rows):
    if lax.axis_size("gy") == 2:
        return lax.ppermute(rows, "gy", ring("gy", 1))
    return jnp.stack(
        [
            lax.ppermute(rows[0], "gy", ring("gy", -1)),
            lax.ppermute(rows[1], "gy", ring("gy", 1)),
        ]
    )


def swap_near(near):
    count = lax.axis_size("gx")
    assert count % 2 == 0
    return lax.ppermute(near, "gx", [(i, i ^ 1) for i in range(count)])


def swap_far(far):
    count = lax.axis_size("gx")
    return lax.ppermute(
        far, "gx", [(i, (i + 1 if i % 2 else i - 1) % count) for i in range(count)]
    )


def flips(value, axis, flip_list):
    count = lax.axis_size(axis)
    parts = [lax.ppermute(value, axis, [(i, i ^ flip) for i in range(count)]) for flip in flip_list]
    return sum(parts, value)


def sum_bits(value, axis, start):
    count = lax.axis_size(axis)
    while start < count:
        stop = min(4 * start, count)
        value = flips(value, axis, range(start, stop, start))
        start = stop
    return value


def last_exchange(lam, packed):
    width, height = lam.shape[1], lam.shape[3]
    rows_count = 10 * width
    sums = packed[rows_count:]
    count = lax.axis_size("gx")
    apart = count & (count - 1) == 0 and count > 2
    joined = apart and lax.axis_size("gy") == 2
    if joined:
        got = lax.ppermute(packed, "gy", ring("gy", 1))
        rows, got = got[:rows_count], got[rows_count:]
        got = got + lax.ppermute(sums, "gx", [(i, i ^ 2) for i in range(count)])
        got = got + lax.ppermute(
            sums, ("gx", "gy"), [(i, i ^ 5) for i in range(2 * count)]
        )
    else:
        rows = swap_rows(packed[:rows_count].reshape(2, rows_count // 2, -1))
        rows = rows.reshape(rows_count, -1)
        spans = lax.axis_size("gy")
        got = (lax.psum(sums, "gy") if spans & (spans - 1) else sum_bits(sums, "gy", 1)) - sums
    near, far = call(
        last_faces_kernel,
        [(5, lam.shape[2], height), (6, lam.shape[2], height)],
        lam,
        rows,
        micros=0.1,
    )
    sums = sums + got
    if apart and not joined:
        sums = flips(sums, "gx", [2])
    got_near, got_far = swap_near(near), swap_far(far)
    if apart:
        (sums,) = call(pass_kernel, [sums.shape], sums, got_near, micros=0.1)
        sums = sum_bits(flips(sums, "gx", [1]), "gx", 4)
    else:
        sums = lax.psum(sums, "gx")
    return rows, got_near, got_far, sums


def shards(fwd_pops, fwd_scale, seed_adjoint, turbine_map, thrust):
    steps, _, width, span, height = fwd_pops.shape
    assert steps == 3 and span == 8
    turbines = thrust.shape[0]
    turbine_rows = -(-turbines // 8) * 8
    sublanes = -(-(width + 4) // 8) * 8
    whole = (19, width, span, height)
    (begun,) = call(start_kernel, [(8, height)], micros=400)
    fields, first, thrust_rows, slope_rows = call(
        pack_kernel,
        [
            (FIELDS, width, span, height),
            (2, FIRST_ROWS, height),
            (turbine_rows, height),
            (turbine_rows, height),
        ],
        begun,
        thrust.reshape(1, turbines),
        turbine_map,
        fwd_scale,
        fwd_pops,
        seed_adjoint,
        micros=0.6,
    )
    first = swap_rows(first)
    coefs = call(
        coef_kernel,
        [(COEFS, width, span, height)] * steps,
        thrust_rows,
        turbine_map,
        fwd_scale,
        fwd_pops,
        micros=0.8,
    )
    (rows,) = call(
        rows_kernel,
        [(2, (HALO + FIELDS) * width, height)],
        seed_adjoint,
        fields,
        coefs[2],
        micros=0.1,
    )
    rows = swap_rows(rows)
    face, edge = (FACE_TILES, span, height), (2, 5, sublanes, height)
    tile = (19, span, height)
    (far,) = call(
        far_kernel,
        [face],
        thrust_rows,
        seed_adjoint,
        fields,
        first,
        coefs[2],
        scratch=[(20, span, height), tile, tile],
        micros=2000,
    )
    far = swap_far(far)
    near, pack, part_edge = call(
        faces_kernel,
        [face, (2, FIELDS, sublanes, height), edge],
        thrust_rows,
        seed_adjoint,
        fields,
        rows,
        coefs[2],
        scratch=[(2, len(PACK_LIST[0]), sublanes, height), face, face],
        micros=0.4,
    )
    near = swap_near(near)
    parts = call(
        middle_kernel,
        [whole, (width, span, height)],
        seed_adjoint,
        rows,
        coefs[2],
        micros=0.6,
    )
    lam, packed = call(
        lambda *refs: pair_kernel(turbines, *refs),
        [whole, (10 * width + turbine_rows, height)],
        thrust_rows,
        seed_adjoint,
        rows,
        near,
        far,
        coefs[2],
        coefs[1],
        fields,
        *parts,
        part_edge,
        pack,
        scratch=[
            (19, 2, span, height),
            edge,
            (2, 2, sublanes, height),
            face,
            face,
            (2, 5, span, height),
        ],
        micros=0.8,
    )
    rows, near, far, sums = last_exchange(lam, packed)
    (lam,) = call(last_kernel, [whole], lam, rows, near, far, coefs[0], micros=0.5)
    thrust_grad = jnp.sum((slope_rows * sums)[:turbines], axis=1)
    return (lam, thrust_grad)


def solution(mesh):
    placed = (
        P(None, None, "gx", "gy", None),
        P(None, "gx", "gy", None),
        P(None, "gx", "gy", None),
        P("gx", "gy", None),
        P(),
    )
    return jax.shard_map(
        shards,
        mesh=mesh,
        in_specs=placed,
        out_specs=(P(None, "gx", "gy", None), P()),
        check_vma=False,
    )
```

```python
import jax
import jax.numpy as jnp
from jax import lax
from jax.experimental import pallas as pl
from jax.experimental.pallas import tpu as pltpu
from jax.sharding import PartitionSpec as P

VELOCITIES = (
    (0, 0, 0),
    (1, 0, 0),
    (-1, 0, 0),
    (0, 1, 0),
    (0, -1, 0),
    (0, 0, 1),
    (0, 0, -1),
    (1, 1, 0),
    (-1, -1, 0),
    (1, -1, 0),
    (-1, 1, 0),
    (1, 0, 1),
    (-1, 0, -1),
    (1, 0, -1),
    (-1, 0, 1),
    (0, 1, 1),
    (0, -1, -1),
    (0, 1, -1),
    (0, -1, 1),
)
OPPOSITE = (0, 2, 1, 4, 3, 6, 5, 8, 7, 10, 9, 12, 11, 14, 13, 16, 15, 18, 17)
WEIGHTS = tuple([1.0 / 3.0] + [1.0 / 18.0] * 6 + [1.0 / 36.0] * 12)
MEAN_FLOW = 0.1
TAU_BASE = 0.51
SMAG_COEF = 18.0 * 1.4142135623730951 * 0.17 * 0.17
QUAD_FLOOR = 0.0001

X_UP = (1, 7, 9, 11, 13)
X_DOWN = (2, 8, 10, 12, 14)
Y_UP = (3, 7, 10, 15, 17)
Y_DOWN = (4, 8, 9, 16, 18)

KEEP, MASS, FLUX, UX, UY, UZ, Q1 = 19, 20, 21, 22, 23, 24, 25
RATE, BULK, PX, PY, PZ, DRAG, DRAG_U, GAIN = 34, 35, 36, 37, 38, 39, 40, 41
COEFS = 42

FIELDS = 21

VMEM = pltpu.VMEM


def halo_list(axis, sign):
    near = [
        (1, m) for m in range(19) if VELOCITIES[m][axis] * sign >= 0 or VELOCITIES[m][2] != 0
    ]
    return near + [(2, m) for m in range(19) if VELOCITIES[m][axis] * sign == 1]


SIGNS = (1, -1)
ROW_LIST = [halo_list(1, sign) for sign in SIGNS]
INNER_LIST = [[(0, m) for m in range(19) if VELOCITIES[m][1] * sign == -1] for sign in SIGNS]
PACK_LIST = [ROW_LIST[side] + INNER_LIST[side] for side in range(2)]
HALO = len(ROW_LIST[0])
CORNER = 6 + FIELDS
NEXT_LIST = [
    [[(far, m) for far, m in ROW_LIST[y] if VELOCITIES[m][0] == sign] for y in range(2)]
    for sign in SIGNS
]
FIRST_ROWS = -(-(HALO + len(NEXT_LIST[0][0]) + FIELDS) // 8) * 8
MIRROR = [VELOCITIES.index((a, -b, c)) for a, b, c in VELOCITIES]
STATIC = 10 + -(-2 * CORNER // 8)
FACE_TILES = STATIC + FIELDS


def base_values():
    values = []
    for member in range(19):
        along = float(VELOCITIES[member][0])
        values.append(
            WEIGHTS[member]
            * (
                1.0
                + 3.0 * MEAN_FLOW * along
                + 4.5 * MEAN_FLOW * MEAN_FLOW * along * along
                - 1.5 * MEAN_FLOW * MEAN_FLOW
            )
        )
    return values


def plane_coefs(pops, thrust_cell):
    rho = pops[0]
    for member in range(1, 19):
        rho = rho + pops[member]
    inv_rho = 1.0 / rho
    vel = []
    for axis_id in range(3):
        moment = None
        for member in range(19):
            component = VELOCITIES[member][axis_id]
            if component == 1:
                moment = pops[member] if moment is None else moment + pops[member]
            elif component == -1:
                moment = moment - pops[member]
        vel.append(moment * inv_rho)
    ux, uy, uz = vel
    speed_sq = ux * ux + uy * uy + uz * uz
    rest = 1.0 - 1.5 * speed_sq
    part = []
    for member in range(19):
        if member == 0:
            part.append(pops[0] - (WEIGHTS[0] * rho) * rest)
            continue
        proj = None
        for axis_id in range(3):
            component = VELOCITIES[member][axis_id]
            if component == 1:
                proj = vel[axis_id] if proj is None else proj + vel[axis_id]
            elif component == -1:
                proj = -vel[axis_id] if proj is None else proj - vel[axis_id]
        part.append(pops[member] - (WEIGHTS[member] * rho) * (rest + 3.0 * proj + 4.5 * proj * proj))

    def pair(member):
        return part[member] + part[member + 1]

    in_xy, in_xz, in_yz = pair(7) + pair(9), pair(11) + pair(13), pair(15) + pair(17)
    pxx, pyy, pzz = pair(1) + in_xy + in_xz, pair(3) + in_xy + in_yz, pair(5) + in_xz + in_yz
    pxy, pxz, pyz = pair(7) - pair(9), pair(11) - pair(13), pair(15) - pair(17)
    square = (
        pxx * pxx + pyy * pyy + pzz * pzz + 2.0 * (pxy * pxy + pxz * pxz + pyz * pyz) + QUAD_FLOOR
    )
    size = jnp.sqrt(square)
    root = jnp.sqrt(TAU_BASE * TAU_BASE + SMAG_COEF * size * inv_rho)
    omega = 1.0 / (0.5 * (TAU_BASE + root))
    pux = pxx * ux + pxy * uy + pxz * uz
    puy = pxy * ux + pyy * uy + pyz * uz
    puz = pxz * ux + pyz * uy + pzz * uz
    flux = omega * (3.0 / 36.0)
    drag = (3.0 / 36.0) * thrust_cell * jnp.abs(ux) * inv_rho
    result = list(part)
    result.append(1.0 - omega)
    result.append((omega * (1.0 / 36.0)) * (1.0 + 1.5 * speed_sq))
    result.append(flux)
    result.extend(vel)
    result.extend((pxx, pyy, pzz))
    result.extend((pxx + pyy + 2.0 * pxy, pxx + pyy - 2.0 * pxy))
    result.extend((pxx + pzz + 2.0 * pxz, pxx + pzz - 2.0 * pxz))
    result.extend((pyy + pzz + 2.0 * pyz, pyy + pzz - 2.0 * pyz))
    result.append((0.25 * SMAG_COEF) * omega * omega * inv_rho / (root * size))
    result.append(
        (pux * ux + puy * uy + puz * uz) - (pxx + pyy + pzz) * (1.0 / 3.0) - square * inv_rho
    )
    result.extend((-2.0 * pux, -2.0 * puy, -2.0 * puz))
    result.append(drag)
    result.append(drag * ux)
    result.append((-1.5 / 36.0) * ux * jnp.abs(ux))
    return result


def plus(*values):
    kept = [value for value in values if value is not None]
    return sum(kept[1:], kept[0]) if kept else None


def minus(left, right):
    if right is None:
        return left
    return -right if left is None else left - right


def times(left, right):
    return None if left is None or right is None else left * right


def plane_adjoint(mu, coef, wanted=range(19)):
    total, diff = {}, {}
    for member in range(1, 19, 2):
        total[member] = plus(mu[member], mu[member + 1])
        diff[member] = minus(mu[member], mu[member + 1])
    two_x, two_y, two_z = times(total[1], 2.0), times(total[3], 2.0), times(total[5], 2.0)
    in_xy, in_xz = plus(total[7], total[9]), plus(total[11], total[13])
    in_yz = plus(total[15], total[17])
    mxx, myy, mzz = plus(two_x, in_xy, in_xz), plus(two_y, in_xy, in_yz), plus(two_z, in_xz, in_yz)
    mxy, mxz = minus(total[7], total[9]), minus(total[11], total[13])
    myz = minus(total[15], total[17])
    m0 = plus(times(mu[0], 12.0), plus(two_x, two_y, two_z), plus(in_xy, in_xz, in_yz))
    mx = plus(times(diff[1], 2.0), plus(diff[7], diff[9]), plus(diff[11], diff[13]))
    my = plus(times(diff[3], 2.0), minus(diff[7], diff[9]), plus(diff[15], diff[17]))
    mz = plus(times(diff[5], 2.0), minus(diff[11], diff[13]), minus(diff[15], diff[17]))
    ux, uy, uz = coef(UX), coef(UY), coef(UZ)
    vx = plus(times(mxx, ux), times(mxy, uy), times(mxz, uz))
    vy = plus(times(mxy, ux), times(myy, uy), times(myz, uz))
    vz = plus(times(mxz, ux), times(myz, uy), times(mzz, uz))
    along = [mu[member] * coef(member) for member in range(19) if mu[member] is not None]
    while len(along) > 1:
        along = [
            along[k] + along[k + 1] if k + 1 < len(along) else along[k]
            for k in range(0, len(along), 2)
        ]
    gamma = along[0] * coef(RATE)
    flux = coef(FLUX)
    alpha = (
        coef(MASS) * m0
        - 1.5 * flux * (vx * ux + vy * uy + vz * uz)
        + gamma * coef(BULK)
        + mx * coef(DRAG_U)
    )
    beta_x = flux * (plus(mx, 3.0 * vx) - ux * m0) + gamma * coef(PX) - mx * coef(DRAG)
    beta_y = flux * (plus(my, 3.0 * vy) - uy * m0) + gamma * coef(PY)
    beta_z = flux * (plus(mz, 3.0 * vz) - uz * m0) + gamma * coef(PZ)
    keep = coef(KEEP)
    odd = {
        1: beta_x,
        3: beta_y,
        5: beta_z,
        7: beta_x + beta_y,
        9: beta_x - beta_y,
        11: beta_x + beta_z,
        13: beta_x - beta_z,
        15: beta_y + beta_z,
        17: beta_y - beta_z,
    }
    result = {}
    for member in wanted:
        if member == 0:
            result[0] = plus(times(mu[0], keep), alpha)
            continue
        forward = member - 1 + member % 2
        even = alpha + gamma * coef(Q1 + forward // 2)
        rest = even + odd[forward] if member == forward else even - odd[forward]
        result[member] = plus(times(mu[member], keep), rest)
    return result, mx


def turbine_cells(ids, thrust_ref):
    ratio = jnp.zeros(ids.shape, jnp.float32)
    for turbine in range(thrust_ref.shape[0]):
        row = thrust_ref[turbine : turbine + 1, :]
        ratio = jnp.where(ids == jnp.asarray(turbine, ids.dtype), row, ratio)
    return jnp.where(ids >= 0, local_thrust(ratio), 0.0)


def local_thrust(values):
    return 4.0 * values / jnp.square(1.0 + jnp.sqrt(1.0 - values))


def decode(scale_ref, pops_ref, instant, plane):
    base = base_values()
    scale = scale_ref[instant, plane]
    return [
        base[member] * (1.0 + scale * pops_ref[instant, member, plane].astype(jnp.float32))
        for member in range(19)
    ]


def coef_kernel(thrust_ref, map_ref, scale_ref, pops_ref, *out_refs):
    for plane in range(pops_ref.shape[2]):
        thrust_cell = turbine_cells(map_ref[plane], thrust_ref)
        for instant, out_ref in enumerate(out_refs):
            pops = decode(scale_ref, pops_ref, instant, plane)
            for index, value in enumerate(plane_coefs(pops, thrust_cell)):
                out_ref[index, plane] = value


def by_parity(even):
    odd = lax.rem(lax.axis_index("gx"), 2) == 1
    pl.when(jnp.logical_not(odd))(lambda: even(True))
    pl.when(odd)(lambda: even(False))


def hand_out(low, high, near_ref, far_ref):
    def write(even):
        for source, out_ref in ((low, far_ref), (high, near_ref)) if even else ((low, near_ref), (high, far_ref)):
            for index in range(out_ref.shape[0]):
                out_ref[index] = source(index)

    by_parity(write)


def take_in(near_ref, far_ref, above_ref, below_ref):
    def write(even):
        for source, out_ref in ((near_ref, above_ref if even else below_ref), (far_ref, below_ref if even else above_ref)):
            for index in range(out_ref.shape[0]):
                out_ref[index] = source[index]

    by_parity(write)


def start_kernel(out_ref):
    out_ref[...] = jnp.zeros(out_ref.shape, jnp.float32)


def write_thrust(thrust_ref, thrust_rows_ref, slope_rows_ref):
    thrust_rows_ref[...] = jnp.zeros(thrust_rows_ref.shape, jnp.float32)
    for turbine in range(thrust_ref.shape[1]):
        thrust_rows_ref[turbine : turbine + 1, :] = jnp.broadcast_to(
            thrust_ref[0:1, turbine : turbine + 1], (1, thrust_rows_ref.shape[1])
        )
    root = jnp.sqrt(1.0 - thrust_rows_ref[...])
    slope_rows_ref[...] = 4.0 / (root * jnp.square(1.0 + root))


def pack_kernel(_, thrust_ref, map_ref, scale_ref, pops_ref, lam_ref, fields_ref, first_ref, thrust_rows_ref, slope_rows_ref):
    width, span = lam_ref.shape[1], lam_ref.shape[2]
    write_thrust(thrust_ref, thrust_rows_ref, slope_rows_ref)
    last = pops_ref.shape[0] - 1
    for plane in range(width):
        for index, value in enumerate(decode(scale_ref, pops_ref, last, plane)):
            fields_ref[index, plane] = value
        fields_ref[19, plane] = map_ref[plane].astype(jnp.float32)
        pops = decode(scale_ref, pops_ref, 0, plane)
        rho, momentum = pops[0], None
        for member in range(1, 19):
            rho = rho + pops[member]
        for member in X_UP:
            pair = pops[member] - pops[member + 1]
            momentum = pair if momentum is None else momentum + pair
        ux = momentum / rho
        fields_ref[20, plane] = (-1.5 / 36.0) * ux * jnp.abs(ux)
    first_ref[...] = jnp.zeros(first_ref.shape, jnp.float32)

    def write(even):
        plane, inner = (0, 1) if even else (width - 1, width - 2)
        for side in range(2):
            picks = [(lam_ref, m, plane, far) for far, m in ROW_LIST[side]]
            picks += [(lam_ref, m, inner, far) for far, m in NEXT_LIST[0 if even else 1][side]]
            picks += [(fields_ref, field, plane, 1) for field in range(FIELDS)]
            for index, (ref, member, at, far) in enumerate(picks):
                row = far - 1 if side == 0 else span - far
                first_ref[side, index : index + 1, :] = ref[member, at, row : row + 1, :]

    by_parity(write)


def rows_kernel(lam_ref, fields_ref, _, rows_ref):
    width, span = lam_ref.shape[1], lam_ref.shape[2]
    for side in range(2):
        for index, (far, member) in enumerate(ROW_LIST[side]):
            row = far - 1 if side == 0 else span - far
            rows_ref[side, index * width : (index + 1) * width, :] = lam_ref[member, :, row, :]
        row = 0 if side == 0 else span - 1
        for field in range(FIELDS):
            start = (HALO + field) * width
            rows_ref[side, start : start + width, :] = fields_ref[field, :, row, :]


def span_shift(value, move, row):
    span = value.shape[0]
    place = lax.broadcasted_iota(jnp.int32, value.shape, 0)
    if move == 1:
        return jnp.where(place == span - 1, row, pltpu.roll(value, span - 1, 0))
    return jnp.where(place == 0, row, pltpu.roll(value, 1, 0))


def roll_z(value, move, edges, walls=None):
    height = value.shape[1]
    if move == 0:
        return value
    shift, edge = (height - 1, edges[1]) if move == 1 else (1, edges[0])
    return jnp.where(edge, 0.0 if walls is None else walls, pltpu.roll(value, shift, 1))


def wall_masks(shape):
    lane = lax.broadcasted_iota(jnp.int32, shape, 1)
    return lane == 0, lane == shape[1] - 1


def gather_mu(source, row_of, plane, edges):
    mu = []
    for member in range(19):
        move_x, move_y, move_z = VELOCITIES[member]
        value = source(plane + move_x, member)
        if value is not None and move_y != 0:
            side = 0 if move_y == 1 else 1
            value = span_shift(value, move_y, row_of(side, plane + move_x, member))
        if move_z != 0:
            walls = source(plane, OPPOSITE[member])
            if value is None:
                value = jnp.where(edges[1 if move_z == 1 else 0], walls, 0.0)
            else:
                value = roll_z(value, move_z, edges, walls)
        mu.append(value)
    return mu


def own_lam(lam_ref):
    def source(plane, member):
        return lam_ref[member, plane] if 0 <= plane < lam_ref.shape[1] else None

    return source


def got_row(rows_ref, width):
    def row_of(side, plane, member):
        place = ROW_LIST[side].index((1, member)) * width + plane
        return rows_ref[side, place : place + 1, :]

    return row_of


def corner_row(face_ref, side, index):
    slot = side * CORNER + index
    return face_ref[10 + slot // 8, slot % 8 : slot % 8 + 1, :]


def far_kernel(thrust_ref, lam_ref, fields_ref, first_ref, coef_ref, out_ref, pop_ref, mu_ref, wall_ref):
    width, span = lam_ref.shape[1], lam_ref.shape[2]
    edges = wall_masks(lam_ref.shape[2:])
    source = own_lam(lam_ref)
    pop_ref[...] = jnp.ones(pop_ref.shape, jnp.float32)

    def write(even):
        x_side, plane, inner, members = (0, 0, 1, X_UP) if even else (1, width - 1, width - 2, X_DOWN)
        inward = SIGNS[x_side]

        def row(side, far, member, at):
            if far == 0:
                last = span - 1 if side == 0 else 0
                return lam_ref[member, at, last : last + 1, :]
            place = (
                ROW_LIST[side].index((far, member))
                if at == plane
                else HALO + NEXT_LIST[x_side][side].index((far, member))
            )
            return first_ref[side, place : place + 1, :]

        def field(side, index):
            place = HALO + len(NEXT_LIST[0][0]) + index
            return first_ref[side, place : place + 1, :]

        def row_of(side, at, member):
            return row(side, 1, member, at)

        for member in range(19):
            move_x, move_y, move_z = VELOCITIES[member]
            for side in range(2):
                same = (member, MIRROR[member])[side]
                wall = (OPPOSITE[member], MIRROR[OPPOSITE[member]])[side]
                pop_ref[member, side : side + 1, :] = field(side, same)
                if move_x != -inward:
                    mu_ref[member, side : side + 1, :] = row(
                        side, 1 + move_y, same, plane if move_x == 0 else inner
                    )
                if move_z != 0:
                    wall_ref[member, side : side + 1, :] = row(side, 1, wall, plane)
        for side in range(2):
            pop_ref[19, side : side + 1, :] = field(side, 19)
        mu = []
        for member in range(19):
            move_x, _, move_z = VELOCITIES[member]
            if move_z == 0:
                mu.append(None if move_x == -inward else mu_ref[member])
            elif move_x == -inward:
                mu.append(jnp.where(edges[1 if move_z == 1 else 0], wall_ref[member], 0.0))
            else:
                mu.append(roll_z(mu_ref[member], move_z, edges, wall_ref[member]))
        coefs = plane_coefs(
            [pop_ref[member] for member in range(19)], turbine_cells(pop_ref[19], thrust_ref)
        )
        corner = VELOCITIES.index((inward, 1, 0))
        corners, _ = plane_adjoint(mu, lambda index: coefs[index], (corner,))
        mu_ref[0] = corners[corner]
        lam, _ = plane_adjoint(
            gather_mu(source, row_of, plane, edges),
            lambda index: coef_ref[index, plane],
            members,
        )
        for index, member in enumerate(members):
            value, move_y = lam_ref[member, plane], VELOCITIES[member][1]
            if move_y != 0:
                value = span_shift(value, move_y, row_of(0 if move_y == 1 else 1, plane, member))
            out_ref[index] = value
            out_ref[5 + index] = lam[member]
        for side, sign in enumerate(SIGNS):
            rows = [row(side, 1 + sign * VELOCITIES[m][1], m, plane) for m in members]
            rows.append(mu_ref[0, side : side + 1, :])
            rows += [field(side, index) for index in range(FIELDS)]
            for index, value in enumerate(rows):
                slot = side * CORNER + index
                out_ref[10 + slot // 8, slot % 8 : slot % 8 + 1, :] = value
        for index in range(FIELDS):
            out_ref[STATIC + index] = fields_ref[index, plane]

    by_parity(write)


def faces_kernel(thrust_ref, lam_ref, fields_ref, rows_ref, coef_ref, near_ref, field_ref, part_ref, pack_ref, low_ref, high_ref):
    width, span = lam_ref.shape[1], lam_ref.shape[2]
    edges = wall_masks(lam_ref.shape[2:])
    source, row_of = own_lam(lam_ref), got_row(rows_ref, width)
    pack_ref[...] = jnp.zeros(pack_ref.shape, jnp.float32)
    field_ref[...] = jnp.zeros(field_ref.shape, jnp.float32)
    for side in range(2):
        for index, (far, member) in enumerate(PACK_LIST[side]):
            if far > 0:
                rows = rows_ref[side, index * width : (index + 1) * width, :]
            else:
                rows = lam_ref[member, :, span - 1 if side == 0 else 0, :]
            pack_ref[side, index, 2 : width + 2, :] = rows
        for field in range(FIELDS):
            start = (HALO + field) * width
            field_ref[side, field, 2 : width + 2, :] = rows_ref[side, start : start + width, :]
    place = lax.broadcasted_iota(jnp.int32, pack_ref.shape[2:], 0)
    inside = jnp.logical_and(place >= 2, place < width + 2)
    pack_edges = wall_masks(pack_ref.shape[2:])
    for side, (sign, wanted) in enumerate(((1, Y_UP), (-1, Y_DOWN))):
        mu = []
        for member in range(19):
            move_x, move_y, move_z = VELOCITIES[member]
            value = pack_ref[side, PACK_LIST[side].index((1 + sign * move_y, member))]
            if move_x != 0:
                value = pltpu.roll(value, (-move_x) % value.shape[0], 0)
            if move_z != 0:
                walls = pack_ref[side, PACK_LIST[side].index((1, OPPOSITE[member]))]
                value = roll_z(value, move_z, pack_edges, walls)
            mu.append(value)
        pops = [field_ref[side, member] for member in range(19)]
        coefs = plane_coefs(pops, turbine_cells(field_ref[side, 19], thrust_ref))
        lam, _ = plane_adjoint(mu, lambda index: coefs[index], wanted)
        for index, member in enumerate(wanted):
            part_ref[side, index] = jnp.where(inside, lam[member], 0.0)
    for out_ref, plane, members in ((low_ref, 0, X_UP), (high_ref, width - 1, X_DOWN)):
        lam, _ = plane_adjoint(
            gather_mu(source, row_of, plane, edges),
            lambda index: coef_ref[index, plane],
            members,
        )
        for index, member in enumerate(members):
            value, move_y = lam_ref[member, plane], VELOCITIES[member][1]
            if move_y != 0:
                value = span_shift(value, move_y, row_of(0 if move_y == 1 else 1, plane, member))
            out_ref[index] = value
            out_ref[5 + index] = lam[member]
        for side, (sign, wanted) in enumerate(((1, Y_UP), (-1, Y_DOWN))):
            sources = [
                pack_ref.at[side, PACK_LIST[side].index((1 + sign * VELOCITIES[member][1], member))]
                for member in members
            ]
            corner = VELOCITIES.index((VELOCITIES[members[0]][0], sign, 0))
            sources.append(part_ref.at[side, wanted.index(corner)])
            sources += [field_ref.at[side, field] for field in range(FIELDS)]
            for index, ref in enumerate(sources):
                slot = side * CORNER + index
                out_ref[10 + slot // 8, slot % 8 : slot % 8 + 1, :] = ref[plane + 2 : plane + 3, :]

    def write(even):
        near_ref[0:STATIC] = (high_ref if even else low_ref)[0:STATIC]
        for index in range(FIELDS):
            near_ref[STATIC + index] = fields_ref[index, width - 1 if even else 0]

    by_parity(write)


def middle_kernel(lam_ref, rows_ref, coef_ref, mid_ref, cell_ref):
    width = lam_ref.shape[1]
    edges = wall_masks(lam_ref.shape[2:])
    source, row_of = own_lam(lam_ref), got_row(rows_ref, width)
    for plane in range(width):
        mu = gather_mu(source, row_of, plane, edges)
        lam, mx = plane_adjoint(mu, lambda index: coef_ref[index, plane])
        for member in range(19):
            mid_ref[member, plane] = lam[member]
        cell_ref[plane] = mx * coef_ref[GAIN, plane]


def pair_kernel(turbines, thrust_ref, lam_ref, rows_ref, near_ref, far_ref, late_ref, early_ref, fields_ref,
                part_mid_ref, part_cell_ref, part_edge_ref, pack_ref,
                out_ref, next_ref, mid_ref, edge_ref, line_ref, above_ref, below_ref, part_face_ref):
    width, span, height = lam_ref.shape[1:]
    take_in(near_ref, far_ref, above_ref, below_ref)
    edges = wall_masks((span, height))
    pack_shape = pack_ref.shape[2:]
    pack_edges = wall_masks(pack_shape)
    place = lax.broadcasted_iota(jnp.int32, pack_shape, 0)
    totals = [part_cell_ref[plane] for plane in range(width)]
    for face_ref, plane, members in ((above_ref, width - 1, X_UP), (below_ref, 0, X_DOWN)):
        mu = [None] * 19
        for index, member in enumerate(members):
            mu[member] = roll_z(face_ref[index], VELOCITIES[member][2], edges)
        lam, mx = plane_adjoint(mu, lambda index: late_ref[index, plane])
        for member in range(19):
            mid_ref[member, 0 if plane == 0 else 1] = part_mid_ref[member, plane] + lam[member]
        totals[plane] = totals[plane] + mx * late_ref[GAIN, plane]

    for side, (static_ref, plane, members, wanted) in enumerate(
        ((above_ref, width - 1, X_DOWN, X_UP), (below_ref, 0, X_UP, X_DOWN))
    ):
        mu = [None] * 19
        for member in members:
            value, (_, move_y, move_z) = lam_ref[member, plane], VELOCITIES[member]
            if move_y != 0:
                value = span_shift(value, move_y, got_row(rows_ref, width)(0 if move_y == 1 else 1, plane, member))
            mu[member] = roll_z(value, move_z, edges)
        pops = [static_ref[STATIC + member] for member in range(19)]
        coefs = plane_coefs(pops, turbine_cells(static_ref[STATIC + 19], thrust_ref))
        lam, _ = plane_adjoint(mu, lambda index: coefs[index], wanted)
        for index, member in enumerate(wanted):
            part_face_ref[side, index] = lam[member]

    def beyond(below, above, rest):
        return jnp.where(place == 1, below, jnp.where(place == width + 2, above, rest))

    halo_tiles = []
    for side, (sign, wanted) in enumerate(((1, Y_UP), (-1, Y_DOWN))):
        mu = [None] * 19
        for members, got_ref, got_place, own_place in (
            (X_UP, above_ref, width + 1, 1),
            (X_DOWN, below_ref, 2, width + 2),
        ):
            plane = 0 if own_place == 1 else width - 1
            for index, member in enumerate(members):
                far = 1 + sign * VELOCITIES[member][1]
                if far > 0:
                    start = ROW_LIST[side].index((far, member)) * width + plane
                    own = rows_ref[side, start : start + 1, :]
                else:
                    inner = span - 1 if side == 0 else 0
                    own = lam_ref[member, plane, inner : inner + 1, :]
                value = jnp.where(
                    place == got_place,
                    corner_row(got_ref, side, index),
                    jnp.where(place == own_place, own, 0.0),
                )
                mu[member] = roll_z(value, VELOCITIES[member][2], pack_edges)
        fields = [
            beyond(
                corner_row(below_ref, side, 6 + field),
                corner_row(above_ref, side, 6 + field),
                pack_ref[side, field],
            )
            for field in range(FIELDS)
        ]
        coefs = plane_coefs(fields[:19], turbine_cells(fields[19], thrust_ref))
        lam, _ = plane_adjoint(mu, lambda index: coefs[index], wanted)
        for index, member in enumerate(wanted):
            value = part_edge_ref[side, index] + lam[member]
            if VELOCITIES[member][0] == 1:
                value = value + jnp.where(place == width + 2, corner_row(above_ref, side, 5), 0.0)
            elif VELOCITIES[member][0] == -1:
                value = value + jnp.where(place == 1, corner_row(below_ref, side, 5), 0.0)
            edge_ref[side, index] = value
        halo_tiles.append((fields[20], fields[19]))

    def middle(plane, member):
        if plane >= width:
            index = X_UP.index(member)
            return above_ref[5 + index] + part_face_ref[0, index]
        if plane < 0:
            index = X_DOWN.index(member)
            return below_ref[5 + index] + part_face_ref[1, index]
        if plane in (0, width - 1):
            return mid_ref[member, 0 if plane == 0 else 1]
        return part_mid_ref[member, plane]

    def middle_row(side, plane, member):
        index = (Y_UP, Y_DOWN)[side].index(member)
        return edge_ref[side, index, plane + 2 : plane + 3, :]

    for plane in range(width):
        mu = gather_mu(middle, middle_row, plane, edges)
        lam, mx = plane_adjoint(mu, lambda index: early_ref[index, plane])
        for member in range(19):
            out_ref[member, plane] = lam[member]
        totals[plane] = totals[plane] + mx * early_ref[GAIN, plane]

    for side, (members, row) in enumerate(((Y_UP, 0), (Y_DOWN, span - 1))):
        for index, member in enumerate(members):
            start = (5 * side + index) * width
            next_ref[start : start + width, :] = out_ref[member, :, row, :]

    nothing = jnp.zeros((1, height), jnp.float32)
    up, down = [], []
    for plane in range(width):
        up.append(
            2.0 * out_ref[1, plane]
            + span_shift(out_ref[7, plane], 1, nothing)
            + span_shift(out_ref[9, plane], -1, nothing)
            + roll_z(out_ref[11, plane], 1, edges)
            + roll_z(out_ref[13, plane], -1, edges)
        )
        down.append(
            2.0 * out_ref[2, plane]
            + span_shift(out_ref[8, plane], -1, nothing)
            + span_shift(out_ref[10, plane], 1, nothing)
            + roll_z(out_ref[12, plane], -1, edges)
            + roll_z(out_ref[14, plane], 1, edges)
        )
    tiles = []
    for plane in range(-1, width + 1):
        value = None
        if plane + 1 < width:
            value = up[plane + 1]
        if plane >= 1:
            value = -down[plane - 1] if value is None else value - down[plane - 1]
        if plane < 0 or plane >= width:
            face_ref = below_ref if plane < 0 else above_ref
            tiles.append((face_ref[STATIC + 20] * value, face_ref[STATIC + 19]))
            continue
        value = value + jnp.where(edges[1], out_ref[12, plane] - out_ref[13, plane], 0.0)
        value = value + jnp.where(edges[0], out_ref[14, plane] - out_ref[11, plane], 0.0)
        tiles.append((totals[plane] + fields_ref[20, plane] * value, fields_ref[19, plane]))
    line_ref[...] = jnp.zeros(line_ref.shape, jnp.float32)
    for side, (upward, downward, row) in enumerate(((9, 8, span - 1), (7, 10, 0))):
        line_ref[side, 0, 1 : width + 1, :] = out_ref[upward, :, row, :]
        line_ref[side, 1, 3 : width + 3, :] = out_ref[downward, :, row, :]
        gain, ids = halo_tiles[side]
        tiles.append(((line_ref[side, 0] - line_ref[side, 1]) * gain, ids))
    start = 10 * width
    next_ref[start:, :] = jnp.zeros((next_ref.shape[0] - start, height), jnp.float32)
    for turbine in range(turbines):
        row = None
        for value, ids in tiles:
            kept = jnp.sum(jnp.where(ids == float(turbine), value, 0.0), axis=0, keepdims=True)
            row = kept if row is None else row + kept
        next_ref[start + turbine : start + turbine + 1, :] = row


def last_faces_kernel(lam_ref, rows_ref, near_ref, far_ref):
    width = lam_ref.shape[1]

    def row_of(side, plane, member):
        place = (5 * side + (Y_UP, Y_DOWN)[side].index(member)) * width + plane
        return rows_ref[place : place + 1, :]

    def moved(members, plane):
        def tile(index):
            member = members[index]
            value, move_y = lam_ref[member, plane], VELOCITIES[member][1]
            if move_y == 0:
                return value
            return span_shift(value, move_y, row_of(0 if move_y == 1 else 1, plane, member))

        return tile

    far_ref[5:] = jnp.zeros((far_ref.shape[0] - 5,) + far_ref.shape[1:], jnp.float32)
    hand_out(moved(X_UP, 0), moved(X_DOWN, width - 1), near_ref, far_ref.at[0:5])


def pass_kernel(value_ref, _, out_ref):
    out_ref[...] = value_ref[...]


def last_kernel(lam_ref, rows_ref, near_ref, far_ref, coef_ref, out_ref):
    width, span, height = lam_ref.shape[1:]
    lane = lax.broadcasted_iota(jnp.int32, (span, height), 1)
    first, last = lane == 0, lane == height - 1
    odd = jnp.full((span, height), lax.rem(lax.axis_index("gx"), 2)) == 1

    def source(plane, member):
        if plane >= width:
            index = X_UP.index(member)
            return jnp.where(odd, far_ref[index], near_ref[index])
        if plane < 0:
            index = X_DOWN.index(member)
            return jnp.where(odd, near_ref[index], far_ref[index])
        value, move_y = lam_ref[member, plane], VELOCITIES[member][1]
        if move_y == 0:
            return value
        side = 0 if move_y == 1 else 1
        place = (5 * side + (Y_UP, Y_DOWN)[side].index(member)) * width + plane
        return span_shift(value, move_y, rows_ref[place : place + 1, :])

    for plane in range(width):
        mu = []
        for member in range(19):
            move_x, _, move_z = VELOCITIES[member]
            value = source(plane + move_x, member)
            if move_z == 1:
                value = jnp.where(
                    last, lam_ref[OPPOSITE[member], plane], pltpu.roll(value, height - 1, 1)
                )
            elif move_z == -1:
                value = jnp.where(first, lam_ref[OPPOSITE[member], plane], pltpu.roll(value, 1, 1))
            mu.append(value)
        lam, _ = plane_adjoint(mu, lambda index: coef_ref[index, plane])
        for member in range(19):
            out_ref[member, plane] = lam[member]


def call(kernel, outs, *args, scratch=(), micros=1):
    return pl.pallas_call(
        kernel,
        out_shape=tuple(jax.ShapeDtypeStruct(shape, jnp.float32) for shape in outs),
        in_specs=[pl.BlockSpec(memory_space=VMEM)] * len(args),
        out_specs=tuple(pl.BlockSpec(memory_space=VMEM) for _ in outs),
        scratch_shapes=[pltpu.VMEM(shape, jnp.float32) for shape in scratch],
        cost_estimate=pl.CostEstimate(
            flops=int(1e6 * micros), bytes_accessed=int(2e6 * micros), transcendentals=0
        ),
        compiler_params=pltpu.CompilerParams(vmem_limit_bytes=32 * 1024 * 1024),
    )(*args)


def ring(axis, step):
    count = lax.axis_size(axis)
    return [(i, (i + step) % count) for i in range(count)]


def swap_rows(rows):
    if lax.axis_size("gy") == 2:
        return lax.ppermute(rows, "gy", ring("gy", 1))
    return jnp.stack(
        [
            lax.ppermute(rows[0], "gy", ring("gy", -1)),
            lax.ppermute(rows[1], "gy", ring("gy", 1)),
        ]
    )


def swap_near(near):
    count = lax.axis_size("gx")
    assert count % 2 == 0
    return lax.ppermute(near, "gx", [(i, i ^ 1) for i in range(count)])


def swap_far(far):
    count = lax.axis_size("gx")
    return lax.ppermute(
        far, "gx", [(i, (i + 1 if i % 2 else i - 1) % count) for i in range(count)]
    )


def flips(value, axis, flip_list):
    count = lax.axis_size(axis)
    parts = [lax.ppermute(value, axis, [(i, i ^ flip) for i in range(count)]) for flip in flip_list]
    return sum(parts, value)


def sum_bits(value, axis, start):
    count = lax.axis_size(axis)
    while start < count:
        stop = min(4 * start, count)
        value = flips(value, axis, [step * start for step in (1, 3, 2) if step * start < stop])
        start = stop
    return value


def last_exchange(lam, packed):
    width, height = lam.shape[1], lam.shape[3]
    rows_count = 10 * width
    sums = packed[rows_count:]
    count = lax.axis_size("gx")
    apart = count & (count - 1) == 0 and count > 2
    joined = apart and lax.axis_size("gy") == 2
    if joined:
        got = lax.ppermute(packed, "gy", ring("gy", 1))
        rows, got = got[:rows_count], got[rows_count:]
        got = got + lax.ppermute(sums, "gx", [(i, i ^ 2) for i in range(count)])
        got = got + lax.ppermute(
            sums, ("gx", "gy"), [(i, i ^ 5) for i in range(2 * count)]
        )
    else:
        rows = swap_rows(packed[:rows_count].reshape(2, rows_count // 2, -1))
        rows = rows.reshape(rows_count, -1)
        spans = lax.axis_size("gy")
        got = (lax.psum(sums, "gy") if spans & (spans - 1) else sum_bits(sums, "gy", 1)) - sums
    near, far = call(
        last_faces_kernel,
        [(5, lam.shape[2], height), (6, lam.shape[2], height)],
        lam,
        rows,
        micros=0.1,
    )
    sums = sums + got
    if apart and not joined:
        sums = flips(sums, "gx", [2])
    got_near, got_far = swap_near(near), swap_far(far)
    if apart:
        (sums,) = call(pass_kernel, [sums.shape], sums, got_near, micros=0.1)
        sums = sum_bits(flips(sums, "gx", [1]), "gx", 4)
    else:
        sums = lax.psum(sums, "gx")
    return rows, got_near, got_far, sums


def shards(fwd_pops, fwd_scale, seed_adjoint, turbine_map, thrust):
    steps, _, width, span, height = fwd_pops.shape
    assert steps == 3 and span == 8
    turbines = thrust.shape[0]
    turbine_rows = -(-turbines // 8) * 8
    sublanes = -(-(width + 4) // 8) * 8
    whole = (19, width, span, height)
    (begun,) = call(start_kernel, [(8, height)], micros=400)
    fields, first, thrust_rows, slope_rows = call(
        pack_kernel,
        [
            (FIELDS, width, span, height),
            (2, FIRST_ROWS, height),
            (turbine_rows, height),
            (turbine_rows, height),
        ],
        begun,
        thrust.reshape(1, turbines),
        turbine_map,
        fwd_scale,
        fwd_pops,
        seed_adjoint,
        micros=0.6,
    )
    first = swap_rows(first)
    coefs = call(
        coef_kernel,
        [(COEFS, width, span, height)] * steps,
        thrust_rows,
        turbine_map,
        fwd_scale,
        fwd_pops,
        micros=0.8,
    )
    (rows,) = call(
        rows_kernel,
        [(2, (HALO + FIELDS) * width, height)],
        seed_adjoint,
        fields,
        coefs[2],
        micros=0.1,
    )
    rows = swap_rows(rows)
    face, edge = (FACE_TILES, span, height), (2, 5, sublanes, height)
    tile = (19, span, height)
    (far,) = call(
        far_kernel,
        [face],
        thrust_rows,
        seed_adjoint,
        fields,
        first,
        coefs[2],
        scratch=[(20, span, height), tile, tile],
        micros=2000,
    )
    far = swap_far(far)
    near, pack, part_edge = call(
        faces_kernel,
        [face, (2, FIELDS, sublanes, height), edge],
        thrust_rows,
        seed_adjoint,
        fields,
        rows,
        coefs[2],
        scratch=[(2, len(PACK_LIST[0]), sublanes, height), face, face],
        micros=0.4,
    )
    near = swap_near(near)
    parts = call(
        middle_kernel,
        [whole, (width, span, height)],
        seed_adjoint,
        rows,
        coefs[2],
        micros=0.6,
    )
    lam, packed = call(
        lambda *refs: pair_kernel(turbines, *refs),
        [whole, (10 * width + turbine_rows, height)],
        thrust_rows,
        seed_adjoint,
        rows,
        near,
        far,
        coefs[2],
        coefs[1],
        fields,
        *parts,
        part_edge,
        pack,
        scratch=[
            (19, 2, span, height),
            edge,
            (2, 2, sublanes, height),
            face,
            face,
            (2, 5, span, height),
        ],
        micros=0.8,
    )
    rows, near, far, sums = last_exchange(lam, packed)
    (lam,) = call(last_kernel, [whole], lam, rows, near, far, coefs[0], micros=0.5)
    thrust_grad = jnp.sum((slope_rows * sums)[:turbines], axis=1)
    return (lam, thrust_grad)


def solution(mesh):
    placed = (
        P(None, None, "gx", "gy", None),
        P(None, "gx", "gy", None),
        P(None, "gx", "gy", None),
        P("gx", "gy", None),
        P(),
    )
    return jax.shard_map(
        shards,
        mesh=mesh,
        in_specs=placed,
        out_specs=(P(None, "gx", "gy", None), P()),
        check_vma=False,
    )
```
